128 devices in a mesh: shard: 4 (over x_hi, core), ctx: 4 (over z), tp: 8 (over x_lo, y).
Axes of the slice: x: 4 (x_hi: 2, x_lo: 2; x = x_hi * 2 + x_lo), y: 4, z: 4, core: 2. Of those that a mesh axis runs over, the one named last changes fastest.
Arguments:
- latent_in: bfloat16 [16, 1024, 1024], P('shard', 'ctx'), may hold values from -6 to 6
- condition: bfloat16 [16, 1024], P('shard'), may hold values from -6 to 6
- ada_weight: bfloat16 [1024, 6, 1024], P('shard', None, 'tp'), may hold values from -0.1875 to 0.1875
- qkv_weight: bfloat16 [1024, 3, 1024], P('shard', None, 'tp'), may hold values from -0.1875 to 0.1875
- proj_weight: bfloat16 [1024, 1024], P('tp', 'shard'), may hold values from -0.5 to 0.5
- up_matrix: bfloat16 [1024, 4096], P('shard', 'tp'), may hold values from -0.1875 to 0.1875
- down_matrix: bfloat16 [4096, 1024], P('tp', 'shard'), may hold values from -0.09375 to 0.09375
- out_grad: bfloat16 [16, 1024, 1024], P('shard', 'ctx'), may hold values from -6 to 6
Outputs:
- latent_out: float32 [16, 1024, 1024], P('shard', 'ctx')
- latent_grad: float32 [16, 1024, 1024], P('shard', 'ctx')
- condition_grad: float32 [16, 1024], P('shard')
- ada_grad: float32 [1024, 6, 1024], P('shard', None, 'tp')
- qkv_grad: float32 [1024, 3, 1024], P('shard', None, 'tp')
- proj_grad: float32 [1024, 1024], P('tp', 'shard')
- up_grad: float32 [1024, 4096], P('shard', 'tp')
- down_grad: float32 [4096, 1024], P('tp', 'shard')
The draws below stay inside these ranges and needn't reach their ends.
All inputs are finite; a program needn't handle non-finite values.
Results may differ from the reference program's by a relative error of at most 0.019.
Values may be sent and summed in bfloat16 or wider, within the bound.
No kernel may reach another device: no remote copies, remote signals or barrier semaphores. Data moves between devices by JAX's collectives and lax.ppermute only.
A program may use at most 128 MiB of HBM per device.

```python
import jax
import jax.numpy as jnp
from jax import lax

D = 1024
HEADS = 16
HD = 64
FF = 4096
SEQ = 1024
LATENTS = 16


def level_of(rng, dims, shards, least, high):
    def one(position, blocks):
        draws = jax.random.uniform(jax.random.fold_in(jax.random.fold_in(rng, 6), position), (blocks,), jnp.float32, least / len(shards), high / len(shards))
        return jnp.repeat(jnp.exp(draws), dims[position] // blocks).reshape((-1,) + (1,) * (len(dims) - position - 1))

    gain = one(*shards[0])
    for cut in shards[1:]:
        gain = gain * one(*cut)
    return gain


def gaussian(rng, dims, spread, reach, cuts=(), kind=jnp.bfloat16):
    values = spread * jax.random.normal(rng, dims, jnp.float32)
    if cuts:
        values = values * level_of(rng, dims, cuts, -0.22, 0.18)
    return jnp.clip(values, -reach, reach).astype(kind)


def setup_inputs(seed: int = 0) -> dict:
    splits = jax.random.split(jax.random.key(seed), 9)
    return {
        "latent_in": gaussian(splits[0], (LATENTS, SEQ, D), 1.0, 6.0, ((0, 4), (1, 4))),
        "condition": gaussian(splits[1], (LATENTS, D), 1.0, 6.0, ((0, 4),)),
        "ada_weight": gaussian(splits[2], (D, 6, D), D ** -0.5, 0.1875, ((0, 4), (2, 8))),
        "qkv_weight": gaussian(splits[3], (D, 3, D), D ** -0.5, 0.1875, ((0, 4), (2, 8))),
        "proj_weight": gaussian(splits[4], (D, D), (D // 8) ** -0.5, 0.5, ((0, 8), (1, 4))),
        "up_matrix": gaussian(splits[5], (D, FF), D ** -0.5, 0.1875, ((0, 4), (1, 8))),
        "down_matrix": gaussian(splits[6], (FF, D), FF ** -0.5, 0.09375, ((0, 8), (1, 4))),
        "out_grad": gaussian(splits[7], (LATENTS, SEQ, D), 1.0, 6.0, ((0, 4), (1, 4))),
    }


@jax.custom_vjp
def low(v):
    return lax.optimization_barrier(v.astype(jnp.bfloat16)).astype(jnp.float32)

@jax.custom_vjp
def low_back(v):
    return v

def low_keep(v):
    return (low(v), None)

def low_pass(kept, grad):
    return (grad,)

def back_keep(v):
    return (v, None)

def back_low(kept, grad):
    return (low(grad),)
low.defvjp(low_keep, low_pass)
low_back.defvjp(back_keep, back_low)
HIGHEST_PRECISE = lax.Precision.HIGHEST

def normalize(rows):
    centred = rows - lax.optimization_barrier(jnp.mean(rows, axis=-1, keepdims=True))
    return centred * lax.rsqrt(lax.optimization_barrier(jnp.mean(centred * centred, axis=-1, keepdims=True)) + 1e-06)

def attend_one(triple):
    queries, key_rows, values = triple
    scores = low_back(jnp.einsum('qhd,khd->hqk', queries, key_rows, precision=HIGHEST_PRECISE) * HD ** (-0.5))
    row_peak = lax.optimization_barrier(jnp.max(scores, axis=-1, keepdims=True))
    powered = jnp.exp(scores - row_peak)
    probs = powered / lax.optimization_barrier(jnp.sum(powered, axis=-1, keepdims=True))
    weights = low(probs)
    return jnp.einsum('hqk,khd->qhd', weights, values, precision=HIGHEST_PRECISE)

def forward(latent, condition, ada_weight, qkv_weight, proj_weight, up_matrix, down_matrix):
    silu_cond = low(jax.nn.silu(condition))
    modulation = low(jnp.einsum('ld,dke->lke', silu_cond, ada_weight, precision=HIGHEST_PRECISE))
    shift_a = modulation[:, 0][:, None, :]
    scale_a = modulation[:, 1][:, None, :]
    gate_a = modulation[:, 2][:, None, :]
    shift_b = modulation[:, 3][:, None, :]
    scale_b = modulation[:, 4][:, None, :]
    gate_b = modulation[:, 5][:, None, :]
    input_a = low(normalize(latent) * (1.0 + scale_a) + shift_a)
    triple = low(low_back(jnp.einsum('lsd,dke->lske', input_a, qkv_weight, precision=HIGHEST_PRECISE)))
    shaped = triple.reshape(LATENTS, SEQ, 3, HEADS, HD)
    heads_out = lax.map(jax.checkpoint(attend_one), (shaped[:, :, 0], shaped[:, :, 1], shaped[:, :, 2]))
    attended = low(low_back(heads_out.reshape(LATENTS, SEQ, D)))
    attn = low_back(jnp.einsum('lse,ed->lsd', attended, proj_weight, precision=HIGHEST_PRECISE))
    middle = latent + gate_a * attn
    input_second = low(normalize(middle) * (1.0 + scale_b) + shift_b)
    up_projected = low_back(jnp.einsum('tjq,qo->tjo', input_second, up_matrix, precision=HIGHEST_PRECISE))
    active_rows = low(jax.nn.gelu(up_projected, approximate=True))
    feedforward_output = low_back(jnp.einsum('qwc,cz->qwz', active_rows, down_matrix, precision=HIGHEST_PRECISE))
    return middle + gate_b * feedforward_output

def reference(latent_in, condition, ada_weight, qkv_weight, proj_weight, up_matrix, down_matrix, out_grad):
    inputs = tuple((entry.astype(jnp.float32) for entry in (latent_in, condition, ada_weight, qkv_weight, proj_weight, up_matrix, down_matrix)))
    output, pullback = jax.vjp(forward, *inputs)
    grads = pullback(out_grad.astype(jnp.float32))
    return (output, grads[0], grads[1], grads[2], grads[3], grads[4], grads[5], grads[6])
```

```python
import jax
import jax.numpy as jnp
from jax import lax
from jax.experimental import pallas as pl
from jax.experimental.pallas import tpu as pltpu
from jax.sharding import PartitionSpec as P

HD = 64
EPSILON = 1e-06
HIGHEST = lax.Precision.HIGHEST
BF = jnp.bfloat16
F32 = jnp.float32


def swap(value, axis, bits):
    size = {"shard": 4, "ctx": 4, "tp": 8}[axis]
    return lax.ppermute(value, axis, [(i, i ^ bits) for i in range(size)])


def swap_x(value, bits):
    if bits == 1:
        return swap(value, "tp", 4)
    if bits == 2:
        return swap(value, "shard", 2)
    return lax.ppermute(value, ("shard", "tp"), [(i, i ^ 20) for i in range(32)])


def pick(array, index, axis=0):
    return lax.dynamic_index_in_dim(array, index, axis, keepdims=False)


def dot(a, b, contract):
    return lax.dot_general(a, b, (contract, ((), ())), preferred_element_type=F32)


def normalize(rows):
    centred = rows - jnp.mean(rows, axis=-1, keepdims=True)
    inverse = lax.rsqrt(jnp.mean(centred * centred, axis=-1, keepdims=True) + EPSILON)
    return centred * inverse, inverse


def norm_back(grad, normed, inverse):
    first = jnp.mean(grad, axis=-1, keepdims=True)
    second = jnp.mean(grad * normed, axis=-1, keepdims=True)
    return inverse * (grad - first - normed * second)


GELU_A = 0.7978845608028654
GELU_B = 0.044715


def gelu(v):
    return 0.5 * v * (1.0 + jnp.tanh(GELU_A * (v + GELU_B * v * v * v)))


def gelu_slope(v):
    t = jnp.tanh(GELU_A * (v + GELU_B * v * v * v))
    return 0.5 * (1.0 + t) + 0.5 * v * (1.0 - t * t) * (GELU_A * (1.0 + 3.0 * GELU_B * v * v))


def arrange(index, *arrays):
    def body(idx, *refs):
        half = len(refs) // 2
        for src, dst in zip(refs[:half], refs[half:]):
            for i in range(4):
                start = pl.multiple_of(idx[6 + i] * 256, 256)
                dst[0, 0, :, i * 256 : (i + 1) * 256] = src[0, :, pl.ds(start, 256)]

    count = len(arrays)
    return pl.pallas_call(
        body,
        grid_spec=pltpu.PrefetchScalarGridSpec(
            num_scalar_prefetch=1,
            grid=(4, 2),
            in_specs=[pl.BlockSpec((1, 64, 1024), lambda r, l, idx: (idx[l], idx[2 + r], 0))] * count,
            out_specs=[pl.BlockSpec((1, 1, 64, 1024), lambda r, l, idx: (r, l, 0, 0))] * count,
        ),
        out_shape=[jax.ShapeDtypeStruct((4, 2, 64, 1024), a.dtype) for a in arrays],
        name="arrange",
    )(index, *arrays)


def restore(index, blocks):
    def body(idx, *refs):
        out = refs[-1]
        for x in range(2):
            for r in range(4):
                for l in range(2):
                    row = pl.multiple_of(idx[2 + r] * 64, 64)
                    for i in range(4):
                        col = pl.multiple_of(idx[6 + i] * 256, 256)
                        out[idx[10 + 2 * x + l], pl.ds(row, 64), pl.ds(col, 256)] = refs[4 * x + r][
                            l, :, i * 256 : (i + 1) * 256
                        ].astype(F32)

    return pl.pallas_call(
        body,
        in_specs=[pl.BlockSpec(memory_space=pltpu.SMEM)] + [pl.BlockSpec(memory_space=pltpu.VMEM)] * 8,
        out_specs=pl.BlockSpec(memory_space=pltpu.VMEM),
        out_shape=jax.ShapeDtypeStruct((4, 256, 1024), F32),
        compiler_params=pltpu.CompilerParams(vmem_limit_bytes=32 * 2**20),
        name="restore",
    )(index, *blocks)


def load_heads(refs, q_s, k_s, v_s):
    for i, ref in enumerate(refs):
        rows = slice(i * 256, (i + 1) * 256)
        q_s[rows] = ref[:, 0:128] * jnp.asarray(HD**-0.5, BF)
        k_s[rows] = ref[:, 128:256]
        v_s[rows] = ref[:, 256:384]


def only_head(block, head, axis):
    lane = lax.broadcasted_iota(jnp.int32, block.shape, axis)
    return jnp.where((lane >= head * HD) & (lane < (head + 1) * HD), block, jnp.zeros_like(block))


def head_probs(k, q_head):
    scores = dot(k, q_head, ((1,), (1,)))
    powered = jnp.exp(scores - jnp.max(scores, axis=0, keepdims=True))
    return powered * (1.0 / jnp.sum(powered, axis=0, keepdims=True))


def attention(parts):
    def body(*refs):
        ins, outs, (q_s, k_s, v_s) = refs[:4], refs[4:8], refs[8:]
        load_heads(ins, q_s, k_s, v_s)
        v_t = v_s[...].T
        for i in range(4):
            q = q_s[i * 256 : (i + 1) * 256]
            total = None
            for head in range(2):
                probs = head_probs(k_s[...], only_head(q, head, 1)).astype(BF)
                term = dot(only_head(v_t, head, 0), probs, ((1,), (0,)))
                total = term if total is None else total + term
            outs[i][...] = total.T.astype(BF)

    return pl.pallas_call(
        body,
        out_shape=[jax.ShapeDtypeStruct((256, 128), BF)] * 4,
        scratch_shapes=[pltpu.VMEM((1024, 128), BF)] * 3,
        compiler_params=pltpu.CompilerParams(vmem_limit_bytes=48 * 2**20),
        cost_estimate=pl.CostEstimate(flops=2**31, bytes_accessed=2**20, transcendentals=2**21),
        name="attention",
    )(*parts)


def attention_back(parts, grads):
    def body(*refs):
        ins, gs, outs = refs[:4], refs[4:8], refs[8:12]
        q_s, k_s, v_s, dk_s, dv_s = refs[12:]
        load_heads(ins, q_s, k_s, v_s)
        k_t = k_s[...].T
        dk_s[...] = jnp.zeros_like(dk_s)
        dv_s[...] = jnp.zeros_like(dv_s)
        for i in range(4):
            q = q_s[i * 256 : (i + 1) * 256]
            g = gs[i][...]
            dq_t = None
            for head in range(2):
                q_head, g_head = only_head(q, head, 1), only_head(g, head, 1)
                probs = head_probs(k_s[...], q_head)
                g_probs = dot(v_s[...], g_head, ((1,), (1,)))
                dv_s[...] += dot(probs.astype(BF), g_head, ((1,), (0,)))
                inner = jnp.sum(probs * g_probs, axis=0, keepdims=True)
                g_scores = (probs * (g_probs - inner)).astype(BF)
                dk_s[...] += dot(g_scores, q_head, ((1,), (0,)))
                term = dot(only_head(k_t, head, 0), g_scores, ((1,), (0,)))
                dq_t = term if dq_t is None else dq_t + term
            outs[i][:, 0:128] = (dq_t.T * HD**-0.5).astype(BF)
        for i in range(4):
            rows = slice(i * 256, (i + 1) * 256)
            outs[i][:, 128:256] = dk_s[rows].astype(BF)
            outs[i][:, 256:384] = dv_s[rows].astype(BF)

    return pl.pallas_call(
        body,
        out_shape=[jax.ShapeDtypeStruct((256, 384), BF)] * 4,
        scratch_shapes=[pltpu.VMEM((1024, 128), BF)] * 3 + [pltpu.VMEM((1024, 128), F32)] * 2,
        compiler_params=pltpu.CompilerParams(vmem_limit_bytes=48 * 2**20),
        cost_estimate=pl.CostEstimate(flops=5 * 2**30, bytes_accessed=2**21, transcendentals=2**21),
        name="attention_back",
    )(*parts, *grads)


def scatter_y(partial):
    sent = partial[1:].astype(BF)
    got = [swap(sent[r - 1], "tp", r).astype(F32) for r in (1, 2, 3)]
    return partial[0] + (got[0] + got[1] + got[2])


def gather_y(block):
    return jnp.stack([block] + [swap(block, "tp", r) for r in (1, 2, 3)])


def exchange_z(blocks):
    return [blocks[0]] + [swap(blocks[q], "ctx", q) for q in (1, 2, 3)]


def spread(index, block):
    own = block.astype(BF)
    blocks = [own] + [swap(own, "tp", r) for r in (1, 2, 3)]
    return restore(index, blocks + [swap(b, "tp", 4) for b in blocks])


def gather_x(block):
    mine = jnp.stack([block] + [swap_x(block, b) for b in (1, 2, 3)])
    other = swap(mine, "shard", 1)
    return [[(other if i & 1 else mine)[2 * (i >> 1) + j] for j in range(2)] for i in range(4)]


def reduce_grads(partial):
    kept = partial[:, 0::2] + swap(partial[:, 1::2], "shard", 1)
    sent = kept.astype(BF)
    total = kept[:, 0, :, 0]
    got = [swap_x(sent[:, b >> 1, :, b & 1], b).astype(F32) for b in (1, 2, 3)]
    total = (total + (got[0] + got[1] + got[2])).astype(BF)
    terms = [total.astype(F32)] + [swap(total, "ctx", q).astype(F32) for q in (1, 2, 3)]
    return (terms[0] + terms[1]) + (terms[2] + terms[3])


def shards(
    latent_in, condition, ada_weight, qkv_weight, proj_weight, up_matrix, down_matrix, out_grad
):
    s, z, t = lax.axis_index("shard"), lax.axis_index("ctx"), lax.axis_index("tp")
    x_lo, y, z_lat, z_head = t >> 2, t & 3, z >> 1, z & 1
    index = jnp.stack(
        [2 * x_lo + (l ^ z_lat) for l in range(2)]
        + [y ^ r for r in range(4)]
        + [s ^ i for i in range(4)]
        + [2 * (x_lo ^ x) + (l ^ z_lat) for x in range(2) for l in range(2)]
    ).astype(jnp.int32)

    cond_pair = jnp.stack([condition, swap(condition, "shard", 1)])
    cond_all = jnp.concatenate([cond_pair, swap(cond_pair, "shard", 2)])
    cond_rows = lax.dynamic_slice_in_dim(cond_all, s * 256, 256, 2)
    silu_rows = jax.nn.silu(cond_rows.astype(F32)).astype(BF)
    mod_part = dot(silu_rows.reshape(16, 256), ada_weight.reshape(256, 768), ((1,), (0,)))
    mod_part = mod_part.reshape(4, 2, 2, 768)
    mod_kept = mod_part[0::2] + swap(mod_part[1::2], "shard", 1)
    mod_x = [pick(mod_kept[b >> 1], x_lo ^ (b & 1)) for b in range(4)]
    mod_x = [mod_x[0]] + [swap_x(mod_x[b], b) for b in (1, 2, 3)]
    mod_y = jnp.stack([mod_x[0] + mod_x[2], mod_x[1] + mod_x[3]]).astype(BF)
    mod_cols = gather_y(mod_y).reshape(8, 2, 6, 128)
    pieces = []
    for p in range(8):
        column = 2 * (s ^ (p >> 1)) + (p & 1)
        pieces.append(pick(mod_cols, 2 * ((column & 3) ^ y) + ((column >> 2) ^ x_lo)))
    modulation = jnp.concatenate(pieces, axis=-1).astype(F32)
    modulation = jnp.where(z_lat == 1, modulation[::-1], modulation)
    shift_a, scale_a, gate_a, shift_b, scale_b, gate_b = [modulation[:, k][:, None, :] for k in range(6)]

    qkv_blocks = gather_x(qkv_weight.reshape(256, 384))
    qkv_all = jnp.concatenate(
        [
            jnp.concatenate(
                [jnp.where(z_head == 1, b[1], b[0]), jnp.where(z_head == 1, b[0], b[1])], axis=1
            )
            for b in qkv_blocks
        ],
        axis=0,
    )
    packed = jnp.concatenate([proj_weight, up_matrix[:, :256], up_matrix[:, 256:], down_matrix], axis=0)
    rest = gather_x(packed)
    proj_j = [jnp.concatenate([rest[i][j][:128] for i in range(4)], axis=1) for j in range(2)]
    proj_all = jnp.concatenate(
        [jnp.where(z_head == 1, proj_j[1], proj_j[0]), jnp.where(z_head == 1, proj_j[0], proj_j[1])],
        axis=0,
    )
    up_all = jnp.concatenate(
        [
            jnp.concatenate([rest[i][j][k : k + 256] for j in range(2) for k in (128, 384)], axis=1)
            for i in range(4)
        ],
        axis=0,
    )
    down_all = jnp.concatenate(
        [jnp.concatenate([rest[i][j][640:] for i in range(4)], axis=1) for j in range(2)], axis=0
    )

    latent, grad_out = arrange(index, latent_in, out_grad)
    latent_f = latent.astype(F32)
    normed_a, inv_a = normalize(latent_f)
    input_a = (normed_a * (1.0 + scale_a) + shift_a).astype(BF).reshape(512, 1024)
    triple = dot(input_a, qkv_all, ((1,), (0,))).astype(BF).reshape(4, 2, 64, 768)
    parts = exchange_z(
        [triple[:, q >> 1, :, 384 * (q & 1) : 384 * (q & 1) + 384].reshape(256, 384) for q in range(4)]
    )
    heads = exchange_z(attention(parts))

    def by_token(blocks):
        width = blocks[0].shape[-1]
        shaped = [b.reshape(4, 1, 64, width) for b in blocks]
        pairs = [jnp.concatenate(shaped[2 * l : 2 * l + 2], axis=-1) for l in range(2)]
        return jnp.concatenate(pairs, axis=1).reshape(512, 2 * width)

    attended = by_token(heads)
    attn = scatter_y(dot(attended, proj_all, ((1,), (0,))).reshape(4, 128, 1024)).reshape(2, 64, 1024)
    middle = latent_f[0] + gate_a * attn
    normed_b, inv_b = normalize(middle)
    input_b = (normed_b * (1.0 + scale_b) + shift_b).astype(BF).reshape(128, 1024)
    input_b = gather_y(input_b).reshape(512, 1024)
    up = dot(input_b, up_all, ((1,), (0,)))
    act = gelu(up).astype(BF)
    g_out = grad_out.astype(F32)
    g_mlp = (gate_b * g_out).astype(BF).reshape(512, 1024)
    g_act = dot(g_mlp, down_all, ((1,), (1,)))
    g_up = (g_act * gelu_slope(up)).astype(BF)
    g_in_b = scatter_y(dot(g_up, up_all, ((1,), (1,))).reshape(4, 128, 1024)).reshape(2, 64, 1024)

    mlp = scatter_y(dot(act, down_all, ((1,), (0,))).reshape(4, 128, 1024)).reshape(2, 64, 1024)
    latent_out = spread(index, middle + gate_b * mlp)

    ud_part = jnp.stack([dot(input_b, g_up, ((0,), (0,))), dot(g_mlp, act, ((0,), (0,)))])
    ud = reduce_grads(ud_part.reshape(2, 4, 256, 2, 512))

    g_mid = g_out[0] + norm_back(g_in_b * (1.0 + scale_b), normed_b, inv_b)
    g_attn = gather_y((gate_a * g_mid).astype(BF).reshape(128, 1024)).reshape(512, 1024)
    g_heads = dot(g_attn, proj_all, ((1,), (1,))).astype(BF).reshape(4, 2, 64, 256)
    g_parts = exchange_z(
        [g_heads[:, q >> 1, :, 128 * (q & 1) : 128 * (q & 1) + 128].reshape(256, 128) for q in range(4)]
    )
    g_triple = by_token(exchange_z(attention_back(parts, g_parts)))
    in_a_part = dot(g_triple, qkv_all, ((1,), (1,)))
    g_in_a = scatter_y(in_a_part.reshape(4, 128, 1024)).reshape(2, 64, 1024)
    latent_grad = spread(
        index, g_mid + norm_back(g_in_a * (1.0 + scale_a), normed_a[0], inv_a[0])
    )

    qkv_part = dot(input_a, g_triple, ((0,), (0,))).reshape(1024, 2, 384)
    proj_part = dot(g_attn, attended, ((0,), (0,))).reshape(1024, 2, 128)
    qp_part = jnp.concatenate([qkv_part, proj_part], axis=-1)
    qp_part = jnp.where(z_head == 1, qp_part[:, ::-1], qp_part)
    qp = reduce_grads(qp_part.reshape(1, 4, 256, 2, 512))[0]

    in_a_shaped = in_a_part.reshape(4, 2, 64, 1024)
    g_mod = jnp.stack(
        [
            jnp.sum(in_a_shaped, axis=(0, 2)),
            jnp.sum(in_a_shaped * normed_a, axis=(0, 2)),
            jnp.sum(g_mid * attn, axis=1),
            jnp.sum(g_in_b, axis=1),
            jnp.sum(g_in_b * normed_b, axis=1),
            jnp.sum(g_out[0] * mlp, axis=1),
        ],
        axis=1,
    )
    g_mod = jnp.where(z_lat == 1, g_mod[::-1], g_mod)
    g_mod = jnp.concatenate([lax.dynamic_slice_in_dim(g_mod, (s ^ i) * 256, 256, 2) for i in range(4)], axis=2)
    g_mod = g_mod.reshape(2, 6, 2, 4, 128)
    g_mod = [pick(g_mod, y ^ r, 3) for r in range(4)]
    g_mod = [g_mod[0]] + [swap(g_mod[r], "tp", r) for r in (1, 2, 3)]
    g_mod = (g_mod[0] + g_mod[1]) + (g_mod[2] + g_mod[3])
    g_mod = [g_mod] + [swap(g_mod, "ctx", q) for q in (1, 2, 3)]
    g_mod = (g_mod[0] + g_mod[1]) + (g_mod[2] + g_mod[3])
    g_mod = [pick(g_mod, x_lo ^ (b & 1), 2) for b in range(4)]
    g_mod = jnp.stack([g_mod[0]] + [swap_x(g_mod[b], b) for b in (1, 2, 3)])
    other = swap(g_mod, "shard", 1)
    g_mod = jnp.stack([(other if i & 1 else g_mod)[2 * (i >> 1) : 2 * (i >> 1) + 2] for i in range(4)])
    g_mod = g_mod.reshape(16, 768)
    silu_grad = silu_rows.astype(F32).reshape(4, 2, 2, 256)
    silu_grad = jnp.where(x_lo == 1, silu_grad[:, ::-1], silu_grad).reshape(16, 256)
    ada_grad = lax.dot_general(silu_grad, g_mod, (((0,), (0,)), ((), ())), precision=HIGHEST)
    ada_f = ada_weight.astype(F32).reshape(256, 768)
    terms = lax.dot_general(g_mod, ada_f, (((1,), (1,)), ((), ())), precision=HIGHEST)
    terms = terms.reshape(4, 2, 2, 256)
    terms = jnp.where(x_lo == 1, terms[:, ::-1], terms).reshape(4, 4, 256)
    theirs = swap(terms[1::2], "shard", 1)
    terms = jnp.stack([terms[0::2], theirs], axis=1)
    got = [terms[0]] + [swap_x(terms[b >> 1], b) for b in (1, 2, 3)]
    terms = jnp.stack([got[0] + got[1], got[2] + got[3]]).reshape(4, 4, 256)
    terms = [terms] + [swap(terms, "tp", r) for r in (1, 2, 3)]
    terms = (terms[0] + terms[1]) + (terms[2] + terms[3])
    cond_own = jnp.concatenate([pick(terms, s ^ i) for i in range(4)], axis=1)
    silu_own, silu_pull = jax.vjp(jax.nn.silu, condition.astype(F32))
    condition_grad = silu_pull(cond_own)[0]

    return (
        latent_out,
        latent_grad,
        condition_grad,
        ada_grad.reshape(256, 6, 128),
        qp[:, :384].reshape(256, 3, 128),
        qp[:, 384:].T,
        ud[0],
        ud[1].T,
    )


def solution(mesh):
    placed = (
        P("shard", "ctx", None),
        P("shard", None),
        P("shard", None, "tp"),
        P("shard", None, "tp"),
        P("tp", "shard"),
        P("shard", "tp"),
        P("tp", "shard"),
        P("shard", "ctx", None),
    )
    return jax.shard_map(
        shards,
        mesh=mesh,
        in_specs=placed,
        out_specs=(
            P("shard", "ctx", None),
            P("shard", "ctx", None),
            P("shard", None),
            P("shard", None, "tp"),
            P("shard", None, "tp"),
            P("tp", "shard"),
            P("shard", "tp"),
            P("tp", "shard"),
        ),
        check_vma=False,
    )
```

```python
import jax
import jax.numpy as jnp
from jax import lax
from jax.experimental import pallas as pl
from jax.experimental.pallas import tpu as pltpu
from jax.sharding import PartitionSpec as P

HD = 64
EPSILON = 1e-06
HIGHEST = lax.Precision.HIGHEST
BF = jnp.bfloat16
F32 = jnp.float32


def swap(value, axis, bits):
    size = {"shard": 4, "ctx": 4, "tp": 8}[axis]
    return lax.ppermute(value, axis, [(i, i ^ bits) for i in range(size)])


def swap_x(value, bits):
    if bits == 1:
        return swap(value, "tp", 4)
    if bits == 2:
        return swap(value, "shard", 2)
    return lax.ppermute(value, ("shard", "tp"), [(i, i ^ 20) for i in range(32)])


def pick(array, index, axis=0):
    return lax.dynamic_index_in_dim(array, index, axis, keepdims=False)


def dot(a, b, contract):
    return lax.dot_general(a, b, (contract, ((), ())), preferred_element_type=F32)


def normalize(rows):
    centred = rows - jnp.mean(rows, axis=-1, keepdims=True)
    inverse = lax.rsqrt(jnp.mean(centred * centred, axis=-1, keepdims=True) + EPSILON)
    return centred * inverse, inverse


def norm_back(grad, normed, inverse):
    first = jnp.mean(grad, axis=-1, keepdims=True)
    second = jnp.mean(grad * normed, axis=-1, keepdims=True)
    return inverse * (grad - first - normed * second)


GELU_A = 0.7978845608028654
GELU_B = 0.044715


def gelu_and_slope(v):
    square = v * v
    t = jnp.tanh(GELU_A * (v + GELU_B * v * square))
    half = 0.5 * (1.0 + t)
    return v * half, half + 0.5 * v * (1.0 - t * t) * (GELU_A * (1.0 + 3.0 * GELU_B * square))


LAT, TOK, FEAT, OUT_LAT, Z_HEAD, X_LO, Z_LAT, COLS = 0, 2, 6, 10, 14, 15, 16, 17


def kernel(body, outs, index, *arrays, scratch=(), vmem=40, flops=2**28, name):
    return pl.pallas_call(
        body,
        in_specs=[pl.BlockSpec(memory_space=pltpu.SMEM)]
        + [pl.BlockSpec(memory_space=pltpu.VMEM)] * len(arrays),
        out_specs=[pl.BlockSpec(memory_space=pltpu.VMEM)] * len(outs),
        out_shape=[jax.ShapeDtypeStruct(shape, kind) for shape, kind in outs],
        scratch_shapes=[pltpu.VMEM(shape, kind) for shape, kind in scratch],
        compiler_params=pltpu.CompilerParams(vmem_limit_bytes=vmem * 2**20),
        cost_estimate=pl.CostEstimate(flops=flops, bytes_accessed=2**22, transcendentals=0),
        name=name,
    )(index, *arrays)


def aligned(start, step):
    return pl.ds(pl.multiple_of(start * step, step), step)


def arrange(index, *arrays):
    def body(idx, *refs):
        half = len(refs) // 2
        for src, dst in zip(refs[:half], refs[half:]):
            for r in range(4):
                for l in range(2):
                    for i in range(4):
                        dst[r * 128 + l * 64 : r * 128 + l * 64 + 64, i * 256 : (i + 1) * 256] = src[
                            idx[LAT + l] - 2 * idx[X_LO], aligned(idx[TOK + r], 64), aligned(idx[FEAT + i], 256)
                        ]

    count = len(arrays)
    return pl.pallas_call(
        body,
        grid_spec=pltpu.PrefetchScalarGridSpec(
            num_scalar_prefetch=1,
            grid=(1,),
            in_specs=[pl.BlockSpec((2, 256, 1024), lambda n, idx: (idx[X_LO], 0, 0))] * count,
            out_specs=[pl.BlockSpec((512, 1024), lambda n, idx: (0, 0))] * count,
        ),
        out_shape=[jax.ShapeDtypeStruct((512, 1024), a.dtype) for a in arrays],
        compiler_params=pltpu.CompilerParams(vmem_limit_bytes=24 * 2**20),
        name="arrange",
    )(index, *arrays)


def restore(index, blocks):
    def body(idx, *refs):
        out = refs[-1]
        for x in range(2):
            for r in range(4):
                for l in range(2):
                    for i in range(4):
                        out[idx[OUT_LAT + 2 * x + l], aligned(idx[TOK + r], 64), aligned(idx[FEAT + i], 256)] = refs[
                            4 * x + r
                        ][l * 64 : l * 64 + 64, i * 256 : (i + 1) * 256].astype(F32)

    return kernel(body, [((4, 256, 1024), F32)], index, *blocks, vmem=24, name="restore")[0]


def mod_rows(mod, k, width=64):
    return jnp.concatenate(
        [jnp.broadcast_to(mod[6 * l + k : 6 * l + k + 1], (64, mod.shape[1])) for l in range(2)], axis=0
    )


def latent_sums(value):
    return [jnp.sum(value[l * 64 : (l + 1) * 64], axis=0, keepdims=True) for l in range(2)]


def project_in(index, latent, mod, mine, other):
    def body(idx, x_ref, mod_ref, mine_ref, other_ref, in_ref, w_ref, stat_ref, *outs):
        for i in range(4):
            for j in range(2):
                source = other_ref if i & 1 else mine_ref
                w_ref[i * 256 : (i + 1) * 256, j * 384 : (j + 1) * 384] = source[2 * (i >> 1) + (j ^ idx[Z_HEAD])]

        @pl.loop(0, 4)
        def _(r):
            rows = aligned(r, 128)
            x = x_ref[rows].astype(F32)
            centred = x - jnp.mean(x, axis=-1, keepdims=True)
            inverse = lax.rsqrt(jnp.mean(centred * centred, axis=-1, keepdims=True) + EPSILON)
            normed = centred * inverse
            in_ref[rows] = (normed * (1.0 + mod_rows(mod_ref[...], 1)) + mod_rows(mod_ref[...], 0)).astype(BF)
            stat_ref[rows, 0:128] = jnp.broadcast_to(x[:, 0:1] - centred[:, 0:1], (128, 128))
            stat_ref[rows, 128:256] = jnp.broadcast_to(inverse, (128, 128))

        for j in range(2):
            block = dot(in_ref[...], w_ref[:, j * 384 : (j + 1) * 384], ((1,), (0,))).astype(BF)
            block = block.reshape(4, 2, 64, 384)
            for l in range(2):
                outs[2 * l + j][...] = block[:, l].reshape(256, 384)

    return kernel(
        body,
        [((512, 1024), BF), ((1024, 768), BF), ((512, 256), F32)] + [((256, 384), BF)] * 4,
        index, latent, mod, mine, other, flops=2**30, name="project_in",
    )


def assemble(index, mine, other):
    def body(idx, mine_ref, other_ref, proj_ref, up_ref, down_ref):
        for i in range(4):
            source = other_ref if i & 1 else mine_ref
            wide = slice(i * 256, (i + 1) * 256)
            for j in range(2):
                block = 2 * (i >> 1) + j
                proj_ref[j * 128 : (j + 1) * 128, wide] = source[2 * (i >> 1) + (j ^ idx[Z_HEAD]), 0:128]
                up_ref[wide, j * 512 : j * 512 + 256] = source[block, 128:384]
                up_ref[wide, j * 512 + 256 : (j + 1) * 512] = source[block, 384:640]
                down_ref[j * 512 : (j + 1) * 512, wide] = source[block, 640:1152]

    outs = [((256, 1024), BF), ((1024, 1024), BF), ((1024, 1024), BF)]
    return kernel(body, outs, index, mine, other, name="assemble")


def load_heads(refs, q_s, k_s, v_s):
    for i, ref in enumerate(refs):
        rows = slice(i * 256, (i + 1) * 256)
        q_s[rows] = ref[:, 0:128] * jnp.asarray(HD**-0.5, BF)
        k_s[rows] = ref[:, 128:256]
        v_s[rows] = ref[:, 256:384]


def only_head(block, head, axis):
    lane = lax.broadcasted_iota(jnp.int32, block.shape, axis)
    return jnp.where((lane >= head * HD) & (lane < (head + 1) * HD), block, jnp.zeros_like(block))


def head_probs(k, q_head):
    scores = dot(k, q_head, ((1,), (1,)))
    powered = jnp.exp(scores - jnp.max(scores, axis=0, keepdims=True))
    return powered * (1.0 / jnp.sum(powered, axis=0, keepdims=True))


def attention(index, parts):
    def body(idx, *refs):
        ins, outs, (q_s, k_s, v_s) = refs[:4], refs[4:8], refs[8:]
        load_heads(ins, q_s, k_s, v_s)
        v_t = v_s[...].T
        for i in range(4):
            q = q_s[i * 256 : (i + 1) * 256]
            total = None
            for head in range(2):
                probs = head_probs(k_s[...], only_head(q, head, 1)).astype(BF)
                term = dot(only_head(v_t, head, 0), probs, ((1,), (0,)))
                total = term if total is None else total + term
            outs[i][...] = total.T.astype(BF)

    return kernel(
        body, [((256, 128), BF)] * 4, index, *parts,
        scratch=[((1024, 128), BF)] * 3, vmem=24, flops=2**31, name="attention",
    )


def attention_back(index, parts, grads):
    def body(idx, *refs):
        ins, gs, outs = refs[:4], refs[4:8], refs[8:12]
        q_s, k_s, v_s, dk_s, dv_s = refs[12:]
        load_heads(ins, q_s, k_s, v_s)
        k_t = k_s[...].T
        dk_s[...] = jnp.zeros_like(dk_s)
        dv_s[...] = jnp.zeros_like(dv_s)
        for i in range(4):
            q = q_s[i * 256 : (i + 1) * 256]
            g = gs[i][...]
            dq_t = None
            for head in range(2):
                q_head, g_head = only_head(q, head, 1), only_head(g, head, 1)
                probs = head_probs(k_s[...], q_head)
                g_probs = dot(v_s[...], g_head, ((1,), (1,)))
                dv_s[...] += dot(probs.astype(BF), g_head, ((1,), (0,)))
                inner = jnp.sum(probs * g_probs, axis=0, keepdims=True)
                g_scores = (probs * (g_probs - inner)).astype(BF)
                dk_s[...] += dot(g_scores, q_head, ((1,), (0,)))
                term = dot(only_head(k_t, head, 0), g_scores, ((1,), (0,)))
                dq_t = term if dq_t is None else dq_t + term
            outs[i][:, 0:128] = (dq_t.T * HD**-0.5).astype(BF)
        for i in range(4):
            rows = slice(i * 256, (i + 1) * 256)
            outs[i][:, 128:256] = dk_s[rows].astype(BF)
            outs[i][:, 256:384] = dv_s[rows].astype(BF)

    return kernel(
        body, [((256, 384), BF)] * 4, index, *parts, *grads,
        scratch=[((1024, 128), BF)] * 3 + [((1024, 128), F32)] * 2, vmem=24, flops=5 * 2**30, name="attention_back",
    )


def by_token(refs, dst):
    width = refs[0].shape[-1]
    for l in range(2):
        for j in range(2):
            for r in range(4):
                dst[r * 128 + l * 64 : r * 128 + l * 64 + 64, j * width : (j + 1) * width] = refs[2 * l + j][
                    r * 64 : (r + 1) * 64
                ]


ROWS_OUT = [((128, 1024), F32)] + [((128, 1024), BF)] * 3


def put_rows(value, outs, cols):
    outs[0][:, cols] = value[0:128]
    for r in (1, 2, 3):
        outs[r][:, cols] = value[r * 128 : (r + 1) * 128].astype(BF)


def project_out(index, heads, proj):
    def body(idx, a, b, c, d, w_ref, att_ref, *outs):
        by_token((a, b, c, d), att_ref)

        @pl.loop(0, 4)
        def _(n):
            cols = aligned(n, 256)
            put_rows(dot(att_ref[...], w_ref[:, cols], ((1,), (0,))), outs, cols)

    return kernel(body, [((512, 256), BF)] + ROWS_OUT, index, *heads, proj, name="project_out")


def sum_rows(refs):
    return refs[0][...] + (refs[1][...].astype(F32) + refs[2][...].astype(F32) + refs[3][...].astype(F32))


def middle_rows(index, terms, latent, mod):
    def body(idx, a, b, c, d, x_ref, mod_ref, attn_ref, mid_ref, in_ref):
        mod = mod_ref[...]
        attn = sum_rows((a, b, c, d))
        middle = x_ref[0:128].astype(F32) + mod_rows(mod, 2) * attn
        normed, _ = normalize(middle)
        attn_ref[...] = attn
        mid_ref[...] = middle
        in_ref[...] = (normed * (1.0 + mod_rows(mod, 4)) + mod_rows(mod, 3)).astype(BF)

    outs = [((128, 1024), F32), ((128, 1024), F32), ((128, 1024), BF)]
    return kernel(body, outs, index, *terms, latent, mod, name="middle_rows")


def grad_mlp(index, grad_out, mod):
    def body(idx, g_ref, mod_ref, out_ref):
        @pl.loop(0, 4)
        def _(r):
            rows = aligned(r, 128)
            out_ref[rows] = (mod_rows(mod_ref[...], 5) * g_ref[rows].astype(F32)).astype(BF)

    return kernel(body, [((512, 1024), BF)], index, grad_out, mod, name="grad_mlp")[0]


def grad_act(index, g_mlp, down):
    def body(idx, g_ref, w_ref, out_ref):
        @pl.loop(0, 4)
        def _(n):
            out_ref[:, aligned(n, 256)] = dot(g_ref[...], w_ref[aligned(n, 256)], ((1,), (1,)))

    return kernel(body, [((512, 1024), F32)], index, g_mlp, down, flops=2**30, name="grad_act")[0]


def feed_forward(index, blocks, g_act, up):
    def body(idx, a, b, c, d, g_ref, w_ref, x_ref, act_ref, gup_ref, *outs):
        for r, ref in enumerate((a, b, c, d)):
            x_ref[r * 128 : (r + 1) * 128] = ref[...]

        @pl.loop(0, 4)
        def _(n):
            cols = aligned(n, 256)
            act, slope = gelu_and_slope(dot(x_ref[...], w_ref[:, cols], ((1,), (0,))))
            act_ref[:, cols] = act.astype(BF)
            gup_ref[:, cols] = (g_ref[:, cols] * slope).astype(BF)

        @pl.loop(0, 4)
        def _(n):
            cols = aligned(n, 256)
            put_rows(dot(gup_ref[...], w_ref[cols], ((1,), (1,))), outs, cols)

    return kernel(
        body, [((512, 1024), BF)] * 3 + ROWS_OUT, index, *blocks, g_act, up, flops=2**31, name="feed_forward"
    )


def mlp_rows(index, act, down):
    def body(idx, a_ref, w_ref, *outs):
        @pl.loop(0, 4)
        def _(n):
            cols = aligned(n, 256)
            put_rows(dot(a_ref[...], w_ref[:, cols], ((1,), (0,))), outs, cols)

    return kernel(body, ROWS_OUT, index, act, down, flops=2**30, name="mlp_rows")


def hidden_grads(index, rows, g_up, g_mlp, act):
    def body(idx, x_ref, gup_ref, gm_ref, act_ref, kept_ref, sent_ref):
        for n, (left, right) in enumerate(((x_ref, gup_ref), (gm_ref, act_ref))):
            for i in range(4):
                turned = left[:, i * 256 : (i + 1) * 256].T
                dst = sent_ref if i & 1 else kept_ref

                @pl.loop(0, 4)
                def _(m):
                    cols = aligned(m, 256)
                    dst[n, i >> 1, :, cols] = dot(turned, right[:, cols], ((1,), (0,)))

    return kernel(
        body, [((2, 2, 256, 1024), F32)] * 2, index, rows, g_up, g_mlp, act, flops=2**31, name="hidden_grads"
    )


def out_rows(index, terms, middle, grad_out, mod):
    def body(idx, a, b, c, d, mid_ref, g_ref, mod_ref, out_ref, row_ref):
        mlp = sum_rows((a, b, c, d))
        out_ref[...] = (mid_ref[...] + mod_rows(mod_ref[...], 5) * mlp).astype(BF)
        sums = latent_sums(g_ref[0:128].astype(F32) * mlp)
        row_ref[...] = jnp.zeros_like(row_ref)
        for l in range(2):
            row_ref[l : l + 1] = sums[l]

    outs = [((128, 1024), BF), ((8, 1024), F32)]
    return kernel(body, outs, index, *terms, middle, grad_out, mod, name="out_rows")


def middle_back(index, terms, middle, attn, grad_out, mod):
    def body(idx, a, b, c, d, mid_ref, attn_ref, g_ref, mod_ref, gmid_ref, gattn_ref, row_ref):
        mod = mod_ref[...]
        g_in = sum_rows((a, b, c, d))
        normed, inverse = normalize(mid_ref[...])
        g_mid = g_ref[0:128].astype(F32) + norm_back(g_in * (1.0 + mod_rows(mod, 4)), normed, inverse)
        gmid_ref[...] = g_mid
        gattn_ref[...] = (mod_rows(mod, 2) * g_mid).astype(BF)
        row_ref[...] = jnp.zeros_like(row_ref)
        for k, value in enumerate((g_mid * attn_ref[...], g_in, g_in * normed)):
            sums = latent_sums(value)
            for l in range(2):
                row_ref[3 * l + k : 3 * l + k + 1] = sums[l]

    outs = [((128, 1024), F32), ((128, 1024), BF), ((8, 1024), F32)]
    return kernel(body, outs, index, *terms, middle, attn, grad_out, mod, name="middle_back")


def heads_back(index, blocks, proj):
    def body(idx, a, b, c, d, w_ref, g_ref, *outs):
        for r, ref in enumerate((a, b, c, d)):
            g_ref[r * 128 : (r + 1) * 128] = ref[...]
        for j in range(2):
            block = dot(g_ref[...], w_ref[j * 128 : (j + 1) * 128], ((1,), (1,))).astype(BF).reshape(4, 2, 64, 128)
            for l in range(2):
                outs[2 * l + j][...] = block[:, l].reshape(256, 128)

    outs = [((512, 1024), BF)] + [((256, 128), BF)] * 4
    return kernel(body, outs, index, *blocks, proj, name="heads_back")


def input_back(index, blocks, w_qkv, latent, stats, row_mlp, rows_mid):
    def body(idx, a, b, c, d, w_ref, x_ref, stat_ref, row5_ref, row234_ref, g_ref, *rest):
        outs, mods, gm = rest[:4], rest[4:8], rest[8]
        by_token((a, b, c, d), g_ref)
        gm[...] = jnp.zeros_like(gm)

        @pl.loop(0, 4)
        def _(n):
            cols = aligned(n, 256)
            value = dot(g_ref[...], w_ref[cols], ((1,), (1,)))
            put_rows(value, outs, cols)
            mean = jnp.concatenate([stat_ref[:, 0:128]] * 2, axis=1)
            inverse = jnp.concatenate([stat_ref[:, 128:256]] * 2, axis=1)
            scaled = value * ((x_ref[:, cols].astype(F32) - mean) * inverse)
            for l in range(2):
                for k, part in enumerate((value, scaled)):
                    total = part.reshape(4, 2, 64, 256)[:, l].reshape(256, 256)
                    gm[6 * l + k : 6 * l + k + 1, cols] = jnp.sum(total, axis=0, keepdims=True)

        for l in range(2):
            for k in range(3):
                gm[6 * l + 2 + k : 6 * l + 3 + k] = row234_ref[3 * l + k : 3 * l + k + 1]
            gm[6 * l + 5 : 6 * l + 6] = row5_ref[l : l + 1]
        for r in range(4):
            for x in range(2):
                block = gm[:, aligned(idx[COLS + 2 * r + x], 128)]
                flipped = jnp.concatenate([block[6:12], block[0:6], block[12:16]], axis=0)
                mods[r][:, x * 128 : (x + 1) * 128] = jnp.where(idx[Z_LAT] == 1, flipped, block)

    return kernel(
        body,
        [((512, 768), BF)] + ROWS_OUT + [((16, 256), F32)] * 4,
        index, *blocks, w_qkv, latent, stats, row_mlp, rows_mid,
        scratch=[((16, 1024), F32)], flops=2**30, name="input_back",
    )


def attention_grads(index, rows, g_triple, g_attn, attended):
    def body(idx, x_ref, gt_ref, ga_ref, att_ref, kept_ref, sent_ref):
        for i in range(4):
            dst = sent_ref if i & 1 else kept_ref
            x_t = x_ref[:, i * 256 : (i + 1) * 256].T
            g_t = ga_ref[:, i * 256 : (i + 1) * 256].T
            for j in range(2):
                start = (j ^ idx[Z_HEAD]) * 512
                dst[i >> 1, :, pl.ds(pl.multiple_of(start, 512), 384)] = dot(
                    x_t, gt_ref[:, j * 384 : (j + 1) * 384], ((1,), (0,))
                )
                dst[i >> 1, :, pl.ds(pl.multiple_of(start + 384, 128), 128)] = dot(
                    g_t, att_ref[:, j * 128 : (j + 1) * 128], ((1,), (0,))
                )

    return kernel(
        body, [((2, 256, 1024), F32)] * 2, index, rows, g_triple, g_attn, attended, flops=2**31, name="attention_grads"
    )


def latent_back(index, terms, g_mid, latent, mod):
    def body(idx, a, b, c, d, gmid_ref, x_ref, mod_ref, out_ref):
        normed, inverse = normalize(x_ref[0:128].astype(F32))
        g_in = sum_rows((a, b, c, d)) * (1.0 + mod_rows(mod_ref[...], 1))
        out_ref[...] = (gmid_ref[...] + norm_back(g_in, normed, inverse)).astype(BF)

    return kernel(body, [((128, 1024), BF)], index, *terms, g_mid, latent, mod, name="latent_back")[0]


def core_sum(index, kept, got):
    count = kept.shape[0]

    def body(idx, kept_ref, got_ref, own_ref, *outs):
        for n in range(count):
            for b in range(4):
                cols = slice((b & 1) * 512, (b & 1) * 512 + 512)
                value = kept_ref[n, b >> 1, :, cols] + got_ref[n, b >> 1, :, cols]
                if b == 0:
                    own_ref[n] = value
                else:
                    outs[b - 1][n] = value.astype(BF)

    outs = [((count, 256, 512), F32)] + [((count, 256, 512), BF)] * 3
    return kernel(body, outs, index, kept, got, name="core_sum")


def exchange_y(blocks):
    return [blocks[0]] + [swap(blocks[r], "tp", r) for r in (1, 2, 3)]


def gather_y(block):
    return [block] + [swap(block, "tp", r) for r in (1, 2, 3)]


def exchange_z(blocks):
    return [blocks[0]] + [swap(blocks[q], "ctx", q) for q in (1, 2, 3)]


def gather_x(block):
    mine = jnp.stack([block] + [swap_x(block, b) for b in (1, 2, 3)])
    return mine, swap(mine, "shard", 1)


def ring_sum(index, kept, sent):
    own, *sends = core_sum(index, kept, swap(sent, "shard", 1))
    got = [swap_x(sends[b - 1], b).astype(F32) for b in (1, 2, 3)]
    return own + (got[0] + got[1] + got[2])


def sum_four(terms):
    return (terms[0] + terms[1]) + (terms[2] + terms[3])


def shards(
    latent_in, condition, ada_weight, qkv_weight, proj_weight, up_matrix, down_matrix, out_grad
):
    s, z, t = lax.axis_index("shard"), lax.axis_index("ctx"), lax.axis_index("tp")
    x_lo, y, z_lat, z_head = t >> 2, t & 3, z >> 1, z & 1
    columns = [[((4 * x + (y ^ r)) >> 1 ^ s) * 2 + ((y ^ r) & 1) for x in range(2)] for r in range(4)]
    index = jnp.stack(
        [2 * x_lo + (l ^ z_lat) for l in range(2)]
        + [y ^ r for r in range(4)]
        + [s ^ i for i in range(4)]
        + [2 * (x_lo ^ x) + (l ^ z_lat) for x in range(2) for l in range(2)]
        + [z_head, x_lo, z_lat]
        + [c for pair in columns for c in pair]
    ).astype(jnp.int32)

    ada = ada_weight.reshape(256, 768)
    ada_far = swap(ada, "shard", 2)
    ada_rows = [ada, swap(ada, "shard", 1), ada_far, swap(ada_far, "shard", 1)]
    qkv_mine, qkv_other = gather_x(qkv_weight.reshape(256, 384))
    silu_own = jax.nn.silu(condition.astype(F32)).astype(BF)
    mod_cols = [
        dot(lax.dynamic_slice_in_dim(silu_own, (s ^ i) * 256, 256, 1), ada_rows[i], ((1,), (0,))) for i in range(4)
    ]
    mod_cols = sum_four(mod_cols).astype(BF).reshape(2, 2, 768)
    mod_x = [pick(mod_cols, x_lo), swap(pick(mod_cols, x_lo ^ 1), "tp", 4)]
    mod_y = jnp.stack(gather_y(jnp.stack(mod_x))).reshape(8, 2, 6, 128)
    pieces = []
    for p in range(8):
        column = 2 * (s ^ (p >> 1)) + (p & 1)
        pieces.append(pick(mod_y, 2 * ((column & 3) ^ y) + ((column >> 2) ^ x_lo)))
    mod = jnp.concatenate(pieces, axis=-1).astype(F32)
    mod = jnp.where(z_lat == 1, mod[::-1], mod).reshape(12, 1024)

    latent, grad_out = arrange(index, latent_in, out_grad)
    input_a, w_qkv, stats, *parts = project_in(index, latent, mod, qkv_mine, qkv_other)
    packed = jnp.concatenate([proj_weight, up_matrix[:, :256], up_matrix[:, 256:], down_matrix], axis=0)
    far = [swap_x(packed, b) for b in (1, 2, 3)]
    parts = exchange_z(parts)
    far, parts = lax.optimization_barrier((far, parts))
    mine = jnp.stack([packed] + far)
    proj, up, down = assemble(index, mine, swap(mine, "shard", 1))
    g_mlp = grad_mlp(index, grad_out, mod)
    g_act = grad_act(index, g_mlp, down)

    heads = exchange_z(attention(index, parts))
    attended, *terms = project_out(index, heads, proj)
    attn, middle, input_b = middle_rows(index, exchange_y(terms), latent, mod)
    rows_b, act, g_up, *terms = feed_forward(index, gather_y(input_b), g_act, up)
    g_mid, g_attn, rows_mid = middle_back(index, exchange_y(terms), middle, attn, grad_out, mod)
    g_attn, *g_parts = heads_back(index, gather_y(g_attn), proj)
    g_parts = exchange_z(g_parts)

    out_block, row_mlp = out_rows(index, exchange_y(mlp_rows(index, act, down)), middle, grad_out, mod)
    out_all = lax.all_gather(out_block, "tp", axis=0)
    latent_out = restore(index, [pick(out_all, t ^ (4 * x + r)) for x in range(2) for r in range(4)])
    ud = lax.psum(ring_sum(index, *hidden_grads(index, rows_b, g_up, g_mlp, act)), "ctx")

    g_blocks = exchange_z(attention_back(index, parts, g_parts))
    g_triple, *rest = input_back(index, g_blocks, w_qkv, latent, stats, row_mlp, rows_mid)
    terms, g_mod = rest[:4], rest[4:]
    g_mod = sum_four(exchange_y(g_mod))
    own = latent_back(index, exchange_y(terms), g_mid, latent, mod)
    kept, sent = attention_grads(index, input_a, g_triple, g_attn, attended)
    qp = ring_sum(index, kept[None], sent[None])[0].astype(BF)
    qp = sum_four([qp.astype(F32)] + [swap(qp, "ctx", q).astype(F32) for q in (1, 2, 3)])
    blocks = gather_y(own)
    latent_grad = restore(index, blocks + [swap(b, "tp", 4) for b in blocks])

    cond_pair = jnp.stack([condition, swap(condition, "shard", 1)])
    cond_all = jnp.concatenate([cond_pair, swap(cond_pair, "shard", 2)])
    silu_rows = jax.nn.silu(lax.dynamic_slice_in_dim(cond_all, s * 256, 256, 2).astype(F32)).astype(BF)
    g_mod = sum_four([g_mod] + [swap(g_mod, "ctx", q) for q in (1, 2, 3)])
    g_mod = [lax.dynamic_slice_in_dim(g_mod, (x_lo ^ (b & 1)) * 128, 128, 1) for b in range(4)]
    g_mod = jnp.stack([g_mod[0]] + [swap_x(g_mod[b], b) for b in (1, 2, 3)])
    other = swap(g_mod, "shard", 1)
    g_mod = jnp.stack([(other if i & 1 else g_mod)[2 * (i >> 1) : 2 * (i >> 1) + 2, :12] for i in range(4)])
    g_mod = g_mod.reshape(16, 768)
    silu_grad = silu_rows.astype(F32).reshape(4, 2, 2, 256)
    silu_grad = jnp.where(x_lo == 1, silu_grad[:, ::-1], silu_grad).reshape(16, 256)
    ada_grad = lax.dot_general(silu_grad, g_mod, (((0,), (0,)), ((), ())), precision=HIGHEST)
    ada_f = ada_weight.astype(F32).reshape(256, 768)
    terms = lax.dot_general(g_mod, ada_f, (((1,), (1,)), ((), ())), precision=HIGHEST)
    terms = terms.reshape(4, 2, 2, 256)
    terms = jnp.where(x_lo == 1, terms[:, ::-1], terms).reshape(4, 4, 256)
    theirs = swap(terms[1::2], "shard", 1)
    terms = jnp.stack([terms[0::2], theirs], axis=1)
    got = [terms[0]] + [swap_x(terms[b >> 1], b) for b in (1, 2, 3)]
    terms = jnp.stack([got[0] + got[1], got[2] + got[3]]).reshape(4, 4, 256)
    terms = sum_four([terms] + [swap(terms, "tp", r) for r in (1, 2, 3)])
    cond_own = jnp.concatenate([pick(terms, s ^ i) for i in range(4)], axis=1)
    _, silu_pull = jax.vjp(jax.nn.silu, condition.astype(F32))
    condition_grad = silu_pull(cond_own)[0]

    return (
        latent_out,
        latent_grad,
        condition_grad,
        ada_grad.reshape(256, 6, 128),
        qp[:, :384].reshape(256, 3, 128),
        qp[:, 384:].T,
        ud[0],
        ud[1].T,
    )


def solution(mesh):
    placed = (
        P("shard", "ctx", None),
        P("shard", None),
        P("shard", None, "tp"),
        P("shard", None, "tp"),
        P("tp", "shard"),
        P("shard", "tp"),
        P("tp", "shard"),
        P("shard", "ctx", None),
    )
    return jax.shard_map(
        shards,
        mesh=mesh,
        in_specs=placed,
        out_specs=(
            P("shard", "ctx", None),
            P("shard", "ctx", None),
            P("shard", None),
            P("shard", None, "tp"),
            P("shard", None, "tp"),
            P("tp", "shard"),
            P("shard", "tp"),
            P("tp", "shard"),
        ),
        check_vma=False,
    )
```

```python
import jax
import jax.numpy as jnp
from jax import lax
from jax.experimental import pallas as pl
from jax.experimental.pallas import tpu as pltpu
from jax.sharding import PartitionSpec as P

HD = 64
EPSILON = 1e-06
HIGHEST = lax.Precision.HIGHEST
BF = jnp.bfloat16
F32 = jnp.float32


def swap(value, axis, bits):
    size = {"shard": 4, "ctx": 4, "tp": 8}[axis]
    return lax.ppermute(value, axis, [(i, i ^ bits) for i in range(size)])


def swap_x(value, bits):
    if bits == 1:
        return swap(value, "tp", 4)
    if bits == 2:
        return swap(value, "shard", 2)
    return lax.ppermute(value, ("shard", "tp"), [(i, i ^ 20) for i in range(32)])


def pick(array, index, axis=0):
    return lax.dynamic_index_in_dim(array, index, axis, keepdims=False)


def dot(a, b, contract):
    return lax.dot_general(a, b, (contract, ((), ())), preferred_element_type=F32)


def normalize(rows):
    centred = rows - jnp.mean(rows, axis=-1, keepdims=True)
    inverse = lax.rsqrt(jnp.mean(centred * centred, axis=-1, keepdims=True) + EPSILON)
    return centred * inverse, inverse


def norm_back(grad, normed, inverse):
    first = jnp.mean(grad, axis=-1, keepdims=True)
    second = jnp.mean(grad * normed, axis=-1, keepdims=True)
    return inverse * (grad - first - normed * second)


GELU_A = 0.7978845608028654
GELU_B = 0.044715


def gelu_and_slope(v):
    square = v * v
    t = jnp.tanh(GELU_A * (v + GELU_B * v * square))
    half = 0.5 * (1.0 + t)
    return v * half, half + 0.5 * v * (1.0 - t * t) * (GELU_A * (1.0 + 3.0 * GELU_B * square))


LAT, TOK, FEAT, OUT_LAT, Z_HEAD, X_LO, Z_LAT, TP, COLS = 0, 2, 6, 10, 14, 15, 16, 17, 18


def kernel(body, outs, index, *arrays, scratch=(), after=(), vmem=20, cost=10, name):
    count = 1 + len(arrays)

    def run(*refs):
        body(*refs[:count], *refs[count + len(after) :])

    return pl.pallas_call(
        run,
        in_specs=[pl.BlockSpec(memory_space=pltpu.SMEM)]
        + [pl.BlockSpec(memory_space=pltpu.VMEM)] * len(arrays)
        + [pl.BlockSpec(memory_space=pl.ANY)] * len(after),
        out_specs=[pl.BlockSpec(memory_space=pltpu.VMEM)] * len(outs),
        out_shape=[jax.ShapeDtypeStruct(shape, kind) for shape, kind in outs],
        scratch_shapes=[pltpu.VMEM(shape, kind) for shape, kind in scratch],
        compiler_params=pltpu.CompilerParams(vmem_limit_bytes=vmem * 2**20),
        cost_estimate=pl.CostEstimate(flops=2**cost, bytes_accessed=1024, transcendentals=0),
        name=name,
    )(index, *arrays, *after)


def aligned(start, step):
    return pl.ds(pl.multiple_of(start * step, step), step)


def arrange(index, array, after=()):
    def body(idx, src, *refs):
        dst = refs[-1]
        for r in range(4):
            for l in range(2):
                for i in range(4):
                    dst[r * 128 + l * 64 : r * 128 + l * 64 + 64, i * 256 : (i + 1) * 256] = src[
                        idx[LAT + l] - 2 * idx[X_LO], aligned(idx[TOK + r], 64), aligned(idx[FEAT + i], 256)
                    ]

    return pl.pallas_call(
        body,
        grid_spec=pltpu.PrefetchScalarGridSpec(
            num_scalar_prefetch=1,
            grid=(1,),
            in_specs=[pl.BlockSpec((2, 256, 1024), lambda n, idx: (idx[X_LO], 0, 0))]
            + [pl.BlockSpec(memory_space=pl.ANY)] * len(after),
            out_specs=pl.BlockSpec((512, 1024), lambda n, idx: (0, 0)),
        ),
        out_shape=jax.ShapeDtypeStruct((512, 1024), array.dtype),
        compiler_params=pltpu.CompilerParams(vmem_limit_bytes=16 * 2**20),
        cost_estimate=pl.CostEstimate(flops=2**31, bytes_accessed=1024, transcendentals=0),
        name="arrange",
    )(index, array, *after)


def restore(index, blocks):
    def body(idx, *refs):
        out = refs[-1]
        for x in range(2):
            for r in range(4):
                base = 128 * r if x and len(refs) == 6 else 0
                for l in range(2):
                    for i in range(4):
                        out[idx[OUT_LAT + 2 * x + l], aligned(idx[TOK + r], 64), aligned(idx[FEAT + i], 256)] = refs[
                            min(4 * x + r, len(refs) - 2)
                        ][base + l * 64 : base + l * 64 + 64, i * 256 : (i + 1) * 256].astype(F32)

    return kernel(body, [((4, 256, 1024), F32)], index, *blocks, cost=31, name="restore")[0]


def pack_first(index, qkv, proj, after):
    def body(idx, q_ref, p_ref, out_ref):
        for j in range(3):
            out_ref[:, j * 128 : (j + 1) * 128] = q_ref[:, j]
        for h in range(2):
            out_ref[h * 128 : (h + 1) * 128, 384:512] = p_ref[:, h * 128 : (h + 1) * 128]

    return kernel(body, [((256, 512), BF)], index, qkv, proj, after=after, name="pack_first")[0]


def pack_second(index, up, down, after):
    def body(idx, u_ref, d_ref, out_ref):
        out_ref[0:256] = u_ref[:, 0:256]
        out_ref[256:512] = u_ref[:, 256:512]
        out_ref[512:1024] = d_ref[...]

    return kernel(body, [((1024, 256), BF)], index, up, down, after=after, cost=31, name="pack_second")[0]


def modulate(index, condition, rows, after=()):
    def body(idx, c_ref, a, b, c, d, out_ref):
        total = None
        for i, ref in enumerate((a, b, c, d)):
            silu = jax.nn.silu(c_ref[:, aligned(idx[FEAT + i], 256)].astype(F32)).astype(BF)
            term = dot(silu, ref[...], ((1,), (0,)))
            total = term if total is None else total + term
        out_ref[...] = total.astype(BF).astype(F32)

    return kernel(body, [((4, 768), F32)], index, condition, *rows, after=after, name="modulate")[0]


def mod_split(index, blocks, after):
    def body(idx, a, b, c, d, own_ref, far_ref):
        for r, ref in enumerate((a, b, c, d)):
            low, high = ref[0:2], ref[2:4]
            own_ref[r] = jnp.where(idx[X_LO] == 1, high, low)
            far_ref[r] = jnp.where(idx[X_LO] == 1, low, high)

    return kernel(body, [((4, 2, 768), F32)] * 2, index, *blocks, after=after, name="mod_split")


def mod_assemble(index, own, far):
    def body(idx, own_ref, far_ref, out_ref):
        for p in range(8):
            column = 2 * idx[FEAT + (p >> 1)] + (p & 1)
            source = (column & 3) ^ idx[TOK]
            block = jnp.where(column >> 2 == idx[X_LO], own_ref[source], far_ref[source])
            block = jnp.where(idx[Z_LAT] == 1, jnp.concatenate([block[1:2], block[0:1]], axis=0), block)
            for l in range(2):
                for k in range(6):
                    out_ref[6 * l + k : 6 * l + k + 1, p * 128 : (p + 1) * 128] = block[
                        l : l + 1, k * 128 : (k + 1) * 128
                    ]

    return kernel(body, [((12, 1024), F32)], index, own, far, name="mod_assemble")[0]


def mod_rows(mod, k, width=64):
    return jnp.concatenate(
        [jnp.broadcast_to(mod[6 * l + k : 6 * l + k + 1], (64, mod.shape[1])) for l in range(2)], axis=0
    )


def latent_sums(value):
    return [jnp.sum(value[l * 64 : (l + 1) * 64], axis=0, keepdims=True) for l in range(2)]


def project_in(index, latent, mod, mine, other, after=()):
    def body(idx, x_ref, mod_ref, *refs):
        blocks, (in_ref, w_ref, stat_ref, proj_ref), outs = refs[:8], refs[8:12], refs[12:]
        flip = idx[Z_HEAD] == 1
        for i in range(4):
            pair = [blocks[4 * (i & 1) + 2 * (i >> 1) + j] for j in range(2)]
            for j in range(2):
                block = jnp.where(flip, pair[1 - j][...], pair[j][...])
                w_ref[i * 256 : (i + 1) * 256, j * 384 : (j + 1) * 384] = block[:, 0:384]
                for h in range(2):
                    proj_ref[j * 128 : (j + 1) * 128, i * 256 + h * 128 : i * 256 + (h + 1) * 128] = block[
                        h * 128 : (h + 1) * 128, 384:512
                    ]

        @pl.loop(0, 4)
        def _(r):
            rows = aligned(r, 128)
            x = x_ref[rows].astype(F32)
            centred = x - jnp.mean(x, axis=-1, keepdims=True)
            inverse = lax.rsqrt(jnp.mean(centred * centred, axis=-1, keepdims=True) + EPSILON)
            normed = centred * inverse
            in_ref[rows] = (normed * (1.0 + mod_rows(mod_ref[...], 1)) + mod_rows(mod_ref[...], 0)).astype(BF)
            stat_ref[rows, 0:128] = jnp.broadcast_to(x[:, 0:1] - centred[:, 0:1], (128, 128))
            stat_ref[rows, 128:256] = jnp.broadcast_to(inverse, (128, 128))

        for j in range(2):
            block = dot(in_ref[...], w_ref[:, j * 384 : (j + 1) * 384], ((1,), (0,))).astype(BF)
            block = block.reshape(4, 2, 64, 384)
            for l in range(2):
                outs[2 * l + j][...] = block[:, l].reshape(256, 384)

    return kernel(
        body,
        [((512, 1024), BF), ((1024, 768), BF), ((512, 256), F32), ((256, 1024), BF)] + [((256, 384), BF)] * 4,
        index, latent, mod, *mine, *other, after=after, cost=33, name="project_in",
    )


def assemble(index, blocks):
    def body(idx, in_ref, up_ref, down_ref):
        for i in range(4):
            wide = slice(i * 256, (i + 1) * 256)
            for j in range(2):
                block = in_ref.at[idx[FEAT + i], j]
                up_ref[wide, j * 512 : j * 512 + 256] = block[0:256]
                up_ref[wide, j * 512 + 256 : (j + 1) * 512] = block[256:512]
                down_ref[j * 512 : (j + 1) * 512, wide] = block[512:1024]

    return kernel(body, [((1024, 1024), BF)] * 2, index, blocks, cost=32, name="assemble")


def load_heads(refs, q_s, k_s, v_s):
    for i, ref in enumerate(refs):
        rows = slice(i * 256, (i + 1) * 256)
        q_s[rows] = ref[:, 0:128] * jnp.asarray(HD**-0.5, BF)
        k_s[rows] = ref[:, 128:256]
        v_s[rows] = ref[:, 256:384]


def only_head(block, head, axis):
    lane = lax.broadcasted_iota(jnp.int32, block.shape, axis)
    return jnp.where((lane >= head * HD) & (lane < (head + 1) * HD), block, jnp.zeros_like(block))


def head_probs(k, q_head):
    scores = dot(k, q_head, ((1,), (1,)))
    powered = jnp.exp(scores - jnp.max(scores, axis=0, keepdims=True))
    return powered * (1.0 / jnp.sum(powered, axis=0, keepdims=True))


def attention(index, parts, after=()):
    def body(idx, *refs):
        ins, outs, (q_s, k_s, v_s) = refs[:4], refs[4:8], refs[8:]
        load_heads(ins, q_s, k_s, v_s)
        v_t = v_s[...].T
        for i in range(4):
            q = q_s[i * 256 : (i + 1) * 256]
            total = None
            for head in range(2):
                probs = head_probs(k_s[...], only_head(q, head, 1)).astype(BF)
                term = dot(only_head(v_t, head, 0), probs, ((1,), (0,)))
                total = term if total is None else total + term
            outs[i][...] = total.T.astype(BF)

    return kernel(
        body, [((256, 128), BF)] * 4, index, *parts,
        scratch=[((1024, 128), BF)] * 3, after=after, cost=35, name="attention",
    )


def attention_back(index, parts, grads, after):
    def body(idx, *refs):
        ins, gs, outs = refs[:4], refs[4:8], refs[8:12]
        q_s, k_s, v_s, dk_s, dv_s = refs[12:]
        load_heads(ins, q_s, k_s, v_s)
        k_t = k_s[...].T
        dk_s[...] = jnp.zeros_like(dk_s)
        dv_s[...] = jnp.zeros_like(dv_s)
        for i in range(4):
            q = q_s[i * 256 : (i + 1) * 256]
            g = gs[i][...]
            dq_t = None
            for head in range(2):
                q_head, g_head = only_head(q, head, 1), only_head(g, head, 1)
                probs = head_probs(k_s[...], q_head)
                g_probs = dot(v_s[...], g_head, ((1,), (1,)))
                dv_s[...] += dot(probs.astype(BF), g_head, ((1,), (0,)))
                inner = jnp.sum(probs * g_probs, axis=0, keepdims=True)
                g_scores = (probs * (g_probs - inner)).astype(BF)
                dk_s[...] += dot(g_scores, q_head, ((1,), (0,)))
                term = dot(only_head(k_t, head, 0), g_scores, ((1,), (0,)))
                dq_t = term if dq_t is None else dq_t + term
            outs[i][:, 0:128] = (dq_t.T * HD**-0.5).astype(BF)
        for i in range(4):
            rows = slice(i * 256, (i + 1) * 256)
            outs[i][:, 128:256] = dk_s[rows].astype(BF)
            outs[i][:, 256:384] = dv_s[rows].astype(BF)

    return kernel(
        body, [((256, 384), BF)] * 4, index, *parts, *grads,
        scratch=[((1024, 128), BF)] * 3 + [((1024, 128), F32)] * 2, after=after, cost=36, name="attention_back",
    )


def by_token(refs, dst):
    width = refs[0].shape[-1]
    for l in range(2):
        for j in range(2):
            for r in range(4):
                dst[r * 128 + l * 64 : r * 128 + l * 64 + 64, j * width : (j + 1) * width] = refs[2 * l + j][
                    r * 64 : (r + 1) * 64
                ]


ROWS_OUT = [((128, 1024), F32)] + [((128, 1024), BF)] * 3


def put_rows(value, outs, cols):
    outs[0][:, cols] = value[0:128]
    for r in (1, 2, 3):
        outs[r][0:128, cols] = value[r * 128 : (r + 1) * 128].astype(BF)


def project_out(index, heads, proj):
    def body(idx, a, b, c, d, w_ref, att_ref, *outs):
        by_token((a, b, c, d), att_ref)

        @pl.loop(0, 4)
        def _(n):
            cols = aligned(n, 256)
            put_rows(dot(att_ref[...], w_ref[:, cols], ((1,), (0,))), outs, cols)

    return kernel(body, [((512, 256), BF)] + ROWS_OUT, index, *heads, proj, name="project_out")


def sum_rows(refs):
    return refs[0][...] + (refs[1][0:128].astype(F32) + refs[2][0:128].astype(F32) + refs[3][0:128].astype(F32))


def middle_rows(index, terms, latent, mod, after=()):
    def body(idx, a, b, c, d, x_ref, mod_ref, attn_ref, mid_ref, in_ref):
        mod = mod_ref[...]
        attn = sum_rows((a, b, c, d))
        middle = x_ref[0:128].astype(F32) + mod_rows(mod, 2) * attn
        normed, _ = normalize(middle)
        attn_ref[...] = attn
        mid_ref[...] = middle
        in_ref[...] = (normed * (1.0 + mod_rows(mod, 4)) + mod_rows(mod, 3)).astype(BF)

    outs = [((128, 1024), F32), ((128, 1024), F32), ((128, 1024), BF)]
    return kernel(body, outs, index, *terms, latent, mod, after=after, name="middle_rows")


def grad_mlp(index, grad_out, mod, after=()):
    def body(idx, g_ref, mod_ref, out_ref):
        @pl.loop(0, 4)
        def _(r):
            rows = aligned(r, 128)
            out_ref[rows] = (mod_rows(mod_ref[...], 5) * g_ref[rows].astype(F32)).astype(BF)

    return kernel(body, [((512, 1024), BF)], index, grad_out, mod, after=after, cost=31, name="grad_mlp")[0]


def grad_act(index, g_mlp, down):
    def body(idx, g_ref, w_ref, out_ref):
        @pl.loop(0, 4)
        def _(n):
            out_ref[:, aligned(n, 256)] = dot(g_ref[...], w_ref[aligned(n, 256)], ((1,), (1,)))

    return kernel(body, [((512, 1024), F32)], index, g_mlp, down, cost=33, name="grad_act")[0]


def feed_forward(index, blocks, g_act, up):
    def body(idx, a, b, c, d, g_ref, w_ref, x_ref, act_ref, gup_ref, *outs):
        for r, ref in enumerate((a, b, c, d)):
            x_ref[r * 128 : (r + 1) * 128] = ref[...]

        @pl.loop(0, 4)
        def _(n):
            cols = aligned(n, 256)
            act, slope = gelu_and_slope(dot(x_ref[...], w_ref[:, cols], ((1,), (0,))))
            act_ref[:, cols] = act.astype(BF)
            gup_ref[:, cols] = (g_ref[:, cols] * slope).astype(BF)

        @pl.loop(0, 4)
        def _(n):
            cols = aligned(n, 256)
            put_rows(dot(gup_ref[...], w_ref[cols], ((1,), (1,))), outs, cols)

    return kernel(
        body, [((512, 1024), BF)] * 3 + ROWS_OUT, index, *blocks, g_act, up, name="feed_forward"
    )


def mlp_rows(index, act, down, after=()):
    def body(idx, a_ref, w_ref, *outs):
        @pl.loop(0, 4)
        def _(n):
            cols = aligned(n, 256)
            put_rows(dot(a_ref[...], w_ref[:, cols], ((1,), (0,))), outs, cols)

    return kernel(body, ROWS_OUT, index, act, down, after=after, cost=33, name="mlp_rows")


def hidden_grads(index, rows, g_up, g_mlp, act):
    def body(idx, x_ref, gup_ref, gm_ref, act_ref, kept_ref, sent_ref):
        for n, (left, right) in enumerate(((x_ref, gup_ref), (gm_ref, act_ref))):
            for i in range(4):
                turned = left[:, i * 256 : (i + 1) * 256].T
                dst = sent_ref if i & 1 else kept_ref

                @pl.loop(0, 4)
                def _(m):
                    cols = aligned(m, 256)
                    dst[n, i >> 1, :, cols] = dot(turned, right[:, cols], ((1,), (0,)))

    return kernel(
        body, [((2, 2, 256, 1024), F32)] * 2, index, rows, g_up, g_mlp, act, cost=33, name="hidden_grads"
    )


def out_rows(index, terms, middle, grad_out, mod):
    def body(idx, a, b, c, d, mid_ref, g_ref, mod_ref, out_ref, row_ref):
        mlp = sum_rows((a, b, c, d))
        out_ref[...] = (mid_ref[...] + mod_rows(mod_ref[...], 5) * mlp).astype(BF)
        sums = latent_sums(g_ref[0:128].astype(F32) * mlp)
        row_ref[...] = jnp.zeros_like(row_ref)
        for l in range(2):
            row_ref[l : l + 1] = sums[l]

    outs = [((128, 1024), BF), ((8, 1024), F32)]
    return kernel(body, outs, index, *terms, middle, grad_out, mod, cost=30, name="out_rows")


def middle_back(index, terms, middle, attn, grad_out, mod, after=()):
    def body(idx, a, b, c, d, mid_ref, attn_ref, g_ref, mod_ref, gmid_ref, gattn_ref, row_ref):
        mod = mod_ref[...]
        g_in = sum_rows((a, b, c, d))
        normed, inverse = normalize(mid_ref[...])
        g_mid = g_ref[0:128].astype(F32) + norm_back(g_in * (1.0 + mod_rows(mod, 4)), normed, inverse)
        gmid_ref[...] = g_mid
        gattn_ref[...] = (mod_rows(mod, 2) * g_mid).astype(BF)
        row_ref[...] = jnp.zeros_like(row_ref)
        for k, value in enumerate((g_mid * attn_ref[...], g_in, g_in * normed)):
            sums = latent_sums(value)
            for l in range(2):
                row_ref[3 * l + k : 3 * l + k + 1] = sums[l]

    outs = [((128, 1024), F32), ((128, 1024), BF), ((8, 1024), F32)]
    return kernel(body, outs, index, *terms, middle, attn, grad_out, mod, after=after, name="middle_back")


def heads_back(index, blocks, proj, after=()):
    def body(idx, a, b, c, d, w_ref, g_ref, *outs):
        for r, ref in enumerate((a, b, c, d)):
            g_ref[r * 128 : (r + 1) * 128] = ref[...]
        for j in range(2):
            block = dot(g_ref[...], w_ref[j * 128 : (j + 1) * 128], ((1,), (1,))).astype(BF).reshape(4, 2, 64, 128)
            for l in range(2):
                outs[2 * l + j][...] = block[:, l].reshape(256, 128)

    outs = [((512, 1024), BF)] + [((256, 128), BF)] * 4
    return kernel(body, outs, index, *blocks, proj, after=after, cost=35, name="heads_back")


def input_back(index, blocks, w_qkv, latent, stats, row_mlp, rows_mid, after):
    def body(idx, a, b, c, d, w_ref, x_ref, stat_ref, row5_ref, row234_ref, g_ref, *rest):
        outs, own_ref, gm = rest[:4], rest[4], rest[5]
        by_token((a, b, c, d), g_ref)
        gm[...] = jnp.zeros_like(gm)

        @pl.loop(0, 4)
        def _(n):
            cols = aligned(n, 256)
            value = dot(g_ref[...], w_ref[cols], ((1,), (1,)))
            put_rows(value, outs, cols)
            mean = jnp.concatenate([stat_ref[:, 0:128]] * 2, axis=1)
            inverse = jnp.concatenate([stat_ref[:, 128:256]] * 2, axis=1)
            scaled = value * ((x_ref[:, cols].astype(F32) - mean) * inverse)
            for l in range(2):
                for k, part in enumerate((value, scaled)):
                    total = part.reshape(4, 2, 64, 256)[:, l].reshape(256, 256)
                    gm[6 * l + k : 6 * l + k + 1, cols] = jnp.sum(total, axis=0, keepdims=True)

        for l in range(2):
            for k in range(3):
                gm[6 * l + 2 + k : 6 * l + 3 + k] = row234_ref[3 * l + k : 3 * l + k + 1]
            gm[6 * l + 5 : 6 * l + 6] = row5_ref[l : l + 1]
        for r in range(4):
            for x in range(2):
                block = gm[:, aligned(idx[COLS + 2 * r + x], 128)]
                flipped = jnp.concatenate([block[6:12], block[0:6], block[12:16]], axis=0)
                block = jnp.where(idx[Z_LAT] == 1, flipped, block)
                if r == 0:
                    own_ref[:, x * 128 : (x + 1) * 128] = block
                else:
                    high = block.astype(BF)
                    outs[r][128:144, x * 128 : (x + 1) * 128] = high
                    outs[r][128:144, 256 + x * 128 : 384 + x * 128] = (block - high.astype(F32)).astype(BF)
                    outs[r][128:144, 512 + x * 256 : 768 + x * 256] = jnp.zeros((16, 256), BF)

    return kernel(
        body,
        [((512, 768), BF), ((128, 1024), F32)] + [((144, 1024), BF)] * 3 + [((16, 256), F32)],
        index, *blocks, w_qkv, latent, stats, row_mlp, rows_mid,
        scratch=[((16, 1024), F32)], after=after, name="input_back",
    )


def attention_grads(index, rows, g_triple, g_attn, attended, after=()):
    def body(idx, x_ref, gt_ref, ga_ref, att_ref, kept_ref, sent_ref):
        for i in range(4):
            dst = sent_ref if i & 1 else kept_ref
            x_t = x_ref[:, i * 256 : (i + 1) * 256].T
            g_t = ga_ref[:, i * 256 : (i + 1) * 256].T
            for j in range(2):
                start = (j ^ idx[Z_HEAD]) * 512
                dst[i >> 1, :, pl.ds(pl.multiple_of(start, 512), 384)] = dot(
                    x_t, gt_ref[:, j * 384 : (j + 1) * 384], ((1,), (0,))
                )
                dst[i >> 1, :, pl.ds(pl.multiple_of(start + 384, 128), 128)] = dot(
                    g_t, att_ref[:, j * 128 : (j + 1) * 128], ((1,), (0,))
                )

    return kernel(
        body, [((2, 256, 1024), F32)] * 2, index, rows, g_triple, g_attn, attended, after=after, cost=33, name="attention_grads"
    )


def latent_back(index, terms, g_mod, g_mid, latent, mod, after=()):
    def body(idx, a, b, c, d, gm_ref, gmid_ref, x_ref, mod_ref, out_ref, sum_ref):
        normed, inverse = normalize(x_ref[0:128].astype(F32))
        g_in = sum_rows((a, b, c, d)) * (1.0 + mod_rows(mod_ref[...], 1))
        out_ref[...] = (gmid_ref[...] + norm_back(g_in, normed, inverse)).astype(BF)
        total = gm_ref[...]
        for ref in (b, c, d):
            total = total + (ref[128:144, 0:256].astype(F32) + ref[128:144, 256:512].astype(F32))
        sum_ref[...] = total

    return kernel(
        body, [((128, 1024), BF), ((16, 256), F32)], index, *terms, g_mod, g_mid, latent, mod, after=after, cost=35, name="latent_back"
    )


def mod_sum(index, terms):
    def body(idx, a, b, c, d, own_ref, far_ref, sum_s):
        sum_s[...] = (a[...] + b[...]) + (c[...] + d[...])
        own_ref[...] = sum_s[:, aligned(idx[X_LO], 128)]
        far_ref[...] = sum_s[:, aligned(1 - idx[X_LO], 128)]

    outs = [((16, 128), F32)] * 2
    return kernel(body, outs, index, *terms, scratch=[((16, 256), F32)], name="mod_sum")


def cond_terms(index, own, far, rows):
    def body(idx, own_ref, far_ref, a, b, c, d, out_ref, g_s):
        g_s[...] = jnp.zeros_like(g_s)
        for x, ref in enumerate((own_ref, far_ref)):
            for l in range(2):
                for k in range(6):
                    g_s[2 * x + l : 2 * x + l + 1, k * 128 : (k + 1) * 128] = ref[6 * l + k : 6 * l + k + 1]
        value = g_s[...]
        value = jnp.where(idx[X_LO] == 1, jnp.concatenate([value[2:4], value[0:2], value[4:8]], axis=0), value)
        high = value.astype(BF)
        rest = value - high.astype(F32)
        middle = rest.astype(BF)
        low = (rest - middle.astype(F32)).astype(BF)
        parts = jnp.concatenate([high.astype(F32), middle.astype(F32), low.astype(F32)], axis=0).astype(BF)
        for i, ref in enumerate((a, b, c, d)):
            term = dot(parts, ref[...], ((1,), (1,)))
            out_ref[:, i * 256 : (i + 1) * 256] = term[0:8] + (term[8:16] + term[16:24])

    return kernel(
        body, [((8, 1024), F32)], index, own, far, *rows, scratch=[((8, 768), F32)], name="cond_terms"
    )[0]


def ada_grads(index, mine, other, conds):
    def body(idx, *refs):
        mine, other, conds, out_ref, g_s, s_s = refs[:4], refs[4], refs[5:9], refs[9], refs[10], refs[11]
        for i, ref in enumerate(conds):
            rows = jax.nn.silu(ref[:, aligned(idx[FEAT], 256)].astype(F32)).astype(BF).astype(F32)
            flipped = jnp.concatenate([rows[2:4], rows[0:2]], axis=0)
            s_s[4 * i : 4 * i + 4] = jnp.where(idx[X_LO] == 1, flipped, rows)
        g_s[...] = jnp.zeros_like(g_s)
        for b in range(4):
            for c in range(2):
                block = other[b] if c else mine[b][...]
                for l in range(2):
                    row = (2 * (b >> 1) + c) * 4 + 2 * (b & 1) + l
                    for k in range(6):
                        g_s[row : row + 1, k * 128 : (k + 1) * 128] = block[6 * l + k : 6 * l + k + 1]
        silu = s_s[...].T
        for k in range(6):
            out_ref[:, k, :] = lax.dot_general(
                silu, g_s[:, k * 128 : (k + 1) * 128], (((1,), (0,)), ((), ())), precision=HIGHEST
            )

    return kernel(
        body, [((256, 6, 128), F32)], index, *mine, other, *conds, scratch=[((16, 768), F32), ((16, 256), F32)], name="ada_grads"
    )[0]


def core_sum(index, kept, got, after=()):
    count = kept.shape[0]

    def body(idx, kept_ref, got_ref, own_ref, *outs):
        for n in range(count):
            for b in range(4):
                cols = slice((b & 1) * 512, (b & 1) * 512 + 512)
                value = kept_ref[n, b >> 1, :, cols] + got_ref[n, b >> 1, :, cols]
                if b == 0:
                    own_ref[n] = value
                else:
                    outs[b - 1][n] = value.astype(BF)

    outs = [((count, 256, 512), F32)] + [((count, 256, 512), BF)] * 3
    return kernel(body, outs, index, kept, got, after=after, cost=31, name="core_sum")


def exchange_y(blocks):
    return [blocks[0]] + [swap(blocks[r], "tp", r) for r in (1, 2, 3)]


def gather_y(block):
    return [block] + [swap(block, "tp", r) for r in (1, 2, 3)]


def exchange_z(blocks):
    return [blocks[0]] + [swap(blocks[q], "ctx", q) for q in (1, 2, 3)]


def gather_x(block):
    mine = [block] + [swap_x(block, b) for b in (1, 2, 3)]
    return mine, [swap(b, "shard", 1) for b in mine]


def ring_sends(index, kept, sent, after=()):
    return core_sum(index, kept, swap(sent, "shard", 1), after)


def ring_total(own, *sends):
    got = [swap_x(sends[b - 1], b).astype(F32) for b in (1, 2, 3)]
    return own + (got[0] + got[1] + got[2])


def sum_four(terms):
    return (terms[0] + terms[1]) + (terms[2] + terms[3])


def shards(
    latent_in, condition, ada_weight, qkv_weight, proj_weight, up_matrix, down_matrix, out_grad
):
    s, z, t = lax.axis_index("shard"), lax.axis_index("ctx"), lax.axis_index("tp")
    x_lo, y, z_lat, z_head = t >> 2, t & 3, z >> 1, z & 1
    columns = [[((4 * x + (y ^ r)) >> 1 ^ s) * 2 + ((y ^ r) & 1) for x in range(2)] for r in range(4)]
    index = jnp.stack(
        [2 * x_lo + (l ^ z_lat) for l in range(2)]
        + [y ^ r for r in range(4)]
        + [s ^ i for i in range(4)]
        + [2 * (x_lo ^ x) + (l ^ z_lat) for x in range(2) for l in range(2)]
        + [z_head, x_lo, z_lat, t]
        + [c for pair in columns for c in pair]
    ).astype(jnp.int32)

    ada = ada_weight.reshape(256, 768)
    ada_far = swap(ada, "shard", 2)
    ada_rows = [ada, swap(ada, "shard", 1), ada_far, swap(ada_far, "shard", 1)]
    latent = arrange(index, latent_in)
    packed = pack_first(index, qkv_weight, proj_weight, (ada_far,))
    first = gather_x(packed)
    mod_cols = modulate(index, condition, ada_rows, (packed,))
    mod_own, mod_far = mod_split(index, gather_y(mod_cols), (latent,))
    mod = mod_assemble(index, mod_own, swap(mod_far, "tp", 4))

    input_a, w_qkv, stats, proj, *parts = project_in(index, latent, mod, *first)
    packed = pack_second(index, up_matrix, down_matrix, (mod,))
    packed = lax.all_gather(jnp.stack([packed, swap(packed, "tp", 4)]), "shard", axis=0)
    up, down = assemble(index, packed)
    grad_out = arrange(index, out_grad, (input_a,))
    conds = [condition, swap(condition, "shard", 1), swap(condition, "shard", 2)]
    conds.append(swap(conds[1], "shard", 2))
    parts = exchange_z(parts)
    g_mlp = grad_mlp(index, grad_out, mod, (input_a,))
    g_act = grad_act(index, g_mlp, down)

    heads = exchange_z(attention(index, parts, (g_mlp, *conds[1:])))
    attended, *terms = project_out(index, heads, proj)
    attn, middle, input_b = middle_rows(index, exchange_y(terms), latent, mod)
    rows_b, act, g_up, *terms = feed_forward(index, gather_y(input_b), g_act, up)
    ud_kept, ud_sent = hidden_grads(index, rows_b, g_up, g_mlp, act)
    g_mid, g_attn, rows_mid = middle_back(index, exchange_y(terms), middle, attn, grad_out, mod, (ud_kept,))
    g_attn, *g_parts = heads_back(index, gather_y(g_attn), proj)
    mlp_terms = mlp_rows(index, act, down, (g_parts[0],))
    ud_sends = ring_sends(index, ud_kept, ud_sent, (g_parts[0],))
    g_parts = exchange_z(g_parts)

    g_blocks = exchange_z(attention_back(index, parts, g_parts, (mlp_terms[0],)))
    out_block, row_mlp = out_rows(index, exchange_y(mlp_terms), middle, grad_out, mod)
    out_blocks = gather_y(out_block)
    ud = ring_total(*ud_sends)

    g_triple, *rest = input_back(index, g_blocks, w_qkv, latent, stats, row_mlp, rows_mid, (ud, *out_blocks[1:]))
    ud = lax.psum(ud, "ctx")
    out_far = swap(jnp.concatenate(out_blocks), "tp", 4)
    kept, sent = attention_grads(index, input_a, g_triple, g_attn, attended)
    own, g_mod = latent_back(index, exchange_y(rest[:4]), rest[4], g_mid, latent, mod, (kept,))
    qp = ring_total(*ring_sends(index, kept[None], sent[None], (own,)))[0].astype(BF)
    qp = sum_four([qp.astype(F32)] + [swap(qp, "ctx", q).astype(F32) for q in (1, 2, 3)])
    blocks = gather_y(own)
    latent_grad = restore(index, blocks + [swap(b, "tp", 4) for b in blocks])
    latent_out = restore(index, out_blocks + [out_far])

    mod_own, mod_far = mod_sum(index, [g_mod] + [swap(g_mod, "ctx", q) for q in (1, 2, 3)])
    mine = [mod_own, swap_x(mod_far, 1), swap_x(mod_own, 2), swap_x(mod_far, 3)]
    other = swap(jnp.stack(mine), "shard", 1)
    ada_grad = ada_grads(index, mine, other, conds)
    terms = cond_terms(index, mine[0], mine[1], ada_rows)
    terms = terms + swap(terms, "tp", 4)
    terms = sum_four([terms] + [swap(terms, "tp", r) for r in (1, 2, 3)])
    cond_own = jnp.concatenate(
        [lax.dynamic_slice_in_dim(terms, (s ^ i) * 256, 256, 1) for i in range(4)], axis=1
    )[:4]
    _, silu_pull = jax.vjp(jax.nn.silu, condition.astype(F32))
    condition_grad = silu_pull(cond_own)[0]

    return (
        latent_out,
        latent_grad,
        condition_grad,
        ada_grad,
        qp[:, :384].reshape(256, 3, 128),
        qp[:, 384:].T,
        ud[0],
        ud[1].T,
    )


def solution(mesh):
    placed = (
        P("shard", "ctx", None),
        P("shard", None),
        P("shard", None, "tp"),
        P("shard", None, "tp"),
        P("tp", "shard"),
        P("shard", "tp"),
        P("tp", "shard"),
        P("shard", "ctx", None),
    )
    return jax.shard_map(
        shards,
        mesh=mesh,
        in_specs=placed,
        out_specs=(
            P("shard", "ctx", None),
            P("shard", "ctx", None),
            P("shard", None),
            P("shard", None, "tp"),
            P("shard", None, "tp"),
            P("tp", "shard"),
            P("shard", "tp"),
            P("tp", "shard"),
        ),
        check_vma=False,
    )
```

```python
import jax
import jax.numpy as jnp
from jax import lax
from jax.experimental import pallas as pl
from jax.experimental.pallas import tpu as pltpu
from jax.sharding import PartitionSpec as P

HD = 64
EPSILON = 1e-06
HIGHEST = lax.Precision.HIGHEST
BF = jnp.bfloat16
F32 = jnp.float32


def swap(value, axis, bits):
    size = {"shard": 4, "ctx": 4, "tp": 8}[axis]
    return lax.ppermute(value, axis, [(i, i ^ bits) for i in range(size)])


def swap_x(value, bits):
    if bits == 1:
        return swap(value, "tp", 4)
    if bits == 2:
        return swap(value, "shard", 2)
    return lax.ppermute(value, ("shard", "tp"), [(i, i ^ 20) for i in range(32)])


def pick(array, index, axis=0):
    return lax.dynamic_index_in_dim(array, index, axis, keepdims=False)


def dot(a, b, contract):
    return lax.dot_general(a, b, (contract, ((), ())), preferred_element_type=F32)


def normalize(rows):
    centred = rows - jnp.mean(rows, axis=-1, keepdims=True)
    inverse = lax.rsqrt(jnp.mean(centred * centred, axis=-1, keepdims=True) + EPSILON)
    return centred * inverse, inverse


def norm_back(grad, normed, inverse):
    first = jnp.mean(grad, axis=-1, keepdims=True)
    second = jnp.mean(grad * normed, axis=-1, keepdims=True)
    return inverse * (grad - first - normed * second)


GELU_A = 0.7978845608028654
GELU_B = 0.044715


def gelu_and_slope(v):
    square = v * v
    t = jnp.tanh(GELU_A * (v + GELU_B * v * square))
    half = 0.5 * (1.0 + t)
    return v * half, half + 0.5 * v * (1.0 - t * t) * (GELU_A * (1.0 + 3.0 * GELU_B * square))


LAT, TOK, FEAT, OUT_LAT, Z_HEAD, X_LO, Z_LAT, TP, COLS = 0, 2, 6, 10, 14, 15, 16, 17, 18


def kernel(body, outs, index, *arrays, scratch=(), after=(), vmem=24, cost=10, space=None, name):
    count = 1 + len(arrays)

    def run(*refs):
        body(*refs[:count], *refs[count + len(after) :])

    return pl.pallas_call(
        run,
        in_specs=[pl.BlockSpec(memory_space=pltpu.SMEM)]
        + [pl.BlockSpec()] * len(arrays)
        + [pl.BlockSpec(memory_space=pl.ANY)] * len(after),
        out_specs=[pl.BlockSpec(memory_space=space)] * len(outs),
        out_shape=[jax.ShapeDtypeStruct(shape, kind) for shape, kind in outs],
        scratch_shapes=[pltpu.VMEM(shape, kind) for shape, kind in scratch],
        compiler_params=pltpu.CompilerParams(vmem_limit_bytes=vmem * 2**20),
        cost_estimate=pl.CostEstimate(flops=2**cost, bytes_accessed=1024, transcendentals=0),
        name=name,
    )(index, *arrays, *after)


def aligned(start, step):
    return pl.ds(pl.multiple_of(start * step, step), step)


def arrange(index, array, after=()):
    def body(idx, src, *refs):
        dst = refs[-1]
        for r in range(4):
            for l in range(2):
                for i in range(4):
                    dst[r * 128 + l * 64 : r * 128 + l * 64 + 64, i * 256 : (i + 1) * 256] = src[
                        idx[LAT + l] - 2 * idx[X_LO], aligned(idx[TOK + r], 64), aligned(idx[FEAT + i], 256)
                    ]

    return pl.pallas_call(
        body,
        grid_spec=pltpu.PrefetchScalarGridSpec(
            num_scalar_prefetch=1,
            grid=(1,),
            in_specs=[pl.BlockSpec((2, 256, 1024), lambda n, idx: (idx[X_LO], 0, 0))]
            + [pl.BlockSpec(memory_space=pl.ANY)] * len(after),
            out_specs=pl.BlockSpec((512, 1024), lambda n, idx: (0, 0)),
        ),
        out_shape=jax.ShapeDtypeStruct((512, 1024), array.dtype),
        compiler_params=pltpu.CompilerParams(vmem_limit_bytes=16 * 2**20),
        cost_estimate=pl.CostEstimate(flops=2**31, bytes_accessed=1024, transcendentals=0),
        name="arrange",
    )(index, array, *after)


def restore(index, blocks):
    def body(idx, *refs):
        out = refs[-1]
        for x in range(2):
            for r in range(4):
                for l in range(2):
                    for i in range(4):
                        out[idx[OUT_LAT + 2 * x + l], aligned(idx[TOK + r], 64), aligned(idx[FEAT + i], 256)] = refs[
                            4 * x + r
                        ][l * 64 : l * 64 + 64, i * 256 : (i + 1) * 256].astype(F32)

    return kernel(body, [((4, 256, 1024), F32)], index, *blocks, cost=31, name="restore")[0]


def pack_first(index, qkv, proj, after):
    def body(idx, q_ref, p_ref, out_ref):
        for j in range(3):
            out_ref[:, j * 128 : (j + 1) * 128] = q_ref[:, j]
        for h in range(2):
            out_ref[h * 128 : (h + 1) * 128, 384:512] = p_ref[:, h * 128 : (h + 1) * 128]

    return kernel(body, [((256, 512), BF)], index, qkv, proj, after=after, name="pack_first")[0]


def pack_second(index, up, down, after):
    def body(idx, u_ref, d_ref, out_ref):
        out_ref[0:256] = u_ref[:, 0:256]
        out_ref[256:512] = u_ref[:, 256:512]
        out_ref[512:1024] = d_ref[...]

    return kernel(body, [((1024, 256), BF)], index, up, down, after=after, cost=31, name="pack_second")[0]


def mod_terms(index, conds, ada):
    def body(idx, a, b, c, d, w_ref, kept_ref, sent_ref, s_s):
        for i, ref in enumerate((a, b, c, d)):
            s_s[4 * i : 4 * i + 4] = jax.nn.silu(ref[:, aligned(idx[FEAT], 256)].astype(F32))
        terms = dot(s_s[...].astype(BF), w_ref[...], ((1,), (0,)))
        for h in range(2):
            kept_ref[4 * h : 4 * h + 4] = terms[8 * h : 8 * h + 4]
            sent_ref[4 * h : 4 * h + 4] = terms[8 * h + 4 : 8 * h + 8]

    return kernel(
        body, [((8, 768), F32)] * 2, index, *conds, ada, scratch=[((16, 256), F32)], name="mod_terms"
    )


def mod_core(index, kept, got):
    def body(idx, a, b, *outs):
        value = a[...] + b[...]
        for n in range(4):
            rows = value[4 * (n >> 1) : 4 * (n >> 1) + 4]
            wanted = idx[X_LO] ^ (n & 1)
            outs[n][...] = jnp.where(wanted == 1, rows[2:4], rows[0:2])

    return kernel(body, [((2, 768), F32)] * 4, index, kept, got, name="mod_core")


def mod_ring(index, terms):
    def body(idx, a, b, c, d, out_ref):
        out_ref[0] = (a[...] + c[...]).astype(BF).astype(F32)
        out_ref[1] = (b[...] + d[...]).astype(BF).astype(F32)

    return kernel(body, [((2, 2, 768), F32)], index, *terms, name="mod_ring")[0]


def mod_assemble(index, near, far, after):
    def body(idx, near_ref, far_ref, out_ref, all_s):
        all_s[0:4] = near_ref[...]
        all_s[4:8] = far_ref[...]
        for p in range(8):
            column = 2 * idx[FEAT + (p >> 1)] + (p & 1)
            block = all_s[2 * ((column & 3) ^ idx[TOK]) + ((column >> 2) ^ idx[X_LO])]
            block = jnp.where(idx[Z_LAT] == 1, jnp.concatenate([block[1:2], block[0:1]], axis=0), block)
            for l in range(2):
                for k in range(6):
                    out_ref[6 * l + k : 6 * l + k + 1, p * 128 : (p + 1) * 128] = block[
                        l : l + 1, k * 128 : (k + 1) * 128
                    ]

    return kernel(
        body, [((12, 1024), F32)], index, near, far, scratch=[((8, 2, 768), F32)], after=after, name="mod_assemble"
    )[0]


def stack_blocks(index, blocks, after):
    rows, width = blocks[0].shape

    def body(idx, *refs):
        for r, ref in enumerate(refs[:-1]):
            refs[-1][r * rows : (r + 1) * rows] = ref[...]

    outs = [((len(blocks) * rows, width), BF)]
    return kernel(body, outs, index, *blocks, after=after, cost=31, name="stack_blocks")[0]


def mod_rows(mod, k, width=64):
    return jnp.concatenate(
        [jnp.broadcast_to(mod[6 * l + k : 6 * l + k + 1], (64, mod.shape[1])) for l in range(2)], axis=0
    )


def latent_sums(value):
    return [jnp.sum(value[l * 64 : (l + 1) * 64], axis=0, keepdims=True) for l in range(2)]


def project_in(index, latent, mod, mine, other, after=()):
    def body(idx, x_ref, mod_ref, *refs):
        blocks, (in_ref, w_ref, stat_ref, proj_ref), outs = refs[:2], refs[2:6], refs[6:]
        flip = idx[Z_HEAD] == 1
        for i in range(4):
            pair = [blocks[i & 1][2 * (i >> 1) + j] for j in range(2)]
            for j in range(2):
                block = jnp.where(flip, pair[1 - j], pair[j])
                w_ref[i * 256 : (i + 1) * 256, j * 384 : (j + 1) * 384] = block[:, 0:384]
                for h in range(2):
                    proj_ref[j * 128 : (j + 1) * 128, i * 256 + h * 128 : i * 256 + (h + 1) * 128] = block[
                        h * 128 : (h + 1) * 128, 384:512
                    ]

        @pl.loop(0, 4)
        def _(r):
            rows = aligned(r, 128)
            x = x_ref[rows].astype(F32)
            centred = x - jnp.mean(x, axis=-1, keepdims=True)
            inverse = lax.rsqrt(jnp.mean(centred * centred, axis=-1, keepdims=True) + EPSILON)
            normed = centred * inverse
            in_ref[rows] = (normed * (1.0 + mod_rows(mod_ref[...], 1)) + mod_rows(mod_ref[...], 0)).astype(BF)
            stat_ref[rows, 0:128] = jnp.broadcast_to(x[:, 0:1] - centred[:, 0:1], (128, 128))
            stat_ref[rows, 128:256] = jnp.broadcast_to(inverse, (128, 128))

        for j in range(2):
            block = dot(in_ref[...], w_ref[:, j * 384 : (j + 1) * 384], ((1,), (0,))).astype(BF)
            block = block.reshape(4, 2, 64, 384)
            for l in range(2):
                outs[2 * l + j][...] = block[:, l].reshape(256, 384)

    return kernel(
        body,
        [((512, 1024), BF), ((1024, 768), BF), ((512, 256), F32), ((256, 1024), BF)] + [((256, 384), BF)] * 4,
        index, latent, mod, mine, other, after=after, cost=33, name="project_in",
    )


def assemble(index, blocks):
    def body(idx, ref, up_ref, down_ref):
        for i in range(4):
            wide = slice(i * 256, (i + 1) * 256)
            for j in range(2):
                block = ref.at[idx[FEAT + i]]
                rows = j * 1024
                up_ref[wide, j * 512 : j * 512 + 256] = block[rows : rows + 256]
                up_ref[wide, j * 512 + 256 : (j + 1) * 512] = block[rows + 256 : rows + 512]
                down_ref[j * 512 : (j + 1) * 512, wide] = block[rows + 512 : rows + 1024]

    return kernel(body, [((1024, 1024), BF)] * 2, index, blocks, cost=32, name="assemble")


def load_heads(refs, q_s, k_s, v_s):
    for i, ref in enumerate(refs):
        rows = slice(i * 256, (i + 1) * 256)
        q_s[rows] = ref[:, 0:128] * jnp.asarray(HD**-0.5, BF)
        k_s[rows] = ref[:, 128:256]
        v_s[rows] = ref[:, 256:384]


def only_head(block, head, axis):
    lane = lax.broadcasted_iota(jnp.int32, block.shape, axis)
    return jnp.where((lane >= head * HD) & (lane < (head + 1) * HD), block, jnp.zeros_like(block))


def head_probs(k, q_head):
    scores = dot(k, q_head, ((1,), (1,)))
    powered = jnp.exp(scores - jnp.max(scores, axis=0, keepdims=True))
    return powered * (1.0 / jnp.sum(powered, axis=0, keepdims=True))


def attention(index, parts, after=()):
    def body(idx, *refs):
        ins, outs, (q_s, k_s, v_s) = refs[:4], refs[4:8], refs[8:]
        load_heads(ins, q_s, k_s, v_s)
        v_t = v_s[...].T
        for i in range(4):
            q = q_s[i * 256 : (i + 1) * 256]
            total = None
            for head in range(2):
                probs = head_probs(k_s[...], only_head(q, head, 1)).astype(BF)
                term = dot(only_head(v_t, head, 0), probs, ((1,), (0,)))
                total = term if total is None else total + term
            outs[i][...] = total.T.astype(BF)

    return kernel(
        body, [((256, 128), BF)] * 4, index, *parts,
        scratch=[((1024, 128), BF)] * 3, after=after, cost=35, name="attention",
    )


def attention_back(index, parts, grads, after):
    def body(idx, *refs):
        ins, gs, outs = refs[:4], refs[4:8], refs[8:12]
        q_s, k_s, v_s, dk_s, dv_s = refs[12:]
        load_heads(ins, q_s, k_s, v_s)
        k_t = k_s[...].T
        dk_s[...] = jnp.zeros_like(dk_s)
        dv_s[...] = jnp.zeros_like(dv_s)
        for i in range(4):
            q = q_s[i * 256 : (i + 1) * 256]
            g = gs[i][...]
            dq_t = None
            for head in range(2):
                q_head, g_head = only_head(q, head, 1), only_head(g, head, 1)
                probs = head_probs(k_s[...], q_head)
                g_probs = dot(v_s[...], g_head, ((1,), (1,)))
                dv_s[...] += dot(probs.astype(BF), g_head, ((1,), (0,)))
                inner = jnp.sum(probs * g_probs, axis=0, keepdims=True)
                g_scores = (probs * (g_probs - inner)).astype(BF)
                dk_s[...] += dot(g_scores, q_head, ((1,), (0,)))
                term = dot(only_head(k_t, head, 0), g_scores, ((1,), (0,)))
                dq_t = term if dq_t is None else dq_t + term
            outs[i][:, 0:128] = (dq_t.T * HD**-0.5).astype(BF)
        for i in range(4):
            rows = slice(i * 256, (i + 1) * 256)
            outs[i][:, 128:256] = dk_s[rows].astype(BF)
            outs[i][:, 256:384] = dv_s[rows].astype(BF)

    return kernel(
        body, [((256, 384), BF)] * 4, index, *parts, *grads,
        scratch=[((1024, 128), BF)] * 3 + [((1024, 128), F32)] * 2, after=after, cost=36, name="attention_back",
    )


def by_token(refs, dst):
    width = refs[0].shape[-1]
    for l in range(2):
        for j in range(2):
            for r in range(4):
                dst[r * 128 + l * 64 : r * 128 + l * 64 + 64, j * width : (j + 1) * width] = refs[2 * l + j][
                    r * 64 : (r + 1) * 64
                ]


ROWS_OUT = [((128, 1024), F32)] + [((128, 1024), BF)] * 3


def put_rows(value, outs, cols):
    outs[0][:, cols] = value[0:128]
    for r in (1, 2, 3):
        outs[r][0:128, cols] = value[r * 128 : (r + 1) * 128].astype(BF)


def project_out(index, heads, proj):
    def body(idx, a, b, c, d, w_ref, att_ref, *outs):
        by_token((a, b, c, d), att_ref)

        @pl.loop(0, 4)
        def _(n):
            cols = aligned(n, 256)
            put_rows(dot(att_ref[...], w_ref[:, cols], ((1,), (0,))), outs, cols)

    return kernel(body, [((512, 256), BF)] + ROWS_OUT, index, *heads, proj, name="project_out")


def sum_rows(refs):
    return refs[0][...] + (refs[1][0:128].astype(F32) + refs[2][0:128].astype(F32) + refs[3][0:128].astype(F32))


def middle_rows(index, terms, latent, mod, after=()):
    def body(idx, a, b, c, d, x_ref, mod_ref, attn_ref, mid_ref, in_ref):
        mod = mod_ref[...]
        attn = sum_rows((a, b, c, d))
        middle = x_ref[0:128].astype(F32) + mod_rows(mod, 2) * attn
        normed, _ = normalize(middle)
        attn_ref[...] = attn
        mid_ref[...] = middle
        in_ref[...] = (normed * (1.0 + mod_rows(mod, 4)) + mod_rows(mod, 3)).astype(BF)

    outs = [((128, 1024), F32), ((128, 1024), F32), ((128, 1024), BF)]
    return kernel(body, outs, index, *terms, latent, mod, after=after, cost=35, name="middle_rows")


def grad_mlp(index, grad_out, mod, after=()):
    def body(idx, g_ref, mod_ref, out_ref):
        @pl.loop(0, 4)
        def _(r):
            rows = aligned(r, 128)
            out_ref[rows] = (mod_rows(mod_ref[...], 5) * g_ref[rows].astype(F32)).astype(BF)

    return kernel(body, [((512, 1024), BF)], index, grad_out, mod, after=after, cost=31, name="grad_mlp")[0]


def grad_act(index, g_mlp, down):
    def body(idx, g_ref, w_ref, out_ref):
        @pl.loop(0, 4)
        def _(n):
            out_ref[:, aligned(n, 256)] = dot(g_ref[...], w_ref[aligned(n, 256)], ((1,), (1,)))

    return kernel(body, [((512, 1024), F32)], index, g_mlp, down, cost=33, name="grad_act")[0]


def feed_forward(index, blocks, g_act, up):
    def body(idx, a, b, c, d, g_ref, w_ref, x_ref, act_ref, gup_ref, *outs):
        for r, ref in enumerate((a, b, c, d)):
            x_ref[r * 128 : (r + 1) * 128] = ref[...]

        @pl.loop(0, 4)
        def _(n):
            cols = aligned(n, 256)
            act, slope = gelu_and_slope(dot(x_ref[...], w_ref[:, cols], ((1,), (0,))))
            act_ref[:, cols] = act.astype(BF)
            gup_ref[:, cols] = (g_ref[:, cols] * slope).astype(BF)

        @pl.loop(0, 4)
        def _(n):
            cols = aligned(n, 256)
            put_rows(dot(gup_ref[...], w_ref[cols], ((1,), (1,))), outs, cols)

    return kernel(
        body, [((512, 1024), BF)] * 3 + ROWS_OUT, index, *blocks, g_act, up, name="feed_forward"
    )


def mlp_rows(index, act, down, after=()):
    def body(idx, a_ref, w_ref, *outs):
        @pl.loop(0, 4)
        def _(n):
            cols = aligned(n, 256)
            put_rows(dot(a_ref[...], w_ref[:, cols], ((1,), (0,))), outs, cols)

    return kernel(body, ROWS_OUT, index, act, down, after=after, cost=33, name="mlp_rows")


def hidden_grads(index, rows, g_up, g_mlp, act):
    def body(idx, x_ref, gup_ref, gm_ref, act_ref, kept_ref, sent_ref):
        for n, (left, right) in enumerate(((x_ref, gup_ref), (gm_ref, act_ref))):
            for i in range(4):
                turned = left[:, i * 256 : (i + 1) * 256].T
                dst = sent_ref if i & 1 else kept_ref

                @pl.loop(0, 4)
                def _(m):
                    cols = aligned(m, 256)
                    dst[n, i >> 1, :, cols] = dot(turned, right[:, cols], ((1,), (0,))).astype(dst.dtype)

    return kernel(
        body, [((2, 2, 256, 1024), F32), ((2, 2, 256, 1024), BF)], index, rows, g_up, g_mlp, act, cost=33, space=pltpu.VMEM, vmem=24, name="hidden_grads"
    )


def out_rows(index, terms, middle, grad_out, mod, after):
    def body(idx, a, b, c, d, mid_ref, g_ref, mod_ref, out_ref, row_ref):
        mlp = sum_rows((a, b, c, d))
        out_ref[...] = (mid_ref[...] + mod_rows(mod_ref[...], 5) * mlp).astype(BF)
        sums = latent_sums(g_ref[0:128].astype(F32) * mlp)
        row_ref[...] = jnp.zeros_like(row_ref)
        for l in range(2):
            row_ref[l : l + 1] = sums[l]

    outs = [((128, 1024), BF), ((8, 1024), F32)]
    return kernel(body, outs, index, *terms, middle, grad_out, mod, after=after, cost=30, name="out_rows")


def middle_back(index, terms, middle, attn, grad_out, mod, after=()):
    def body(idx, a, b, c, d, mid_ref, attn_ref, g_ref, mod_ref, gmid_ref, gattn_ref, row_ref):
        mod = mod_ref[...]
        g_in = sum_rows((a, b, c, d))
        normed, inverse = normalize(mid_ref[...])
        g_mid = g_ref[0:128].astype(F32) + norm_back(g_in * (1.0 + mod_rows(mod, 4)), normed, inverse)
        gmid_ref[...] = g_mid
        gattn_ref[...] = (mod_rows(mod, 2) * g_mid).astype(BF)
        row_ref[...] = jnp.zeros_like(row_ref)
        for k, value in enumerate((g_mid * attn_ref[...], g_in, g_in * normed)):
            sums = latent_sums(value)
            for l in range(2):
                row_ref[3 * l + k : 3 * l + k + 1] = sums[l]

    outs = [((128, 1024), F32), ((128, 1024), BF), ((8, 1024), F32)]
    return kernel(body, outs, index, *terms, middle, attn, grad_out, mod, after=after, cost=35, name="middle_back")


def heads_back(index, blocks, proj, after=()):
    def body(idx, a, b, c, d, w_ref, g_ref, *outs):
        for r, ref in enumerate((a, b, c, d)):
            g_ref[r * 128 : (r + 1) * 128] = ref[...]
        for j in range(2):
            block = dot(g_ref[...], w_ref[j * 128 : (j + 1) * 128], ((1,), (1,))).astype(BF).reshape(4, 2, 64, 128)
            for l in range(2):
                outs[2 * l + j][...] = block[:, l].reshape(256, 128)

    outs = [((512, 1024), BF)] + [((256, 128), BF)] * 4
    return kernel(body, outs, index, *blocks, proj, after=after, name="heads_back")


def input_back(index, blocks, w_qkv, latent, stats, row_mlp, rows_mid, after):
    def body(idx, a, b, c, d, w_ref, x_ref, stat_ref, row5_ref, row234_ref, g_ref, *rest):
        outs, own_ref, gm = rest[:4], rest[4], rest[5]
        by_token((a, b, c, d), g_ref)
        gm[...] = jnp.zeros_like(gm)

        @pl.loop(0, 4)
        def _(n):
            cols = aligned(n, 256)
            value = dot(g_ref[...], w_ref[cols], ((1,), (1,)))
            put_rows(value, outs, cols)
            mean = jnp.concatenate([stat_ref[:, 0:128]] * 2, axis=1)
            inverse = jnp.concatenate([stat_ref[:, 128:256]] * 2, axis=1)
            scaled = value * ((x_ref[:, cols].astype(F32) - mean) * inverse)
            for l in range(2):
                for k, part in enumerate((value, scaled)):
                    total = part.reshape(4, 2, 64, 256)[:, l].reshape(256, 256)
                    gm[6 * l + k : 6 * l + k + 1, cols] = jnp.sum(total, axis=0, keepdims=True)

        for l in range(2):
            for k in range(3):
                gm[6 * l + 2 + k : 6 * l + 3 + k] = row234_ref[3 * l + k : 3 * l + k + 1]
            gm[6 * l + 5 : 6 * l + 6] = row5_ref[l : l + 1]
        for r in range(4):
            for x in range(2):
                block = gm[:, aligned(idx[COLS + 2 * r + x], 128)]
                flipped = jnp.concatenate([block[6:12], block[0:6], block[12:16]], axis=0)
                block = jnp.where(idx[Z_LAT] == 1, flipped, block)
                if r == 0:
                    own_ref[:, x * 128 : (x + 1) * 128] = block
                else:
                    high = block.astype(BF)
                    outs[r][128:144, x * 128 : (x + 1) * 128] = high
                    outs[r][128:144, 256 + x * 128 : 384 + x * 128] = (block - high.astype(F32)).astype(BF)
                    outs[r][128:144, 512 + x * 256 : 768 + x * 256] = jnp.zeros((16, 256), BF)

    return kernel(
        body,
        [((512, 768), BF), ((128, 1024), F32)] + [((144, 1024), BF)] * 3 + [((16, 256), F32)],
        index, *blocks, w_qkv, latent, stats, row_mlp, rows_mid,
        scratch=[((16, 1024), F32)], after=after, name="input_back",
    )


def attention_grads(index, rows, g_triple, g_attn, attended, after=()):
    def body(idx, x_ref, gt_ref, ga_ref, att_ref, kept_ref, sent_ref):
        for i in range(4):
            dst = sent_ref if i & 1 else kept_ref
            x_t = x_ref[:, i * 256 : (i + 1) * 256].T
            g_t = ga_ref[:, i * 256 : (i + 1) * 256].T
            for j in range(2):
                start = (j ^ idx[Z_HEAD]) * 512
                dst[i >> 1, :, pl.ds(pl.multiple_of(start, 512), 384)] = dot(
                    x_t, gt_ref[:, j * 384 : (j + 1) * 384], ((1,), (0,))
                ).astype(dst.dtype)
                dst[i >> 1, :, pl.ds(pl.multiple_of(start + 384, 128), 128)] = dot(
                    g_t, att_ref[:, j * 128 : (j + 1) * 128], ((1,), (0,))
                ).astype(dst.dtype)

    return kernel(
        body, [((2, 256, 1024), F32), ((2, 256, 1024), BF)], index, rows, g_triple, g_attn, attended, after=after, cost=33, name="attention_grads"
    )


def latent_back(index, terms, g_mod, g_mid, latent, mod, after=()):
    def body(idx, a, b, c, d, gm_ref, gmid_ref, x_ref, mod_ref, out_ref, sum_ref):
        normed, inverse = normalize(x_ref[0:128].astype(F32))
        g_in = sum_rows((a, b, c, d)) * (1.0 + mod_rows(mod_ref[...], 1))
        out_ref[...] = (gmid_ref[...] + norm_back(g_in, normed, inverse)).astype(BF)
        total = gm_ref[...]
        for ref in (b, c, d):
            total = total + (ref[128:144, 0:256].astype(F32) + ref[128:144, 256:512].astype(F32))
        sum_ref[...] = total

    return kernel(
        body, [((128, 1024), BF), ((16, 256), F32)], index, *terms, g_mod, g_mid, latent, mod, after=after, cost=35, name="latent_back"
    )


def mod_sum(index, near, far, after):
    def body(idx, a, b, own_ref, far_ref, sum_s):
        sum_s[...] = a[...] + b[...]
        own_ref[...] = sum_s[:, aligned(idx[X_LO], 128)]
        far_ref[...] = sum_s[:, aligned(1 - idx[X_LO], 128)]

    outs = [((16, 128), F32)] * 2
    return kernel(body, outs, index, near, far, scratch=[((16, 256), F32)], after=after, name="mod_sum")


def cond_terms(index, near, rows, after):
    def body(idx, near_ref, rows_ref, out_ref, g_s):
        g_s[...] = jnp.zeros_like(g_s)
        for x in range(2):
            for l in range(2):
                for k in range(6):
                    g_s[2 * x + l : 2 * x + l + 1, k * 128 : (k + 1) * 128] = near_ref[x, 6 * l + k : 6 * l + k + 1]
        value = g_s[...]
        value = jnp.where(idx[X_LO] == 1, jnp.concatenate([value[2:4], value[0:2], value[4:8]], axis=0), value)
        high = value.astype(BF)
        rest = value - high.astype(F32)
        middle = rest.astype(BF)
        low = (rest - middle.astype(F32)).astype(BF)
        parts = jnp.concatenate([high.astype(F32), middle.astype(F32), low.astype(F32)], axis=0).astype(BF)
        for i in range(4):
            term = dot(parts, rows_ref[i], ((1,), (1,)))
            out_ref[:, i * 256 : (i + 1) * 256] = term[0:8] + (term[8:16] + term[16:24])

    return kernel(
        body, [((8, 1024), F32)], index, near, rows, scratch=[((8, 768), F32)], after=after, name="cond_terms"
    )[0]


def ada_grads(index, near, far, other, conds, after):
    def body(idx, *refs):
        near, far, other, conds, out_ref, g_s, s_s = *refs[:3], refs[3:7], *refs[7:]
        for i, ref in enumerate(conds):
            rows = jax.nn.silu(ref[:, aligned(idx[FEAT], 256)].astype(F32)).astype(BF).astype(F32)
            flipped = jnp.concatenate([rows[2:4], rows[0:2]], axis=0)
            s_s[4 * i : 4 * i + 4] = jnp.where(idx[X_LO] == 1, flipped, rows)
        g_s[...] = jnp.zeros_like(g_s)
        for b in range(4):
            for c in range(2):
                block = other[b] if c else (near, far)[b >> 1][b & 1]
                for l in range(2):
                    row = (2 * (b >> 1) + c) * 4 + 2 * (b & 1) + l
                    for k in range(6):
                        g_s[row : row + 1, k * 128 : (k + 1) * 128] = block[6 * l + k : 6 * l + k + 1]
        silu = s_s[...].T
        for k in range(6):
            out_ref[:, k, :] = lax.dot_general(
                silu, g_s[:, k * 128 : (k + 1) * 128], (((1,), (0,)), ((), ())), precision=HIGHEST
            )

    return kernel(
        body, [((256, 6, 128), F32)], index, near, far, other, *conds,
        scratch=[((16, 768), F32), ((16, 256), F32)], after=after, name="ada_grads"
    )[0]


def hidden_core(index, kept, got, after):
    count = kept.shape[0]

    def body(idx, kept_ref, got_ref, own_ref, out_ref):
        for n in range(count):
            for h in range(2):
                own_ref[n, h] = kept_ref[n, h, :, 0:512] + got_ref[n, h, :, 0:512].astype(F32)
                out_ref[n, h] = (kept_ref[n, h, :, 512:1024] + got_ref[n, h, :, 512:1024].astype(F32)).astype(BF)

    outs = [((count, 2, 256, 512), F32), ((count, 2, 256, 512), BF)]
    return kernel(body, outs, index, kept, got, after=after, cost=31, name="hidden_core")


def hidden_x_lo(index, own, got, after):
    count = own.shape[0]

    def body(idx, own_ref, got_ref, kept_ref, out_ref):
        for n in range(count):
            kept_ref[n] = own_ref[n, 0] + got_ref[n, 0].astype(F32)
            out_ref[n] = (own_ref[n, 1] + got_ref[n, 1].astype(F32)).astype(BF)

    outs = [((count, 256, 512), F32), ((count, 256, 512), BF)]
    return kernel(body, outs, index, own, got, after=after, cost=31, name="hidden_x_lo")


def pair_sum(index, own, got, after):
    def body(idx, own_ref, got_ref, out_ref):
        out_ref[...] = (own_ref[...].astype(F32) + got_ref[...].astype(F32)).astype(BF)

    return kernel(body, [(own.shape, BF)], index, own, got, after=after, cost=31, name="pair_sum")[0]


def hidden_out(index, own, got, after):
    def body(idx, own_ref, got_ref, up_ref, down_ref):
        up_ref[...] = own_ref[0].astype(F32) + got_ref[0].astype(F32)
        down_ref[...] = (own_ref[1].astype(F32) + got_ref[1].astype(F32)).T

    outs = [((256, 512), F32), ((512, 256), F32)]
    return kernel(body, outs, index, own, got, after=after, cost=31, name="hidden_out")


def attention_out(index, own, got):
    def body(idx, a, b, qkv_ref, proj_ref):
        def total(cols):
            return a[0, :, cols].astype(F32) + b[0, :, cols].astype(F32)

        for j in range(3):
            qkv_ref[:, j, :] = total(slice(j * 128, (j + 1) * 128))
        proj_ref[...] = total(slice(384, 512)).T

    return kernel(body, [((256, 3, 128), F32), ((128, 256), F32)], index, own, got, name="attention_out")


def exchange_y(blocks):
    return [blocks[0]] + [swap(blocks[r], "tp", r) for r in (1, 2, 3)]


def gather_y(block):
    return [block] + [swap(block, "tp", r) for r in (1, 2, 3)]


def gather_tp(block):
    near = gather_y(block)
    far = swap(block, "tp", 4)
    return near + [far, swap(far, "tp", 1), swap(near[2], "tp", 4), swap(far, "tp", 3)]


def exchange_z(blocks):
    return [blocks[0]] + [swap(blocks[q], "ctx", q) for q in (1, 2, 3)]


def sum_four(terms):
    return (terms[0] + terms[1]) + (terms[2] + terms[3])


def shards(
    latent_in, condition, ada_weight, qkv_weight, proj_weight, up_matrix, down_matrix, out_grad
):
    s, z, t = lax.axis_index("shard"), lax.axis_index("ctx"), lax.axis_index("tp")
    x_lo, y, z_lat, z_head = t >> 2, t & 3, z >> 1, z & 1
    columns = [[((4 * x + (y ^ r)) >> 1 ^ s) * 2 + ((y ^ r) & 1) for x in range(2)] for r in range(4)]
    index = jnp.stack(
        [2 * x_lo + (l ^ z_lat) for l in range(2)]
        + [y ^ r for r in range(4)]
        + [s ^ i for i in range(4)]
        + [2 * (x_lo ^ x) + (l ^ z_lat) for x in range(2) for l in range(2)]
        + [z_head, x_lo, z_lat, t]
        + [c for pair in columns for c in pair]
    ).astype(jnp.int32)

    ada = ada_weight.reshape(256, 768)
    conds = [condition] + [swap(condition, "shard", i) for i in (1, 2, 3)]
    kept, sent = mod_terms(index, conds, ada)
    terms = mod_core(index, kept, swap(sent, "shard", 1))
    terms = [terms[0]] + [swap_x(terms[b], b) for b in (1, 2, 3)]
    packed = pack_first(index, qkv_weight, proj_weight, tuple(terms[1:]))
    first = [packed] + [swap_x(packed, b) for b in (1, 2, 3)]
    packed = pack_second(index, up_matrix, down_matrix, tuple(terms[1:]))
    mod_x = mod_ring(index, terms)
    near = jnp.concatenate([mod_x, swap(mod_x, "tp", 1)])
    latent = arrange(index, latent_in)
    mod = mod_assemble(index, near, swap(near, "tp", 2), (latent,))
    first = jnp.stack(first)
    packed = stack_blocks(index, [packed, swap(packed, "tp", 4)], (mod,))
    hidden_all = lax.all_gather(packed, "shard", axis=0)

    input_a, w_qkv, stats, proj, *parts = project_in(index, latent, mod, first, swap(first, "shard", 1))
    up, down = assemble(index, hidden_all)
    grad_out = arrange(index, out_grad, (input_a,))
    parts = exchange_z(parts)
    g_mlp = grad_mlp(index, grad_out, mod, (input_a,))
    g_act = grad_act(index, g_mlp, down)

    heads = exchange_z(attention(index, parts, (g_mlp, packed)))
    attended, *terms = project_out(index, heads, proj)
    attn, middle, input_b = middle_rows(index, exchange_y(terms), latent, mod)
    rows_b, act, g_up, *terms = feed_forward(index, gather_y(input_b), g_act, up)
    ud_kept, ud_sent = hidden_grads(index, rows_b, g_up, g_mlp, act)
    g_mid, g_attn, rows_mid = middle_back(index, exchange_y(terms), middle, attn, grad_out, mod, (ud_kept,))
    mlp_terms = mlp_rows(index, act, down, (g_attn,))
    ud, ud_sent = hidden_core(index, ud_kept, swap(ud_sent, "shard", 1), (mlp_terms[0],))
    g_attn, *g_parts = heads_back(index, gather_y(g_attn), proj, (ud,))
    g_parts = exchange_z(g_parts)

    ada_all = lax.all_gather(ada, "shard", axis=0)
    g_blocks = attention_back(index, parts, g_parts, (ada_all,))
    out_block, row_mlp = out_rows(index, exchange_y(mlp_terms), middle, grad_out, mod, (g_blocks[0],))
    ud, ud_sent = hidden_x_lo(index, ud, swap(ud_sent, "tp", 4), (out_block,))
    out_blocks = gather_tp(out_block)
    g_blocks = exchange_z(g_blocks)
    g_triple, *rest = input_back(
        index, g_blocks, w_qkv, latent, stats, row_mlp, rows_mid, (ud, *out_blocks[1:4])
    )
    ud_got = swap(ud_sent, "shard", 2)
    ud = pair_sum(index, ud, ud_got, (rest[0],))
    kept, sent = attention_grads(index, input_a, g_triple, g_attn, attended)
    own, g_mod = latent_back(index, exchange_y(rest[:4]), rest[4], g_mid, latent, mod, (kept, ud))

    qp, qp_sent = hidden_core(index, kept[None], swap(sent[None], "shard", 1), (own,))
    blocks = gather_tp(own)
    g_mod = g_mod + swap(g_mod, "ctx", 1)
    mod_own, mod_far = mod_sum(index, g_mod, swap(g_mod, "ctx", 2), (qp,))
    near = jnp.stack([mod_own, swap(mod_far, "tp", 4)])
    qp, qp_sent = hidden_x_lo(index, qp, swap(qp_sent, "tp", 4), tuple(blocks[1:4]))
    terms = cond_terms(index, near, ada_all, (qp,))
    ud = pair_sum(index, ud, swap(ud, "ctx", 1), (terms,))
    qp = pair_sum(index, qp, swap(qp_sent, "shard", 2), (terms,))
    far = swap(near, "shard", 2)
    terms = terms + swap(terms, "tp", 4)
    ada_grad = ada_grads(index, near, far, swap(jnp.concatenate([near, far]), "shard", 1), conds, (qp, ud))
    terms = terms + swap(terms, "tp", 1)
    qp = pair_sum(index, qp, swap(qp, "ctx", 1), (ada_grad,))
    latent_grad = restore(index, blocks)
    latent_out = restore(index, out_blocks)
    up_grad, down_grad = hidden_out(index, ud, swap(ud, "ctx", 2), (qp,))
    terms = terms + swap(terms, "tp", 2)
    qkv_grad, proj_grad = attention_out(index, qp, swap(qp, "ctx", 2))
    _, silu_pull = jax.vjp(jax.nn.silu, condition.astype(F32))
    condition_grad = silu_pull(terms[:4])[0]

    return (
        latent_out,
        latent_grad,
        condition_grad,
        ada_grad,
        qkv_grad,
        proj_grad,
        up_grad,
        down_grad,
    )


def solution(mesh):
    placed = (
        P("shard", "ctx", None),
        P("shard", None),
        P("shard", None, "tp"),
        P("shard", None, "tp"),
        P("tp", "shard"),
        P("shard", "tp"),
        P("tp", "shard"),
        P("shard", "ctx", None),
    )
    return jax.shard_map(
        shards,
        mesh=mesh,
        in_specs=placed,
        out_specs=(
            P("shard", "ctx", None),
            P("shard", "ctx", None),
            P("shard", None),
            P("shard", None, "tp"),
            P("shard", None, "tp"),
            P("tp", "shard"),
            P("shard", "tp"),
            P("tp", "shard"),
        ),
        check_vma=False,
    )
```

```python
import jax
import jax.numpy as jnp
from jax import lax
from jax.experimental import pallas as pl
from jax.experimental.pallas import tpu as pltpu
from jax.sharding import PartitionSpec as P

HD = 64
EPSILON = 1e-06
HIGHEST = lax.Precision.HIGHEST
BF = jnp.bfloat16
F32 = jnp.float32


def swap(value, axis, bits):
    size = {"shard": 4, "ctx": 4, "tp": 8}[axis]
    return lax.ppermute(value, axis, [(i, i ^ bits) for i in range(size)])


def swap_x(value, bits):
    if bits == 1:
        return swap(value, "tp", 4)
    if bits == 2:
        return swap(value, "shard", 2)
    return lax.ppermute(value, ("shard", "tp"), [(i, i ^ 20) for i in range(32)])


def pick(array, index, axis=0):
    return lax.dynamic_index_in_dim(array, index, axis, keepdims=False)


def dot(a, b, contract):
    return lax.dot_general(a, b, (contract, ((), ())), preferred_element_type=F32)


def normalize(rows):
    centred = rows - jnp.mean(rows, axis=-1, keepdims=True)
    inverse = lax.rsqrt(jnp.mean(centred * centred, axis=-1, keepdims=True) + EPSILON)
    return centred * inverse, inverse


def norm_back(grad, normed, inverse):
    first = jnp.mean(grad, axis=-1, keepdims=True)
    second = jnp.mean(grad * normed, axis=-1, keepdims=True)
    return inverse * (grad - first - normed * second)


GELU_A = 0.7978845608028654
GELU_B = 0.044715


def gelu_and_slope(v):
    square = v * v
    t = jnp.tanh(GELU_A * (v + GELU_B * v * square))
    half = 0.5 * (1.0 + t)
    return v * half, half + 0.5 * v * (1.0 - t * t) * (GELU_A * (1.0 + 3.0 * GELU_B * square))


LAT, TOK, FEAT, OUT_LAT, Z_HEAD, X_LO, Z_LAT, TP, COLS = 0, 2, 6, 10, 14, 15, 16, 17, 18


def kernel(body, outs, index, *arrays, scratch=(), after=(), vmem=16, cost=10, space=None, token=False, name):
    count = 1 + len(arrays)

    outs = list(outs)
    if token:
        outs.append(((8, 128), F32))

    def run(*refs):
        results = refs[count + len(after) :]
        if token:
            place = len(outs) - 1
            results[place][...] = jnp.zeros((8, 128), F32)
            results = results[:place] + results[place + 1 :]
        body(*refs[:count], *results)

    return pl.pallas_call(
        run,
        in_specs=[pl.BlockSpec(memory_space=pltpu.SMEM)]
        + [pl.BlockSpec()] * len(arrays)
        + [pl.BlockSpec(memory_space=pl.ANY)] * len(after),
        out_specs=[pl.BlockSpec(memory_space=space)] * len(outs),
        out_shape=[jax.ShapeDtypeStruct(shape, kind) for shape, kind in outs],
        scratch_shapes=[pltpu.VMEM(shape, kind) for shape, kind in scratch],
        compiler_params=pltpu.CompilerParams(vmem_limit_bytes=vmem * 2**20),
        cost_estimate=pl.CostEstimate(flops=2**cost, bytes_accessed=1024, transcendentals=0),
        name=name,
    )(index, *arrays, *after)


def aligned(start, step):
    return pl.ds(pl.multiple_of(start * step, step), step)


def arrange(index, array, after=()):
    def body(idx, src, *refs):
        dst = refs[-1]
        for r in range(4):
            for l in range(2):
                for i in range(4):
                    dst[r * 128 + l * 64 : r * 128 + l * 64 + 64, i * 256 : (i + 1) * 256] = src[
                        idx[LAT + l] - 2 * idx[X_LO], aligned(idx[TOK + r], 64), aligned(idx[FEAT + i], 256)
                    ]

    return pl.pallas_call(
        body,
        grid_spec=pltpu.PrefetchScalarGridSpec(
            num_scalar_prefetch=1,
            grid=(1,),
            in_specs=[pl.BlockSpec((2, 256, 1024), lambda n, idx: (idx[X_LO], 0, 0))]
            + [pl.BlockSpec(memory_space=pl.ANY)] * len(after),
            out_specs=pl.BlockSpec((512, 1024), lambda n, idx: (0, 0)),
        ),
        out_shape=jax.ShapeDtypeStruct((512, 1024), array.dtype),
        compiler_params=pltpu.CompilerParams(vmem_limit_bytes=16 * 2**20),
        cost_estimate=pl.CostEstimate(flops=2**31, bytes_accessed=1024, transcendentals=0),
        name="arrange",
    )(index, array, *after)


def restore(index, blocks, after=()):
    def body(idx, *refs):
        out = refs[-1]
        for x in range(2):
            for r in range(4):
                for l in range(2):
                    for i in range(4):
                        out[idx[OUT_LAT + 2 * x + l], aligned(idx[TOK + r], 64), aligned(idx[FEAT + i], 256)] = refs[
                            4 * x + r
                        ][l * 64 : l * 64 + 64, i * 256 : (i + 1) * 256].astype(F32)

    return kernel(body, [((4, 256, 1024), F32)], index, *blocks, after=after, cost=31, token=True, name="restore")


def pack_first(index, qkv, proj, after):
    def body(idx, q_ref, p_ref, out_ref):
        for j in range(3):
            out_ref[:, j * 128 : (j + 1) * 128] = q_ref[:, j]
        for h in range(2):
            out_ref[h * 128 : (h + 1) * 128, 384:512] = p_ref[:, h * 128 : (h + 1) * 128]

    return kernel(body, [((256, 512), BF)], index, qkv, proj, after=after, name="pack_first")[0]


def pack_second(index, up, down, after):
    def body(idx, u_ref, d_ref, out_ref):
        out_ref[0:256] = u_ref[:, 0:256]
        out_ref[256:512] = u_ref[:, 256:512]
        out_ref[512:1024] = d_ref[...]

    return kernel(body, [((1024, 256), BF)], index, up, down, after=after, cost=31, name="pack_second")[0]


def mod_terms(index, conds, ada):
    def body(idx, a, b, c, d, w_ref, kept_ref, sent_ref, s_s):
        for i, ref in enumerate((a, b, c, d)):
            s_s[4 * i : 4 * i + 4] = jax.nn.silu(ref[:, aligned(idx[FEAT], 256)].astype(F32))
        terms = dot(s_s[...].astype(BF), w_ref[...], ((1,), (0,)))
        for h in range(2):
            kept_ref[4 * h : 4 * h + 4] = terms[8 * h : 8 * h + 4]
            sent_ref[4 * h : 4 * h + 4] = terms[8 * h + 4 : 8 * h + 8]

    return kernel(
        body, [((8, 768), F32)] * 2, index, *conds, ada, scratch=[((16, 256), F32)], name="mod_terms"
    )


def mod_core(index, kept, got):
    def body(idx, a, b, *outs):
        value = a[...] + b[...]
        for n in range(4):
            rows = value[4 * (n >> 1) : 4 * (n >> 1) + 4]
            wanted = idx[X_LO] ^ (n & 1)
            outs[n][...] = jnp.where(wanted == 1, rows[2:4], rows[0:2])

    return kernel(body, [((2, 768), F32)] * 4, index, kept, got, name="mod_core")


def mod_ring(index, terms):
    def body(idx, a, b, c, d, out_ref):
        out_ref[0] = (a[...] + c[...]).astype(BF).astype(F32)
        out_ref[1] = (b[...] + d[...]).astype(BF).astype(F32)

    return kernel(body, [((2, 2, 768), F32)], index, *terms, name="mod_ring")[0]


def mod_assemble(index, near, far, after):
    def body(idx, near_ref, far_ref, out_ref, all_s):
        all_s[0:4] = near_ref[...]
        all_s[4:8] = far_ref[...]
        for p in range(8):
            column = 2 * idx[FEAT + (p >> 1)] + (p & 1)
            block = all_s[2 * ((column & 3) ^ idx[TOK]) + ((column >> 2) ^ idx[X_LO])]
            block = jnp.where(idx[Z_LAT] == 1, jnp.concatenate([block[1:2], block[0:1]], axis=0), block)
            for l in range(2):
                for k in range(6):
                    out_ref[6 * l + k : 6 * l + k + 1, p * 128 : (p + 1) * 128] = block[
                        l : l + 1, k * 128 : (k + 1) * 128
                    ]

    return kernel(
        body, [((12, 1024), F32)], index, near, far, scratch=[((8, 2, 768), F32)], after=after, token=True, name="mod_assemble"
    )


def stack_blocks(index, blocks, after):
    rows, width = blocks[0].shape

    def body(idx, *refs):
        for r, ref in enumerate(refs[:-1]):
            refs[-1][r * rows : (r + 1) * rows] = ref[...]

    outs = [((len(blocks) * rows, width), BF)]
    return kernel(body, outs, index, *blocks, after=after, cost=31, token=True, name="stack_blocks")


def mod_rows(mod, k, width=64):
    return jnp.concatenate(
        [jnp.broadcast_to(mod[6 * l + k : 6 * l + k + 1], (64, mod.shape[1])) for l in range(2)], axis=0
    )


def latent_sums(value):
    return [jnp.sum(value[l * 64 : (l + 1) * 64], axis=0, keepdims=True) for l in range(2)]


def project_in(index, latent, mod, mine, other, after=()):
    def body(idx, x_ref, mod_ref, *refs):
        blocks, (in_ref, w_ref, stat_ref, proj_ref), outs = refs[:2], refs[2:6], refs[6:]
        flip = idx[Z_HEAD] == 1
        for i in range(4):
            pair = [blocks[i & 1][2 * (i >> 1) + j] for j in range(2)]
            for j in range(2):
                block = jnp.where(flip, pair[1 - j], pair[j])
                w_ref[i * 256 : (i + 1) * 256, j * 384 : (j + 1) * 384] = block[:, 0:384]
                for h in range(2):
                    proj_ref[j * 128 : (j + 1) * 128, i * 256 + h * 128 : i * 256 + (h + 1) * 128] = block[
                        h * 128 : (h + 1) * 128, 384:512
                    ]

        @pl.loop(0, 4)
        def _(r):
            rows = aligned(r, 128)
            x = x_ref[rows].astype(F32)
            centred = x - jnp.mean(x, axis=-1, keepdims=True)
            inverse = lax.rsqrt(jnp.mean(centred * centred, axis=-1, keepdims=True) + EPSILON)
            normed = centred * inverse
            in_ref[rows] = (normed * (1.0 + mod_rows(mod_ref[...], 1)) + mod_rows(mod_ref[...], 0)).astype(BF)
            stat_ref[rows, 0:128] = jnp.broadcast_to(x[:, 0:1] - centred[:, 0:1], (128, 128))
            stat_ref[rows, 128:256] = jnp.broadcast_to(inverse, (128, 128))

        for j in range(2):
            block = dot(in_ref[...], w_ref[:, j * 384 : (j + 1) * 384], ((1,), (0,))).astype(BF)
            block = block.reshape(4, 2, 64, 384)
            for l in range(2):
                outs[2 * l + j][...] = block[:, l].reshape(256, 384)

    return kernel(
        body,
        [((512, 1024), BF), ((1024, 768), BF), ((512, 256), F32), ((256, 1024), BF)] + [((256, 384), BF)] * 4,
        index, latent, mod, mine, other, after=after, cost=33, token=True, name="project_in",
    )


def assemble(index, blocks):
    def body(idx, ref, up_ref, down_ref):
        for i in range(4):
            wide = slice(i * 256, (i + 1) * 256)
            for j in range(2):
                block = ref.at[idx[FEAT + i]]
                rows = j * 1024
                up_ref[wide, j * 512 : j * 512 + 256] = block[rows : rows + 256]
                up_ref[wide, j * 512 + 256 : (j + 1) * 512] = block[rows + 256 : rows + 512]
                down_ref[j * 512 : (j + 1) * 512, wide] = block[rows + 512 : rows + 1024]

    return kernel(body, [((1024, 1024), BF)] * 2, index, blocks, cost=32, name="assemble")


def only_head(block, head, axis):
    lane = lax.broadcasted_iota(jnp.int32, block.shape, axis)
    return jnp.where((lane >= head * HD) & (lane < (head + 1) * HD), block, jnp.zeros_like(block))


def head_probs(k, q_head):
    scores = dot(k, q_head, ((1,), (1,)))
    powered = jnp.exp(scores - jnp.max(scores, axis=0, keepdims=True))
    return powered * (1.0 / jnp.sum(powered, axis=0, keepdims=True))


def attention(index, parts, after=()):
    def body(idx, *refs):
        ins, all_ref, outs, out_s = refs[:4], refs[4], refs[5:9], refs[9]
        for i, ref in enumerate(ins):
            rows = slice(i * 256, (i + 1) * 256)
            all_ref[rows, 0:128] = ref[:, 0:128] * jnp.asarray(HD**-0.5, BF)
            all_ref[rows, 128:384] = ref[:, 128:384]
        v_t = all_ref[:, 256:384].T

        @pl.loop(0, 4)
        def _(i):
            rows = aligned(i, 256)
            q = all_ref[rows, 0:128]
            total = None
            for head in range(2):
                probs = head_probs(all_ref[:, 128:256], only_head(q, head, 1)).astype(BF)
                term = dot(only_head(v_t, head, 0), probs, ((1,), (0,)))
                total = term if total is None else total + term
            out_s[rows] = total.T.astype(BF)

        for i in range(4):
            outs[i][...] = out_s[i * 256 : (i + 1) * 256]

    return kernel(
        body, [((1024, 384), BF)] + [((256, 128), BF)] * 4, index, *parts,
        scratch=[((1024, 128), BF)], after=after, cost=35, name="attention",
    )


def attention_back(index, qkv, grads, after):
    def body(idx, all_ref, *refs):
        gs, outs, (g_s, dq_s, dk_s, dv_s) = refs[:4], refs[4:8], refs[8:]
        for i in range(4):
            g_s[i * 256 : (i + 1) * 256] = gs[i][...]
        k_t = all_ref[:, 128:256].T
        dk_s[...] = jnp.zeros_like(dk_s)
        dv_s[...] = jnp.zeros_like(dv_s)

        @pl.loop(0, 4)
        def _(i):
            rows = aligned(i, 256)
            q, g = all_ref[rows, 0:128], g_s[rows]
            dq_t = None
            for head in range(2):
                q_head, g_head = only_head(q, head, 1), only_head(g, head, 1)
                probs = head_probs(all_ref[:, 128:256], q_head)
                g_probs = dot(all_ref[:, 256:384], g_head, ((1,), (1,)))
                dv_s[...] += dot(probs.astype(BF), g_head, ((1,), (0,)))
                inner = jnp.sum(probs * g_probs, axis=0, keepdims=True)
                g_scores = (probs * (g_probs - inner)).astype(BF)
                dk_s[...] += dot(g_scores, q_head, ((1,), (0,)))
                term = dot(only_head(k_t, head, 0), g_scores, ((1,), (0,)))
                dq_t = term if dq_t is None else dq_t + term
            dq_s[rows] = (dq_t.T * HD**-0.5).astype(BF)

        for i in range(4):
            rows = slice(i * 256, (i + 1) * 256)
            outs[i][:, 0:128] = dq_s[rows]
            outs[i][:, 128:256] = dk_s[rows].astype(BF)
            outs[i][:, 256:384] = dv_s[rows].astype(BF)

    return kernel(
        body, [((256, 384), BF)] * 4, index, qkv, *grads,
        scratch=[((1024, 128), BF)] * 2 + [((1024, 128), F32)] * 2, after=after, cost=36, name="attention_back",
    )


def by_token(refs, dst):
    width = refs[0].shape[-1]
    for l in range(2):
        for j in range(2):
            for r in range(4):
                dst[r * 128 + l * 64 : r * 128 + l * 64 + 64, j * width : (j + 1) * width] = refs[2 * l + j][
                    r * 64 : (r + 1) * 64
                ]


ROWS_OUT = [((128, 1024), F32)] + [((128, 1024), BF)] * 3


def put_rows(value, outs, cols):
    outs[0][:, cols] = value[0:128]
    for r in (1, 2, 3):
        outs[r][0:128, cols] = value[r * 128 : (r + 1) * 128].astype(BF)


def project_out(index, heads, proj):
    def body(idx, a, b, c, d, w_ref, att_ref, *outs):
        by_token((a, b, c, d), att_ref)

        @pl.loop(0, 4)
        def _(n):
            cols = aligned(n, 256)
            put_rows(dot(att_ref[...], w_ref[:, cols], ((1,), (0,))), outs, cols)

    return kernel(body, [((512, 256), BF)] + ROWS_OUT, index, *heads, proj, name="project_out")


def sum_rows(refs):
    return refs[0][...] + (refs[1][0:128].astype(F32) + refs[2][0:128].astype(F32) + refs[3][0:128].astype(F32))


def middle_rows(index, terms, latent, mod, after=()):
    def body(idx, a, b, c, d, x_ref, mod_ref, attn_ref, mid_ref, in_ref):
        mod = mod_ref[...]
        attn = sum_rows((a, b, c, d))
        middle = x_ref[0:128].astype(F32) + mod_rows(mod, 2) * attn
        normed, _ = normalize(middle)
        attn_ref[...] = attn
        mid_ref[...] = middle
        in_ref[...] = (normed * (1.0 + mod_rows(mod, 4)) + mod_rows(mod, 3)).astype(BF)

    outs = [((128, 1024), F32), ((128, 1024), F32), ((128, 1024), BF)]
    return kernel(body, outs, index, *terms, latent, mod, after=after, cost=35, name="middle_rows")


def grad_mlp(index, grad_out, mod, after=()):
    def body(idx, g_ref, mod_ref, out_ref):
        @pl.loop(0, 4)
        def _(r):
            rows = aligned(r, 128)
            out_ref[rows] = (mod_rows(mod_ref[...], 5) * g_ref[rows].astype(F32)).astype(BF)

    return kernel(body, [((512, 1024), BF)], index, grad_out, mod, after=after, cost=31, token=True, name="grad_mlp")


def grad_act(index, g_mlp, down):
    def body(idx, g_ref, w_ref, out_ref):
        @pl.loop(0, 4)
        def _(n):
            out_ref[:, aligned(n, 256)] = dot(g_ref[...], w_ref[aligned(n, 256)], ((1,), (1,)))

    return kernel(body, [((512, 1024), F32)], index, g_mlp, down, cost=33, name="grad_act")[0]


def feed_forward(index, blocks, g_act, up):
    def body(idx, a, b, c, d, g_ref, w_ref, x_ref, act_ref, gup_ref, *outs):
        for r, ref in enumerate((a, b, c, d)):
            x_ref[r * 128 : (r + 1) * 128] = ref[...]

        @pl.loop(0, 4)
        def _(n):
            cols = aligned(n, 256)
            act, slope = gelu_and_slope(dot(x_ref[...], w_ref[:, cols], ((1,), (0,))))
            act_ref[:, cols] = act.astype(BF)
            gup_ref[:, cols] = (g_ref[:, cols] * slope).astype(BF)

        @pl.loop(0, 4)
        def _(n):
            cols = aligned(n, 256)
            put_rows(dot(gup_ref[...], w_ref[cols], ((1,), (1,))), outs, cols)

    return kernel(
        body, [((512, 1024), BF)] * 3 + ROWS_OUT, index, *blocks, g_act, up, name="feed_forward"
    )


def mlp_rows(index, act, down, after=()):
    def body(idx, a_ref, w_ref, *outs):
        @pl.loop(0, 4)
        def _(n):
            cols = aligned(n, 256)
            put_rows(dot(a_ref[...], w_ref[:, cols], ((1,), (0,))), outs, cols)

    return kernel(body, ROWS_OUT, index, act, down, after=after, cost=33, token=True, name="mlp_rows")


def hidden_grads(index, rows, g_up, g_mlp, act):
    def body(idx, x_ref, gup_ref, gm_ref, act_ref, kept_ref, sent_ref):
        for n, (left, right) in enumerate(((x_ref, gup_ref), (gm_ref, act_ref))):
            for i in range(4):
                turned = left[:, i * 256 : (i + 1) * 256].T
                dst = sent_ref if i & 1 else kept_ref

                @pl.loop(0, 4)
                def _(m):
                    cols = aligned(m, 256)
                    dst[n, i >> 1, :, cols] = dot(turned, right[:, cols], ((1,), (0,))).astype(dst.dtype)

    return kernel(
        body, [((2, 2, 256, 1024), F32), ((2, 2, 256, 1024), BF)], index, rows, g_up, g_mlp, act, cost=33, space=pltpu.VMEM, token=True, name="hidden_grads"
    )


def out_rows(index, terms, middle, grad_out, mod, after):
    def body(idx, a, b, c, d, mid_ref, g_ref, mod_ref, out_ref, row_ref):
        mlp = sum_rows((a, b, c, d))
        out_ref[...] = (mid_ref[...] + mod_rows(mod_ref[...], 5) * mlp).astype(BF)
        sums = latent_sums(g_ref[0:128].astype(F32) * mlp)
        row_ref[...] = jnp.zeros_like(row_ref)
        for l in range(2):
            row_ref[l : l + 1] = sums[l]

    outs = [((128, 1024), BF), ((8, 1024), F32)]
    return kernel(body, outs, index, *terms, middle, grad_out, mod, after=after, cost=30, name="out_rows")


def middle_back(index, terms, middle, attn, grad_out, mod, after=()):
    def body(idx, a, b, c, d, mid_ref, attn_ref, g_ref, mod_ref, gmid_ref, gattn_ref, row_ref):
        mod = mod_ref[...]
        g_in = sum_rows((a, b, c, d))
        normed, inverse = normalize(mid_ref[...])
        g_mid = g_ref[0:128].astype(F32) + norm_back(g_in * (1.0 + mod_rows(mod, 4)), normed, inverse)
        gmid_ref[...] = g_mid
        gattn_ref[...] = (mod_rows(mod, 2) * g_mid).astype(BF)
        row_ref[...] = jnp.zeros_like(row_ref)
        for k, value in enumerate((g_mid * attn_ref[...], g_in, g_in * normed)):
            sums = latent_sums(value)
            for l in range(2):
                row_ref[3 * l + k : 3 * l + k + 1] = sums[l]

    outs = [((128, 1024), F32), ((128, 1024), BF), ((8, 1024), F32)]
    return kernel(body, outs, index, *terms, middle, attn, grad_out, mod, after=after, cost=35, name="middle_back")


def heads_back(index, blocks, proj, after=()):
    def body(idx, a, b, c, d, w_ref, g_ref, *outs):
        for r, ref in enumerate((a, b, c, d)):
            g_ref[r * 128 : (r + 1) * 128] = ref[...]
        for j in range(2):
            block = dot(g_ref[...], w_ref[j * 128 : (j + 1) * 128], ((1,), (1,))).astype(BF).reshape(4, 2, 64, 128)
            for l in range(2):
                outs[2 * l + j][...] = block[:, l].reshape(256, 128)

    outs = [((512, 1024), BF)] + [((256, 128), BF)] * 4
    return kernel(body, outs, index, *blocks, proj, after=after, name="heads_back")


def input_back(index, blocks, w_qkv, latent, stats, row_mlp, rows_mid, after):
    def body(idx, a, b, c, d, w_ref, x_ref, stat_ref, row5_ref, row234_ref, g_ref, *rest):
        outs, own_ref, gm = rest[:4], rest[4], rest[5]
        by_token((a, b, c, d), g_ref)
        gm[...] = jnp.zeros_like(gm)

        @pl.loop(0, 4)
        def _(n):
            cols = aligned(n, 256)
            value = dot(g_ref[...], w_ref[cols], ((1,), (1,)))
            put_rows(value, outs, cols)
            mean = jnp.concatenate([stat_ref[:, 0:128]] * 2, axis=1)
            inverse = jnp.concatenate([stat_ref[:, 128:256]] * 2, axis=1)
            scaled = value * ((x_ref[:, cols].astype(F32) - mean) * inverse)
            for l in range(2):
                for k, part in enumerate((value, scaled)):
                    total = part.reshape(4, 2, 64, 256)[:, l].reshape(256, 256)
                    gm[6 * l + k : 6 * l + k + 1, cols] = jnp.sum(total, axis=0, keepdims=True)

        for l in range(2):
            for k in range(3):
                gm[6 * l + 2 + k : 6 * l + 3 + k] = row234_ref[3 * l + k : 3 * l + k + 1]
            gm[6 * l + 5 : 6 * l + 6] = row5_ref[l : l + 1]
        for r in range(4):
            for x in range(2):
                block = gm[:, aligned(idx[COLS + 2 * r + x], 128)]
                flipped = jnp.concatenate([block[6:12], block[0:6], block[12:16]], axis=0)
                block = jnp.where(idx[Z_LAT] == 1, flipped, block)
                if r == 0:
                    own_ref[:, x * 128 : (x + 1) * 128] = block
                else:
                    high = block.astype(BF)
                    outs[r][128:144, x * 128 : (x + 1) * 128] = high
                    outs[r][128:144, 256 + x * 128 : 384 + x * 128] = (block - high.astype(F32)).astype(BF)
                    outs[r][128:144, 512 + x * 256 : 768 + x * 256] = jnp.zeros((16, 256), BF)

    return kernel(
        body,
        [((512, 768), BF), ((128, 1024), F32)] + [((144, 1024), BF)] * 3 + [((16, 256), F32)],
        index, *blocks, w_qkv, latent, stats, row_mlp, rows_mid,
        scratch=[((16, 1024), F32)], after=after, token=True, name="input_back",
    )


def attention_grads(index, rows, g_triple, g_attn, attended, after=()):
    def body(idx, x_ref, gt_ref, ga_ref, att_ref, kept_ref, sent_ref):
        for i in range(4):
            dst = sent_ref if i & 1 else kept_ref
            x_t = x_ref[:, i * 256 : (i + 1) * 256].T
            g_t = ga_ref[:, i * 256 : (i + 1) * 256].T
            for j in range(2):
                start = (j ^ idx[Z_HEAD]) * 512
                dst[i >> 1, :, pl.ds(pl.multiple_of(start, 512), 384)] = dot(
                    x_t, gt_ref[:, j * 384 : (j + 1) * 384], ((1,), (0,))
                ).astype(dst.dtype)
                dst[i >> 1, :, pl.ds(pl.multiple_of(start + 384, 128), 128)] = dot(
                    g_t, att_ref[:, j * 128 : (j + 1) * 128], ((1,), (0,))
                ).astype(dst.dtype)

    return kernel(
        body, [((2, 256, 1024), F32), ((2, 256, 1024), BF)], index, rows, g_triple, g_attn, attended, after=after, cost=33, token=True, name="attention_grads"
    )


def latent_back(index, terms, g_mod, g_mid, latent, mod, after=()):
    def body(idx, a, b, c, d, gm_ref, gmid_ref, x_ref, mod_ref, out_ref, sum_ref):
        normed, inverse = normalize(x_ref[0:128].astype(F32))
        g_in = sum_rows((a, b, c, d)) * (1.0 + mod_rows(mod_ref[...], 1))
        out_ref[...] = (gmid_ref[...] + norm_back(g_in, normed, inverse)).astype(BF)
        total = gm_ref[...]
        for ref in (b, c, d):
            total = total + (ref[128:144, 0:256].astype(F32) + ref[128:144, 256:512].astype(F32))
        sum_ref[...] = total

    return kernel(
        body, [((128, 1024), BF), ((16, 256), F32)], index, *terms, g_mod, g_mid, latent, mod, after=after, cost=35, token=True, name="latent_back"
    )


def mod_sum(index, near, far, after):
    def body(idx, a, b, own_ref, far_ref, sum_s):
        sum_s[...] = a[...] + b[...]
        own_ref[...] = sum_s[:, aligned(idx[X_LO], 128)]
        far_ref[...] = sum_s[:, aligned(1 - idx[X_LO], 128)]

    outs = [((16, 128), F32)] * 2
    return kernel(body, outs, index, near, far, scratch=[((16, 256), F32)], after=after, token=True, name="mod_sum")


def cond_terms(index, near, rows, after):
    def body(idx, near_ref, a, b, c, d, out_ref, g_s):
        g_s[...] = jnp.zeros_like(g_s)
        for x in range(2):
            for l in range(2):
                for k in range(6):
                    g_s[2 * x + l : 2 * x + l + 1, k * 128 : (k + 1) * 128] = near_ref[x, 6 * l + k : 6 * l + k + 1]
        value = g_s[...]
        value = jnp.where(idx[X_LO] == 1, jnp.concatenate([value[2:4], value[0:2], value[4:8]], axis=0), value)
        high = value.astype(BF)
        rest = value - high.astype(F32)
        middle = rest.astype(BF)
        low = (rest - middle.astype(F32)).astype(BF)
        parts = jnp.concatenate([high.astype(F32), middle.astype(F32), low.astype(F32)], axis=0).astype(BF)
        for i, ref in enumerate((a, b, c, d)):
            term = dot(parts, ref[...], ((1,), (1,)))
            out_ref[:, aligned(idx[FEAT + i], 256)] = term[0:8] + (term[8:16] + term[16:24])

    return kernel(
        body, [((8, 1024), F32)], index, near, *rows, scratch=[((8, 768), F32)], after=after, token=True, name="cond_terms"
    )


def ada_grads(index, near, far, other, conds, after):
    def body(idx, *refs):
        near, far, other, conds, out_ref, g_s, s_s = *refs[:3], refs[3:7], *refs[7:]
        for i, ref in enumerate(conds):
            rows = jax.nn.silu(ref[:, aligned(idx[FEAT], 256)].astype(F32)).astype(BF).astype(F32)
            flipped = jnp.concatenate([rows[2:4], rows[0:2]], axis=0)
            s_s[4 * i : 4 * i + 4] = jnp.where(idx[X_LO] == 1, flipped, rows)
        g_s[...] = jnp.zeros_like(g_s)
        for b in range(4):
            for c in range(2):
                block = other[b] if c else (near, far)[b >> 1][b & 1]
                for l in range(2):
                    row = (2 * (b >> 1) + c) * 4 + 2 * (b & 1) + l
                    for k in range(6):
                        g_s[row : row + 1, k * 128 : (k + 1) * 128] = block[6 * l + k : 6 * l + k + 1]
        silu = s_s[...].T
        for k in range(6):
            out_ref[:, k, :] = lax.dot_general(
                silu, g_s[:, k * 128 : (k + 1) * 128], (((1,), (0,)), ((), ())), precision=HIGHEST
            )

    return kernel(
        body, [((256, 6, 128), F32)], index, near, far, other, *conds,
        scratch=[((16, 768), F32), ((16, 256), F32)], after=after, token=True, name="ada_grads"
    )


def hidden_core(index, kept, got, after):
    count = kept.shape[0]

    def body(idx, kept_ref, got_ref, own_ref, out_ref):
        for n in range(count):
            for h in range(2):
                own_ref[n, h] = kept_ref[n, h, :, 0:512] + got_ref[n, h, :, 0:512].astype(F32)
                out_ref[n, h] = (kept_ref[n, h, :, 512:1024] + got_ref[n, h, :, 512:1024].astype(F32)).astype(BF)

    outs = [((count, 2, 256, 512), F32), ((count, 2, 256, 512), BF)]
    return kernel(body, outs, index, kept, got, after=after, cost=31, token=True, name="hidden_core")


def hidden_x_lo(index, own, got, after):
    count = own.shape[0]

    def body(idx, own_ref, got_ref, kept_ref, out_ref):
        for n in range(count):
            kept_ref[n] = own_ref[n, 0] + got_ref[n, 0].astype(F32)
            out_ref[n] = (own_ref[n, 1] + got_ref[n, 1].astype(F32)).astype(BF)

    outs = [((count, 256, 512), F32), ((count, 256, 512), BF)]
    return kernel(body, outs, index, own, got, after=after, cost=31, token=True, name="hidden_x_lo")


def pair_sum(index, own, got, after):
    def body(idx, own_ref, got_ref, out_ref):
        out_ref[...] = (own_ref[...].astype(F32) + got_ref[...].astype(F32)).astype(BF)

    return kernel(body, [(own.shape, BF)], index, own, got, after=after, cost=31, token=True, name="pair_sum")


def hidden_out(index, own, got, after):
    def body(idx, own_ref, got_ref, up_ref, down_ref):
        up_ref[...] = own_ref[0].astype(F32) + got_ref[0].astype(F32)
        down_ref[...] = (own_ref[1].astype(F32) + got_ref[1].astype(F32)).T

    outs = [((256, 512), F32), ((512, 256), F32)]
    return kernel(body, outs, index, own, got, after=after, cost=31, token=True, name="hidden_out")


def attention_out(index, own, got):
    def body(idx, a, b, qkv_ref, proj_ref):
        def total(cols):
            return a[0, :, cols].astype(F32) + b[0, :, cols].astype(F32)

        for j in range(3):
            qkv_ref[:, j, :] = total(slice(j * 128, (j + 1) * 128))
        proj_ref[...] = total(slice(384, 512)).T

    return kernel(body, [((256, 3, 128), F32), ((128, 256), F32)], index, own, got, name="attention_out")


def exchange_y(blocks):
    return [blocks[0]] + [swap(blocks[r], "tp", r) for r in (1, 2, 3)]


def gather_y(block):
    return [block] + [swap(block, "tp", r) for r in (1, 2, 3)]


def gather_tp(block):
    near = gather_y(block)
    far = swap(block, "tp", 4)
    return near + [far, swap(far, "tp", 1), swap(near[2], "tp", 4), swap(far, "tp", 3)]


def exchange_z(blocks):
    return [blocks[0]] + [swap(blocks[q], "ctx", q) for q in (1, 2, 3)]


def corner(array):
    return array[:16, :128]


def sum_four(terms):
    return (terms[0] + terms[1]) + (terms[2] + terms[3])


def shards(
    latent_in, condition, ada_weight, qkv_weight, proj_weight, up_matrix, down_matrix, out_grad
):
    s, z, t = lax.axis_index("shard"), lax.axis_index("ctx"), lax.axis_index("tp")
    x_lo, y, z_lat, z_head = t >> 2, t & 3, z >> 1, z & 1
    columns = [[((4 * x + (y ^ r)) >> 1 ^ s) * 2 + ((y ^ r) & 1) for x in range(2)] for r in range(4)]
    index = jnp.stack(
        [2 * x_lo + (l ^ z_lat) for l in range(2)]
        + [y ^ r for r in range(4)]
        + [s ^ i for i in range(4)]
        + [2 * (x_lo ^ x) + (l ^ z_lat) for x in range(2) for l in range(2)]
        + [z_head, x_lo, z_lat, t]
        + [c for pair in columns for c in pair]
    ).astype(jnp.int32)

    ada = ada_weight.reshape(256, 768)
    conds = [condition] + [swap(condition, "shard", i) for i in (1, 2, 3)]
    kept, sent = mod_terms(index, conds, ada)
    terms = mod_core(index, kept, swap(sent, "shard", 1))
    terms = [terms[0]] + [swap_x(terms[b], b) for b in (1, 2, 3)]
    packed = pack_first(index, qkv_weight, proj_weight, tuple(terms[1:]))
    first = [packed] + [swap_x(packed, b) for b in (1, 2, 3)]
    packed = pack_second(index, up_matrix, down_matrix, (corner(first[3]),))
    mod_x = mod_ring(index, terms)
    near = jnp.concatenate([mod_x, swap(mod_x, "tp", 1)])
    latent = arrange(index, latent_in)
    mod, done = mod_assemble(index, near, swap(near, "tp", 2), (latent,))
    first = stack_blocks(index, first, (done,))[0].reshape(4, 256, 512)

    input_a, w_qkv, stats, proj, *parts, done = project_in(index, latent, mod, first, swap(first, "shard", 1))
    parts = exchange_z(parts)
    grad_out = arrange(index, out_grad, (done,))
    g_mlp, g_done = grad_mlp(index, grad_out, mod, (done,))
    packed, done = stack_blocks(index, [packed, swap(packed, "tp", 4)], tuple(parts[1:]))
    ada_far = swap(ada, "shard", 2)
    ada_rows = [ada, swap(ada, "shard", 1), ada_far, swap(ada_far, "shard", 1)]
    up, down = assemble(index, lax.all_gather(packed, "shard", axis=0))
    g_act = grad_act(index, g_mlp, down)

    qkv, *heads = attention(index, parts, (g_done, done))
    heads = exchange_z(heads)
    attended, *terms = project_out(index, heads, proj)
    attn, middle, input_b = middle_rows(index, exchange_y(terms), latent, mod)
    rows_b, act, g_up, *terms = feed_forward(index, gather_y(input_b), g_act, up)
    ud_kept, ud_sent, done = hidden_grads(index, rows_b, g_up, g_mlp, act)
    g_mid, g_attn, rows_mid = middle_back(
        index, exchange_y(terms), middle, attn, grad_out, mod, (done, corner(ada_rows[1]), corner(ada_rows[3]))
    )
    *mlp_terms, done = mlp_rows(index, act, down, (g_attn,))
    ud, ud_sent, done = hidden_core(index, ud_kept, swap(ud_sent, "shard", 1), (done,))
    g_attn, *g_parts = heads_back(index, gather_y(g_attn), proj, (done,))
    g_parts = exchange_z(g_parts)

    g_blocks = attention_back(index, qkv, g_parts, ())
    out_block, row_mlp = out_rows(index, exchange_y(mlp_terms), middle, grad_out, mod, (g_blocks[0],))
    out_blocks = gather_tp(out_block)
    ud, ud_sent, done = hidden_x_lo(index, ud, swap(ud_sent, "tp", 4), (out_block,))
    g_blocks = exchange_z(g_blocks)
    g_triple, *rest, done = input_back(
        index, g_blocks, w_qkv, latent, stats, row_mlp, rows_mid, (done, *[corner(b) for b in out_blocks[1:4]])
    )
    ud, ud_done = pair_sum(index, ud, swap(ud_sent, "shard", 2), (done,))
    kept, sent, done = attention_grads(index, input_a, g_triple, g_attn, attended)
    own, g_mod, done = latent_back(index, exchange_y(rest[:4]), rest[4], g_mid, latent, mod, (done, ud_done))

    blocks = gather_tp(own)
    g_mod = g_mod + swap(g_mod, "ctx", 1)
    qp, qp_sent, done = hidden_core(index, kept[None], swap(sent[None], "shard", 1), (done,))
    mod_own, mod_far, done = mod_sum(index, g_mod, swap(g_mod, "ctx", 2), (done,))
    near = jnp.stack([mod_own, swap(mod_far, "tp", 4)])
    ud, done = pair_sum(index, ud, swap(ud, "ctx", 1), (done,))
    qp, qp_sent, done = hidden_x_lo(
        index, qp, swap(qp_sent, "tp", 4), (done, *[corner(b) for b in blocks[1:4]])
    )
    terms, done = cond_terms(index, near, ada_rows, (done,))
    qp, done = pair_sum(index, qp, swap(qp_sent, "shard", 2), (done,))
    far = swap(near, "shard", 2)
    terms = terms + swap(terms, "tp", 4)
    up_grad, down_grad, done = hidden_out(index, ud, swap(ud, "ctx", 2), (done,))
    ada_grad, done = ada_grads(index, near, far, swap(jnp.concatenate([near, far]), "shard", 1), conds, (done,))
    terms = terms + swap(terms, "tp", 1)
    qp, done = pair_sum(index, qp, swap(qp, "ctx", 1), (done,))
    latent_grad, done = restore(index, blocks, (done,))
    latent_out, done = restore(index, out_blocks, (done,))
    terms = terms + swap(terms, "tp", 2)
    qkv_grad, proj_grad = attention_out(index, qp, swap(qp, "ctx", 2))
    _, silu_pull = jax.vjp(jax.nn.silu, condition.astype(F32))
    condition_grad = silu_pull(terms[:4])[0]

    return (
        latent_out,
        latent_grad,
        condition_grad,
        ada_grad,
        qkv_grad,
        proj_grad,
        up_grad,
        down_grad,
    )


def solution(mesh):
    placed = (
        P("shard", "ctx", None),
        P("shard", None),
        P("shard", None, "tp"),
        P("shard", None, "tp"),
        P("tp", "shard"),
        P("shard", "tp"),
        P("tp", "shard"),
        P("shard", "ctx", None),
    )
    return jax.shard_map(
        shards,
        mesh=mesh,
        in_specs=placed,
        out_specs=(
            P("shard", "ctx", None),
            P("shard", "ctx", None),
            P("shard", None),
            P("shard", None, "tp"),
            P("shard", None, "tp"),
            P("tp", "shard"),
            P("shard", "tp"),
            P("tp", "shard"),
        ),
        check_vma=False,
    )
```

```python
import jax
import jax.numpy as jnp
from jax import lax
from jax.experimental import pallas as pl
from jax.experimental.pallas import tpu as pltpu
from jax.sharding import PartitionSpec as P

HD = 64
EPSILON = 1e-06
HIGHEST = lax.Precision.HIGHEST
BF = jnp.bfloat16
F32 = jnp.float32


def swap(value, axis, bits):
    size = {"shard": 4, "ctx": 4, "tp": 8}[axis]
    return lax.ppermute(value, axis, [(i, i ^ bits) for i in range(size)])


def swap_x(value, bits):
    if bits == 1:
        return swap(value, "tp", 4)
    if bits == 2:
        return swap(value, "shard", 2)
    return lax.ppermute(value, ("shard", "tp"), [(i, i ^ 20) for i in range(32)])


def pick(array, index, axis=0):
    return lax.dynamic_index_in_dim(array, index, axis, keepdims=False)


def dot(a, b, contract):
    return lax.dot_general(a, b, (contract, ((), ())), preferred_element_type=F32)


def normalize(rows):
    centred = rows - jnp.mean(rows, axis=-1, keepdims=True)
    inverse = lax.rsqrt(jnp.mean(centred * centred, axis=-1, keepdims=True) + EPSILON)
    return centred * inverse, inverse


def norm_back(grad, normed, inverse):
    first = jnp.mean(grad, axis=-1, keepdims=True)
    second = jnp.mean(grad * normed, axis=-1, keepdims=True)
    return inverse * (grad - first - normed * second)


GELU_A = 0.7978845608028654
GELU_B = 0.044715


def gelu_and_slope(v):
    square = v * v
    t = jnp.tanh(GELU_A * (v + GELU_B * v * square))
    half = 0.5 * (1.0 + t)
    return v * half, half + 0.5 * v * (1.0 - t * t) * (GELU_A * (1.0 + 3.0 * GELU_B * square))


LAT, TOK, FEAT, OUT_LAT, Z_HEAD, X_LO, Z_LAT, TP, COLS = 0, 2, 6, 10, 14, 15, 16, 17, 18


def kernel(body, outs, index, *arrays, scratch=(), after=(), vmem=16, cost=10, space=None, token=False, name):
    count = 1 + len(arrays)

    outs = list(outs)
    if token:
        outs.append(((8, 128), F32))

    def run(*refs):
        results = refs[count + len(after) :]
        if token:
            place = len(outs) - 1
            results[place][...] = jnp.zeros((8, 128), F32)
            results = results[:place] + results[place + 1 :]
        body(*refs[:count], *results)

    return pl.pallas_call(
        run,
        in_specs=[pl.BlockSpec(memory_space=pltpu.SMEM)]
        + [pl.BlockSpec()] * len(arrays)
        + [pl.BlockSpec(memory_space=pl.ANY)] * len(after),
        out_specs=[pl.BlockSpec(memory_space=space)] * len(outs),
        out_shape=[jax.ShapeDtypeStruct(shape, kind) for shape, kind in outs],
        scratch_shapes=[pltpu.VMEM(shape, kind) for shape, kind in scratch],
        compiler_params=pltpu.CompilerParams(vmem_limit_bytes=vmem * 2**20),
        cost_estimate=pl.CostEstimate(flops=2**cost, bytes_accessed=1024, transcendentals=0),
        name=name,
    )(index, *arrays, *after)


def aligned(start, step):
    return pl.ds(pl.multiple_of(start * step, step), step)


def arrange(index, array, after=()):
    def body(idx, src, *refs):
        dst = refs[-1]
        for r in range(4):
            for l in range(2):
                for i in range(4):
                    dst[r * 128 + l * 64 : r * 128 + l * 64 + 64, i * 256 : (i + 1) * 256] = src[
                        idx[LAT + l] - 2 * idx[X_LO], aligned(idx[TOK + r], 64), aligned(idx[FEAT + i], 256)
                    ]

    return pl.pallas_call(
        body,
        grid_spec=pltpu.PrefetchScalarGridSpec(
            num_scalar_prefetch=1,
            grid=(1,),
            in_specs=[pl.BlockSpec((2, 256, 1024), lambda n, idx: (idx[X_LO], 0, 0))]
            + [pl.BlockSpec(memory_space=pl.ANY)] * len(after),
            out_specs=pl.BlockSpec((512, 1024), lambda n, idx: (0, 0)),
        ),
        out_shape=jax.ShapeDtypeStruct((512, 1024), array.dtype),
        compiler_params=pltpu.CompilerParams(vmem_limit_bytes=16 * 2**20),
        cost_estimate=pl.CostEstimate(flops=2**31, bytes_accessed=1024, transcendentals=0),
        name="arrange",
    )(index, array, *after)


def restore(index, blocks, after=()):
    def body(idx, *refs):
        out = refs[-1]
        for x in range(2):
            for r in range(4):
                for l in range(2):
                    for i in range(4):
                        out[idx[OUT_LAT + 2 * x + l], aligned(idx[TOK + r], 64), aligned(idx[FEAT + i], 256)] = refs[
                            4 * x + r
                        ][l * 64 : l * 64 + 64, i * 256 : (i + 1) * 256].astype(F32)

    return kernel(body, [((4, 256, 1024), F32)], index, *blocks, after=after, cost=31, token=True, name="restore")


def pack_first(index, qkv, proj, after):
    def body(idx, q_ref, p_ref, out_ref):
        for j in range(3):
            out_ref[:, j * 128 : (j + 1) * 128] = q_ref[:, j]
        for h in range(2):
            out_ref[h * 128 : (h + 1) * 128, 384:512] = p_ref[:, h * 128 : (h + 1) * 128]

    return kernel(body, [((256, 512), BF)], index, qkv, proj, after=after, name="pack_first")[0]


def pack_second(index, up, down, after):
    def body(idx, u_ref, d_ref, out_ref):
        out_ref[0:256] = u_ref[:, 0:256]
        out_ref[256:512] = u_ref[:, 256:512]
        out_ref[512:1024] = d_ref[...]

    return kernel(body, [((1024, 256), BF)], index, up, down, after=after, cost=31, name="pack_second")[0]


def mod_terms(index, conds, ada):
    def body(idx, a, b, c, d, w_ref, kept_ref, sent_ref, s_s):
        for i, ref in enumerate((a, b, c, d)):
            s_s[4 * i : 4 * i + 4] = jax.nn.silu(ref[:, aligned(idx[FEAT], 256)].astype(F32))
        terms = dot(s_s[...].astype(BF), w_ref[...], ((1,), (0,)))
        for h in range(2):
            kept_ref[4 * h : 4 * h + 4] = terms[8 * h : 8 * h + 4]
            sent_ref[4 * h : 4 * h + 4] = terms[8 * h + 4 : 8 * h + 8]

    return kernel(
        body, [((8, 768), F32)] * 2, index, *conds, ada, scratch=[((16, 256), F32)], name="mod_terms"
    )


def mod_core(index, kept, got):
    def body(idx, a, b, *outs):
        value = a[...] + b[...]
        for n in range(4):
            rows = value[4 * (n >> 1) : 4 * (n >> 1) + 4]
            wanted = idx[X_LO] ^ (n & 1)
            outs[n][...] = jnp.where(wanted == 1, rows[2:4], rows[0:2])

    return kernel(body, [((2, 768), F32)] * 4, index, kept, got, name="mod_core")


def mod_ring(index, terms):
    def body(idx, a, b, c, d, out_ref):
        out_ref[0] = (a[...] + c[...]).astype(BF).astype(F32)
        out_ref[1] = (b[...] + d[...]).astype(BF).astype(F32)

    return kernel(body, [((2, 2, 768), F32)], index, *terms, name="mod_ring")[0]


def mod_assemble(index, near, far, after):
    def body(idx, near_ref, far_ref, out_ref, all_s):
        all_s[0:4] = near_ref[...]
        all_s[4:8] = far_ref[...]
        for p in range(8):
            column = 2 * idx[FEAT + (p >> 1)] + (p & 1)
            block = all_s[2 * ((column & 3) ^ idx[TOK]) + ((column >> 2) ^ idx[X_LO])]
            block = jnp.where(idx[Z_LAT] == 1, jnp.concatenate([block[1:2], block[0:1]], axis=0), block)
            for l in range(2):
                for k in range(6):
                    out_ref[6 * l + k : 6 * l + k + 1, p * 128 : (p + 1) * 128] = block[
                        l : l + 1, k * 128 : (k + 1) * 128
                    ]

    return kernel(
        body, [((12, 1024), F32)], index, near, far, scratch=[((8, 2, 768), F32)], after=after, token=True, name="mod_assemble"
    )


def stack_blocks(index, blocks, after):
    rows, width = blocks[0].shape

    def body(idx, *refs):
        for r, ref in enumerate(refs[:-1]):
            refs[-1][r * rows : (r + 1) * rows] = ref[...]

    outs = [((len(blocks) * rows, width), BF)]
    return kernel(body, outs, index, *blocks, after=after, cost=31, token=True, name="stack_blocks")


def mod_rows(mod, k, width=64):
    return jnp.concatenate(
        [jnp.broadcast_to(mod[6 * l + k : 6 * l + k + 1], (64, mod.shape[1])) for l in range(2)], axis=0
    )


def latent_sums(value):
    return [jnp.sum(value[l * 64 : (l + 1) * 64], axis=0, keepdims=True) for l in range(2)]


def project_in(index, latent, mod, mine, other, after=()):
    def body(idx, x_ref, mod_ref, *refs):
        blocks, (in_ref, w_ref, stat_ref, proj_ref), outs = refs[:2], refs[2:6], refs[6:]
        flip = idx[Z_HEAD] == 1
        for i in range(4):
            pair = [blocks[i & 1][2 * (i >> 1) + j] for j in range(2)]
            for j in range(2):
                block = jnp.where(flip, pair[1 - j], pair[j])
                w_ref[i * 256 : (i + 1) * 256, j * 384 : (j + 1) * 384] = block[:, 0:384]
                for h in range(2):
                    proj_ref[j * 128 : (j + 1) * 128, i * 256 + h * 128 : i * 256 + (h + 1) * 128] = block[
                        h * 128 : (h + 1) * 128, 384:512
                    ]

        @pl.loop(0, 4)
        def _(r):
            rows = aligned(r, 128)
            x = x_ref[rows].astype(F32)
            centred = x - jnp.mean(x, axis=-1, keepdims=True)
            inverse = lax.rsqrt(jnp.mean(centred * centred, axis=-1, keepdims=True) + EPSILON)
            normed = centred * inverse
            in_ref[rows] = (normed * (1.0 + mod_rows(mod_ref[...], 1)) + mod_rows(mod_ref[...], 0)).astype(BF)
            stat_ref[rows, 0:128] = jnp.broadcast_to(x[:, 0:1] - centred[:, 0:1], (128, 128))
            stat_ref[rows, 128:256] = jnp.broadcast_to(inverse, (128, 128))

        for j in range(2):
            block = dot(in_ref[...], w_ref[:, j * 384 : (j + 1) * 384], ((1,), (0,))).astype(BF)
            block = block.reshape(4, 2, 64, 384)
            for l in range(2):
                outs[2 * l + j][...] = block[:, l].reshape(256, 384)

    return kernel(
        body,
        [((512, 1024), BF), ((1024, 768), BF), ((512, 256), F32), ((256, 1024), BF)] + [((256, 384), BF)] * 4,
        index, latent, mod, mine, other, after=after, cost=33, token=True, name="project_in",
    )


def assemble(index, *blocks):
    def body(idx, a, b, c, d, up_ref, down_ref):
        for i, block in enumerate((a, b, c, d)):
            wide = slice(i * 256, (i + 1) * 256)
            for j in range(2):
                rows = j * 1024
                up_ref[wide, j * 512 : j * 512 + 256] = block[rows : rows + 256]
                up_ref[wide, j * 512 + 256 : (j + 1) * 512] = block[rows + 256 : rows + 512]
                down_ref[j * 512 : (j + 1) * 512, wide] = block[rows + 512 : rows + 1024]

    return kernel(body, [((1024, 1024), BF)] * 2, index, *blocks, cost=32, name="assemble")


def only_head(block, head, axis):
    lane = lax.broadcasted_iota(jnp.int32, block.shape, axis)
    return jnp.where((lane >= head * HD) & (lane < (head + 1) * HD), block, jnp.zeros_like(block))


def head_probs(k, q_head):
    scores = dot(k, q_head, ((1,), (1,)))
    powered = jnp.exp(scores - jnp.max(scores, axis=0, keepdims=True))
    return powered * (1.0 / jnp.sum(powered, axis=0, keepdims=True))


def attention(index, parts, after=()):
    def body(idx, *refs):
        ins, all_ref, outs, out_s = refs[:4], refs[4], refs[5:9], refs[9]
        for i, ref in enumerate(ins):
            rows = slice(i * 256, (i + 1) * 256)
            all_ref[rows, 0:128] = ref[:, 0:128] * jnp.asarray(HD**-0.5, BF)
            all_ref[rows, 128:384] = ref[:, 128:384]
        v_t = all_ref[:, 256:384].T

        @pl.loop(0, 4)
        def _(i):
            rows = aligned(i, 256)
            q = all_ref[rows, 0:128]
            total = None
            for head in range(2):
                probs = head_probs(all_ref[:, 128:256], only_head(q, head, 1)).astype(BF)
                term = dot(only_head(v_t, head, 0), probs, ((1,), (0,)))
                total = term if total is None else total + term
            out_s[rows] = total.T.astype(BF)

        for i in range(4):
            outs[i][...] = out_s[i * 256 : (i + 1) * 256]

    return kernel(
        body, [((1024, 384), BF)] + [((256, 128), BF)] * 4, index, *parts,
        scratch=[((1024, 128), BF)], after=after, cost=35, name="attention",
    )


def attention_back(index, qkv, grads, after):
    def body(idx, all_ref, *refs):
        gs, outs, (g_s, dq_s, dk_s, dv_s) = refs[:4], refs[4:8], refs[8:]
        for i in range(4):
            g_s[i * 256 : (i + 1) * 256] = gs[i][...]
        k_t = all_ref[:, 128:256].T
        dk_s[...] = jnp.zeros_like(dk_s)
        dv_s[...] = jnp.zeros_like(dv_s)

        @pl.loop(0, 4)
        def _(i):
            rows = aligned(i, 256)
            q, g = all_ref[rows, 0:128], g_s[rows]
            dq_t = None
            for head in range(2):
                q_head, g_head = only_head(q, head, 1), only_head(g, head, 1)
                probs = head_probs(all_ref[:, 128:256], q_head)
                g_probs = dot(all_ref[:, 256:384], g_head, ((1,), (1,)))
                dv_s[...] += dot(probs.astype(BF), g_head, ((1,), (0,)))
                inner = jnp.sum(probs * g_probs, axis=0, keepdims=True)
                g_scores = (probs * (g_probs - inner)).astype(BF)
                dk_s[...] += dot(g_scores, q_head, ((1,), (0,)))
                term = dot(only_head(k_t, head, 0), g_scores, ((1,), (0,)))
                dq_t = term if dq_t is None else dq_t + term
            dq_s[rows] = (dq_t.T * HD**-0.5).astype(BF)

        for i in range(4):
            rows = slice(i * 256, (i + 1) * 256)
            outs[i][:, 0:128] = dq_s[rows]
            outs[i][:, 128:256] = dk_s[rows].astype(BF)
            outs[i][:, 256:384] = dv_s[rows].astype(BF)

    return kernel(
        body, [((256, 384), BF)] * 4, index, qkv, *grads,
        scratch=[((1024, 128), BF)] * 2 + [((1024, 128), F32)] * 2, after=after, cost=36, name="attention_back",
    )


def by_token(refs, dst):
    width = refs[0].shape[-1]
    for l in range(2):
        for j in range(2):
            for r in range(4):
                dst[r * 128 + l * 64 : r * 128 + l * 64 + 64, j * width : (j + 1) * width] = refs[2 * l + j][
                    r * 64 : (r + 1) * 64
                ]


ROWS_OUT = [((128, 1024), F32)] + [((128, 1024), BF)] * 3


def put_rows(value, outs, cols):
    outs[0][:, cols] = value[0:128]
    for r in (1, 2, 3):
        outs[r][0:128, cols] = value[r * 128 : (r + 1) * 128].astype(BF)


def project_out(index, heads, proj):
    def body(idx, a, b, c, d, w_ref, att_ref, *outs):
        by_token((a, b, c, d), att_ref)

        @pl.loop(0, 4)
        def _(n):
            cols = aligned(n, 256)
            put_rows(dot(att_ref[...], w_ref[:, cols], ((1,), (0,))), outs, cols)

    return kernel(body, [((512, 256), BF)] + ROWS_OUT, index, *heads, proj, name="project_out")


def sum_rows(refs):
    return refs[0][...] + (refs[1][0:128].astype(F32) + refs[2][0:128].astype(F32) + refs[3][0:128].astype(F32))


def middle_rows(index, terms, latent, mod, after=()):
    def body(idx, a, b, c, d, x_ref, mod_ref, attn_ref, mid_ref, in_ref):
        mod = mod_ref[...]
        attn = sum_rows((a, b, c, d))
        middle = x_ref[0:128].astype(F32) + mod_rows(mod, 2) * attn
        normed, _ = normalize(middle)
        attn_ref[...] = attn
        mid_ref[...] = middle
        in_ref[...] = (normed * (1.0 + mod_rows(mod, 4)) + mod_rows(mod, 3)).astype(BF)

    outs = [((128, 1024), F32), ((128, 1024), F32), ((128, 1024), BF)]
    return kernel(body, outs, index, *terms, latent, mod, after=after, cost=35, name="middle_rows")


def grad_mlp(index, grad_out, mod, after=()):
    def body(idx, g_ref, mod_ref, out_ref):
        @pl.loop(0, 4)
        def _(r):
            rows = aligned(r, 128)
            out_ref[rows] = (mod_rows(mod_ref[...], 5) * g_ref[rows].astype(F32)).astype(BF)

    return kernel(body, [((512, 1024), BF)], index, grad_out, mod, after=after, cost=31, token=True, name="grad_mlp")


def grad_act(index, g_mlp, down):
    def body(idx, g_ref, w_ref, out_ref):
        @pl.loop(0, 4)
        def _(n):
            out_ref[:, aligned(n, 256)] = dot(g_ref[...], w_ref[aligned(n, 256)], ((1,), (1,)))

    return kernel(body, [((512, 1024), F32)], index, g_mlp, down, cost=33, name="grad_act")[0]


def feed_forward(index, blocks, g_act, up):
    def body(idx, a, b, c, d, g_ref, w_ref, x_ref, act_ref, gup_ref, *outs):
        for r, ref in enumerate((a, b, c, d)):
            x_ref[r * 128 : (r + 1) * 128] = ref[...]

        @pl.loop(0, 4)
        def _(n):
            cols = aligned(n, 256)
            act, slope = gelu_and_slope(dot(x_ref[...], w_ref[:, cols], ((1,), (0,))))
            act_ref[:, cols] = act.astype(BF)
            gup_ref[:, cols] = (g_ref[:, cols] * slope).astype(BF)

        @pl.loop(0, 4)
        def _(n):
            cols = aligned(n, 256)
            put_rows(dot(gup_ref[...], w_ref[cols], ((1,), (1,))), outs, cols)

    return kernel(
        body, [((512, 1024), BF)] * 3 + ROWS_OUT, index, *blocks, g_act, up, name="feed_forward"
    )


def mlp_rows(index, act, down, after=()):
    def body(idx, a_ref, w_ref, *outs):
        @pl.loop(0, 4)
        def _(n):
            cols = aligned(n, 256)
            put_rows(dot(a_ref[...], w_ref[:, cols], ((1,), (0,))), outs, cols)

    return kernel(body, ROWS_OUT, index, act, down, after=after, cost=33, token=True, name="mlp_rows")


def hidden_grads(index, rows, g_up, g_mlp, act):
    def body(idx, x_ref, gup_ref, gm_ref, act_ref, kept_ref, sent_ref):
        for n, (left, right) in enumerate(((x_ref, gup_ref), (gm_ref, act_ref))):
            for i in range(4):
                turned = left[:, i * 256 : (i + 1) * 256].T
                dst = sent_ref if i & 1 else kept_ref

                @pl.loop(0, 4)
                def _(m):
                    cols = aligned(m, 256)
                    dst[n, i >> 1, :, cols] = dot(turned, right[:, cols], ((1,), (0,))).astype(dst.dtype)

    return kernel(
        body, [((2, 2, 256, 1024), F32), ((2, 2, 256, 1024), BF)], index, rows, g_up, g_mlp, act, cost=33, space=pltpu.VMEM, token=True, name="hidden_grads"
    )


def out_rows(index, terms, middle, grad_out, mod, after):
    def body(idx, a, b, c, d, mid_ref, g_ref, mod_ref, out_ref, row_ref):
        mlp = sum_rows((a, b, c, d))
        out_ref[...] = (mid_ref[...] + mod_rows(mod_ref[...], 5) * mlp).astype(BF)
        sums = latent_sums(g_ref[0:128].astype(F32) * mlp)
        row_ref[...] = jnp.zeros_like(row_ref)
        for l in range(2):
            row_ref[l : l + 1] = sums[l]

    outs = [((128, 1024), BF), ((8, 1024), F32)]
    return kernel(body, outs, index, *terms, middle, grad_out, mod, after=after, cost=30, name="out_rows")


def middle_back(index, terms, middle, attn, grad_out, mod, after=()):
    def body(idx, a, b, c, d, mid_ref, attn_ref, g_ref, mod_ref, gmid_ref, gattn_ref, row_ref):
        mod = mod_ref[...]
        g_in = sum_rows((a, b, c, d))
        normed, inverse = normalize(mid_ref[...])
        g_mid = g_ref[0:128].astype(F32) + norm_back(g_in * (1.0 + mod_rows(mod, 4)), normed, inverse)
        gmid_ref[...] = g_mid
        gattn_ref[...] = (mod_rows(mod, 2) * g_mid).astype(BF)
        row_ref[...] = jnp.zeros_like(row_ref)
        for k, value in enumerate((g_mid * attn_ref[...], g_in, g_in * normed)):
            sums = latent_sums(value)
            for l in range(2):
                row_ref[3 * l + k : 3 * l + k + 1] = sums[l]

    outs = [((128, 1024), F32), ((128, 1024), BF), ((8, 1024), F32)]
    return kernel(body, outs, index, *terms, middle, attn, grad_out, mod, after=after, cost=35, name="middle_back")


def heads_back(index, blocks, proj, after=()):
    def body(idx, a, b, c, d, w_ref, g_ref, *outs):
        for r, ref in enumerate((a, b, c, d)):
            g_ref[r * 128 : (r + 1) * 128] = ref[...]
        for j in range(2):
            block = dot(g_ref[...], w_ref[j * 128 : (j + 1) * 128], ((1,), (1,))).astype(BF).reshape(4, 2, 64, 128)
            for l in range(2):
                outs[2 * l + j][...] = block[:, l].reshape(256, 128)

    outs = [((512, 1024), BF)] + [((256, 128), BF)] * 4
    return kernel(body, outs, index, *blocks, proj, after=after, name="heads_back")


def input_back(index, blocks, w_qkv, latent, stats, row_mlp, rows_mid, after):
    def body(idx, a, b, c, d, w_ref, x_ref, stat_ref, row5_ref, row234_ref, g_ref, *rest):
        outs, own_ref, gm = rest[:4], rest[4], rest[5]
        by_token((a, b, c, d), g_ref)
        gm[...] = jnp.zeros_like(gm)

        @pl.loop(0, 4)
        def _(n):
            cols = aligned(n, 256)
            value = dot(g_ref[...], w_ref[cols], ((1,), (1,)))
            put_rows(value, outs, cols)
            mean = jnp.concatenate([stat_ref[:, 0:128]] * 2, axis=1)
            inverse = jnp.concatenate([stat_ref[:, 128:256]] * 2, axis=1)
            scaled = value * ((x_ref[:, cols].astype(F32) - mean) * inverse)
            for l in range(2):
                for k, part in enumerate((value, scaled)):
                    total = part.reshape(4, 2, 64, 256)[:, l].reshape(256, 256)
                    gm[6 * l + k : 6 * l + k + 1, cols] = jnp.sum(total, axis=0, keepdims=True)

        for l in range(2):
            for k in range(3):
                gm[6 * l + 2 + k : 6 * l + 3 + k] = row234_ref[3 * l + k : 3 * l + k + 1]
            gm[6 * l + 5 : 6 * l + 6] = row5_ref[l : l + 1]
        for r in range(4):
            for x in range(2):
                block = gm[:, aligned(idx[COLS + 2 * r + x], 128)]
                flipped = jnp.concatenate([block[6:12], block[0:6], block[12:16]], axis=0)
                block = jnp.where(idx[Z_LAT] == 1, flipped, block)
                if r == 0:
                    own_ref[:, x * 128 : (x + 1) * 128] = block
                else:
                    high = block.astype(BF)
                    outs[r][128:144, x * 128 : (x + 1) * 128] = high
                    outs[r][128:144, 256 + x * 128 : 384 + x * 128] = (block - high.astype(F32)).astype(BF)
                    outs[r][128:144, 512 + x * 256 : 768 + x * 256] = jnp.zeros((16, 256), BF)

    return kernel(
        body,
        [((512, 768), BF), ((128, 1024), F32)] + [((144, 1024), BF)] * 3 + [((16, 256), F32)],
        index, *blocks, w_qkv, latent, stats, row_mlp, rows_mid,
        scratch=[((16, 1024), F32)], after=after, token=True, name="input_back",
    )


def attention_grads(index, rows, g_triple, g_attn, attended, after=()):
    def body(idx, x_ref, gt_ref, ga_ref, att_ref, kept_ref, sent_ref):
        for i in range(4):
            dst = sent_ref if i & 1 else kept_ref
            x_t = x_ref[:, i * 256 : (i + 1) * 256].T
            g_t = ga_ref[:, i * 256 : (i + 1) * 256].T
            for j in range(2):
                start = (j ^ idx[Z_HEAD]) * 512
                dst[i >> 1, :, pl.ds(pl.multiple_of(start, 512), 384)] = dot(
                    x_t, gt_ref[:, j * 384 : (j + 1) * 384], ((1,), (0,))
                ).astype(dst.dtype)
                dst[i >> 1, :, pl.ds(pl.multiple_of(start + 384, 128), 128)] = dot(
                    g_t, att_ref[:, j * 128 : (j + 1) * 128], ((1,), (0,))
                ).astype(dst.dtype)

    return kernel(
        body, [((2, 256, 1024), F32), ((2, 256, 1024), BF)], index, rows, g_triple, g_attn, attended, after=after, cost=33, token=True, name="attention_grads"
    )


def latent_back(index, terms, g_mod, g_mid, latent, mod, after=()):
    def body(idx, a, b, c, d, gm_ref, gmid_ref, x_ref, mod_ref, out_ref, sum_ref):
        normed, inverse = normalize(x_ref[0:128].astype(F32))
        g_in = sum_rows((a, b, c, d)) * (1.0 + mod_rows(mod_ref[...], 1))
        out_ref[...] = (gmid_ref[...] + norm_back(g_in, normed, inverse)).astype(BF)
        total = gm_ref[...]
        for ref in (b, c, d):
            total = total + (ref[128:144, 0:256].astype(F32) + ref[128:144, 256:512].astype(F32))
        sum_ref[...] = total

    return kernel(
        body, [((128, 1024), BF), ((16, 256), F32)], index, *terms, g_mod, g_mid, latent, mod, after=after, cost=35, token=True, name="latent_back"
    )


def mod_sum(index, near, far, after):
    def body(idx, a, b, own_ref, far_ref, sum_s):
        sum_s[...] = a[...] + b[...]
        own_ref[...] = sum_s[:, aligned(idx[X_LO], 128)]
        far_ref[...] = sum_s[:, aligned(1 - idx[X_LO], 128)]

    outs = [((16, 128), F32)] * 2
    return kernel(body, outs, index, near, far, scratch=[((16, 256), F32)], after=after, token=True, name="mod_sum")


def cond_terms(index, near, rows, after):
    def body(idx, near_ref, a, b, c, d, out_ref, g_s):
        g_s[...] = jnp.zeros_like(g_s)
        for x in range(2):
            for l in range(2):
                for k in range(6):
                    g_s[2 * x + l : 2 * x + l + 1, k * 128 : (k + 1) * 128] = near_ref[x, 6 * l + k : 6 * l + k + 1]
        value = g_s[...]
        value = jnp.where(idx[X_LO] == 1, jnp.concatenate([value[2:4], value[0:2], value[4:8]], axis=0), value)
        high = value.astype(BF)
        rest = value - high.astype(F32)
        middle = rest.astype(BF)
        low = (rest - middle.astype(F32)).astype(BF)
        parts = jnp.concatenate([high.astype(F32), middle.astype(F32), low.astype(F32)], axis=0).astype(BF)
        for i, ref in enumerate((a, b, c, d)):
            term = dot(parts, ref[...], ((1,), (1,)))
            out_ref[:, aligned(idx[FEAT + i], 256)] = term[0:8] + (term[8:16] + term[16:24])

    return kernel(
        body, [((8, 1024), F32)], index, near, *rows, scratch=[((8, 768), F32)], after=after, token=True, name="cond_terms"
    )


def ada_grads(index, near, far, other, conds, after):
    def body(idx, *refs):
        near, far, other, conds, out_ref, g_s, s_s = *refs[:3], refs[3:7], *refs[7:]
        for i, ref in enumerate(conds):
            rows = jax.nn.silu(ref[:, aligned(idx[FEAT], 256)].astype(F32)).astype(BF).astype(F32)
            flipped = jnp.concatenate([rows[2:4], rows[0:2]], axis=0)
            s_s[4 * i : 4 * i + 4] = jnp.where(idx[X_LO] == 1, flipped, rows)
        g_s[...] = jnp.zeros_like(g_s)
        for b in range(4):
            for c in range(2):
                block = other[b] if c else (near, far)[b >> 1][b & 1]
                for l in range(2):
                    row = (2 * (b >> 1) + c) * 4 + 2 * (b & 1) + l
                    for k in range(6):
                        g_s[row : row + 1, k * 128 : (k + 1) * 128] = block[6 * l + k : 6 * l + k + 1]
        silu = s_s[...].T
        for k in range(6):
            out_ref[:, k, :] = lax.dot_general(
                silu, g_s[:, k * 128 : (k + 1) * 128], (((1,), (0,)), ((), ())), precision=HIGHEST
            )

    return kernel(
        body, [((256, 6, 128), F32)], index, near, far, other, *conds,
        scratch=[((16, 768), F32), ((16, 256), F32)], after=after, token=True, name="ada_grads"
    )


def hidden_core(index, kept, got, after):
    count = kept.shape[0]

    def body(idx, kept_ref, got_ref, own_ref, out_ref):
        for n in range(count):
            for h in range(2):
                own_ref[n, h] = kept_ref[n, h, :, 0:512] + got_ref[n, h, :, 0:512].astype(F32)
                out_ref[n, h] = (kept_ref[n, h, :, 512:1024] + got_ref[n, h, :, 512:1024].astype(F32)).astype(BF)

    outs = [((count, 2, 256, 512), F32), ((count, 2, 256, 512), BF)]
    return kernel(body, outs, index, kept, got, after=after, cost=31, token=True, name="hidden_core")


def hidden_x_lo(index, own, got, after):
    count = own.shape[0]

    def body(idx, own_ref, got_ref, kept_ref, out_ref):
        for n in range(count):
            kept_ref[n] = own_ref[n, 0] + got_ref[n, 0].astype(F32)
            out_ref[n] = (own_ref[n, 1] + got_ref[n, 1].astype(F32)).astype(BF)

    outs = [((count, 256, 512), F32), ((count, 256, 512), BF)]
    return kernel(body, outs, index, own, got, after=after, cost=31, token=True, name="hidden_x_lo")


def pair_sum(index, own, got, after):
    def body(idx, own_ref, got_ref, out_ref):
        out_ref[...] = (own_ref[...].astype(F32) + got_ref[...].astype(F32)).astype(BF)

    return kernel(body, [(own.shape, BF)], index, own, got, after=after, cost=31, token=True, name="pair_sum")


def hidden_out(index, own, got, after):
    def body(idx, own_ref, got_ref, up_ref, down_ref):
        up_ref[...] = own_ref[0].astype(F32) + got_ref[0].astype(F32)
        down_ref[...] = (own_ref[1].astype(F32) + got_ref[1].astype(F32)).T

    outs = [((256, 512), F32), ((512, 256), F32)]
    return kernel(body, outs, index, own, got, after=after, cost=31, token=True, name="hidden_out")


def attention_out(index, own, got):
    def body(idx, a, b, qkv_ref, proj_ref):
        def total(cols):
            return a[0, :, cols].astype(F32) + b[0, :, cols].astype(F32)

        for j in range(3):
            qkv_ref[:, j, :] = total(slice(j * 128, (j + 1) * 128))
        proj_ref[...] = total(slice(384, 512)).T

    return kernel(body, [((256, 3, 128), F32), ((128, 256), F32)], index, own, got, name="attention_out")


def exchange_y(blocks):
    return [blocks[0]] + [swap(blocks[r], "tp", r) for r in (1, 2, 3)]


def gather_y(block):
    return [block] + [swap(block, "tp", r) for r in (1, 2, 3)]


def gather_tp(block):
    near = gather_y(block)
    far = swap(block, "tp", 4)
    return near + [far, swap(far, "tp", 1), swap(near[2], "tp", 4), swap(far, "tp", 3)]


def exchange_z(blocks):
    return [blocks[0]] + [swap(blocks[q], "ctx", q) for q in (1, 2, 3)]


def corner(array):
    return array[:16, :128]


def sum_four(terms):
    return (terms[0] + terms[1]) + (terms[2] + terms[3])


def shards(
    latent_in, condition, ada_weight, qkv_weight, proj_weight, up_matrix, down_matrix, out_grad
):
    s, z, t = lax.axis_index("shard"), lax.axis_index("ctx"), lax.axis_index("tp")
    x_lo, y, z_lat, z_head = t >> 2, t & 3, z >> 1, z & 1
    columns = [[((4 * x + (y ^ r)) >> 1 ^ s) * 2 + ((y ^ r) & 1) for x in range(2)] for r in range(4)]
    index = jnp.stack(
        [2 * x_lo + (l ^ z_lat) for l in range(2)]
        + [y ^ r for r in range(4)]
        + [s ^ i for i in range(4)]
        + [2 * (x_lo ^ x) + (l ^ z_lat) for x in range(2) for l in range(2)]
        + [z_head, x_lo, z_lat, t]
        + [c for pair in columns for c in pair]
    ).astype(jnp.int32)

    ada = ada_weight.reshape(256, 768)
    conds = [condition] + [swap(condition, "shard", i) for i in (1, 2, 3)]
    kept, sent = mod_terms(index, conds, ada)
    terms = mod_core(index, kept, swap(sent, "shard", 1))
    terms = [terms[0]] + [swap_x(terms[b], b) for b in (1, 2, 3)]
    packed = pack_first(index, qkv_weight, proj_weight, tuple(terms[1:]))
    first = [packed] + [swap_x(packed, b) for b in (1, 2, 3)]
    packed = pack_second(index, up_matrix, down_matrix, (corner(first[3]),))
    mod_x = mod_ring(index, terms)
    near = jnp.concatenate([mod_x, swap(mod_x, "tp", 1)])
    latent = arrange(index, latent_in)
    mod, done = mod_assemble(index, near, swap(near, "tp", 2), (latent,))
    first = stack_blocks(index, first, (done,))[0].reshape(4, 256, 512)

    input_a, w_qkv, stats, proj, *parts, done = project_in(index, latent, mod, first, swap(first, "shard", 1))
    parts = exchange_z(parts)
    grad_out = arrange(index, out_grad, (done,))
    g_mlp, g_done = grad_mlp(index, grad_out, mod, (done,))
    packed, done = stack_blocks(index, [packed, swap(packed, "tp", 4)], tuple(corner(b) for b in parts[1:]))
    ada_far = swap(ada, "shard", 2)
    ada_rows = [ada, swap(ada, "shard", 1), ada_far, swap(ada_far, "shard", 1)]
    far = swap(packed, "shard", 2)
    up, down = assemble(index, packed, swap(packed, "shard", 1), far, swap(far, "shard", 1))
    g_act = grad_act(index, g_mlp, down)

    qkv, *heads = attention(index, parts, (g_done, done))
    heads = exchange_z(heads)
    attended, *terms = project_out(index, heads, proj)
    attn, middle, input_b = middle_rows(index, exchange_y(terms), latent, mod, (corner(far),))
    rows_b, act, g_up, *terms = feed_forward(index, gather_y(input_b), g_act, up)
    ud_kept, ud_sent, done = hidden_grads(index, rows_b, g_up, g_mlp, act)
    g_mid, g_attn, rows_mid = middle_back(
        index, exchange_y(terms), middle, attn, grad_out, mod, (done, corner(ada_rows[1]), corner(ada_rows[3]))
    )
    *mlp_terms, done = mlp_rows(index, act, down, (g_attn,))
    ud, ud_sent, done = hidden_core(index, ud_kept, swap(ud_sent, "shard", 1), (done,))
    g_attn, *g_parts = heads_back(index, gather_y(g_attn), proj, (done,))
    g_parts = exchange_z(g_parts)

    g_blocks = attention_back(index, qkv, g_parts, ())
    out_block, row_mlp = out_rows(index, exchange_y(mlp_terms), middle, grad_out, mod, (g_blocks[0],))
    out_blocks = gather_tp(out_block)
    ud, ud_sent, done = hidden_x_lo(index, ud, swap(ud_sent, "tp", 4), (out_block,))
    g_blocks = exchange_z(g_blocks)
    g_triple, *rest, done = input_back(
        index, g_blocks, w_qkv, latent, stats, row_mlp, rows_mid, (done, *[corner(b) for b in out_blocks[1:3]])
    )
    ud, ud_done = pair_sum(index, ud, swap(ud_sent, "shard", 2), (done,))
    kept, sent, done = attention_grads(index, input_a, g_triple, g_attn, attended)
    own, g_mod, done = latent_back(index, exchange_y(rest[:4]), rest[4], g_mid, latent, mod, (done, ud_done))

    blocks = gather_tp(own)
    g_mod = g_mod + swap(g_mod, "ctx", 1)
    qp, qp_sent, done = hidden_core(index, kept[None], swap(sent[None], "shard", 1), (done,))
    mod_own, mod_far, done = mod_sum(index, g_mod, swap(g_mod, "ctx", 2), (done,))
    near = jnp.stack([mod_own, swap(mod_far, "tp", 4)])
    ud, done = pair_sum(index, ud, swap(ud, "ctx", 1), (done,))
    qp, qp_sent, done = hidden_x_lo(
        index, qp, swap(qp_sent, "tp", 4), (done, *[corner(b) for b in blocks[1:4]])
    )
    terms, done = cond_terms(index, near, ada_rows, (done,))
    qp, done = pair_sum(index, qp, swap(qp_sent, "shard", 2), (done,))
    far = swap(near, "shard", 2)
    terms = terms + swap(terms, "tp", 4)
    up_grad, down_grad, done = hidden_out(index, ud, swap(ud, "ctx", 2), (done,))
    ada_grad, done = ada_grads(index, near, far, swap(jnp.concatenate([near, far]), "shard", 1), conds, (done,))
    terms = terms + swap(terms, "tp", 1)
    qp, done = pair_sum(index, qp, swap(qp, "ctx", 1), (done,))
    latent_grad, done = restore(index, blocks, (done,))
    latent_out, done = restore(index, out_blocks, (done,))
    terms = terms + swap(terms, "tp", 2)
    qkv_grad, proj_grad = attention_out(index, qp, swap(qp, "ctx", 2))
    _, silu_pull = jax.vjp(jax.nn.silu, condition.astype(F32))
    condition_grad = silu_pull(terms[:4])[0]

    return (
        latent_out,
        latent_grad,
        condition_grad,
        ada_grad,
        qkv_grad,
        proj_grad,
        up_grad,
        down_grad,
    )


def solution(mesh):
    placed = (
        P("shard", "ctx", None),
        P("shard", None),
        P("shard", None, "tp"),
        P("shard", None, "tp"),
        P("tp", "shard"),
        P("shard", "tp"),
        P("tp", "shard"),
        P("shard", "ctx", None),
    )
    return jax.shard_map(
        shards,
        mesh=mesh,
        in_specs=placed,
        out_specs=(
            P("shard", "ctx", None),
            P("shard", "ctx", None),
            P("shard", None),
            P("shard", None, "tp"),
            P("shard", None, "tp"),
            P("tp", "shard"),
            P("shard", "tp"),
            P("tp", "shard"),
        ),
        check_vma=False,
    )
```

```python
import jax
import jax.numpy as jnp
from jax import lax
from jax.experimental import pallas as pl
from jax.experimental.pallas import tpu as pltpu
from jax.sharding import PartitionSpec as P

HD = 64
EPSILON = 1e-06
HIGHEST = lax.Precision.HIGHEST
BF = jnp.bfloat16
F32 = jnp.float32


def swap(value, axis, bits):
    size = {"shard": 4, "ctx": 4, "tp": 8}[axis]
    return lax.ppermute(value, axis, [(i, i ^ bits) for i in range(size)])


def swap_x(value, bits):
    if bits == 1:
        return swap(value, "tp", 4)
    if bits == 2:
        return swap(value, "shard", 2)
    return lax.ppermute(value, ("shard", "tp"), [(i, i ^ 20) for i in range(32)])


def pick(array, index, axis=0):
    return lax.dynamic_index_in_dim(array, index, axis, keepdims=False)


def dot(a, b, contract):
    return lax.dot_general(a, b, (contract, ((), ())), preferred_element_type=F32)


def normalize(rows):
    centred = rows - jnp.mean(rows, axis=-1, keepdims=True)
    inverse = lax.rsqrt(jnp.mean(centred * centred, axis=-1, keepdims=True) + EPSILON)
    return centred * inverse, inverse


def norm_back(grad, normed, inverse):
    first = jnp.mean(grad, axis=-1, keepdims=True)
    second = jnp.mean(grad * normed, axis=-1, keepdims=True)
    return inverse * (grad - first - normed * second)


GELU_A = 0.7978845608028654
GELU_B = 0.044715


def gelu_and_slope(v):
    square = v * v
    t = jnp.tanh(GELU_A * (v + GELU_B * v * square))
    half = 0.5 * (1.0 + t)
    return v * half, half + 0.5 * v * (1.0 - t * t) * (GELU_A * (1.0 + 3.0 * GELU_B * square))


LAT, TOK, FEAT, OUT_LAT, Z_HEAD, X_LO, Z_LAT, TP, COLS = 0, 2, 6, 10, 14, 15, 16, 17, 18


def kernel(body, outs, index, *arrays, scratch=(), after=(), vmem=16, cost=10, space=None, token=False, name):
    count = 1 + len(arrays)

    outs = list(outs)
    if token:
        outs.append(((8, 128), F32))

    def run(*refs):
        results = refs[count + len(after) :]
        if token:
            place = len(outs) - 1
            results[place][...] = jnp.zeros((8, 128), F32)
            results = results[:place] + results[place + 1 :]
        body(*refs[:count], *results)

    return pl.pallas_call(
        run,
        in_specs=[pl.BlockSpec(memory_space=pltpu.SMEM)]
        + [pl.BlockSpec()] * len(arrays)
        + [pl.BlockSpec(memory_space=pl.ANY)] * len(after),
        out_specs=[pl.BlockSpec(memory_space=space)] * len(outs),
        out_shape=[jax.ShapeDtypeStruct(shape, kind) for shape, kind in outs],
        scratch_shapes=[pltpu.VMEM(shape, kind) for shape, kind in scratch],
        compiler_params=pltpu.CompilerParams(vmem_limit_bytes=vmem * 2**20),
        cost_estimate=pl.CostEstimate(flops=2**cost, bytes_accessed=1024, transcendentals=0),
        name=name,
    )(index, *arrays, *after)


def aligned(start, step):
    return pl.ds(pl.multiple_of(start * step, step), step)


def arrange(index, array, after=()):
    def body(idx, src, *refs):
        dst = refs[-1]
        for r in range(4):
            for l in range(2):
                for i in range(4):
                    dst[r * 128 + l * 64 : r * 128 + l * 64 + 64, i * 256 : (i + 1) * 256] = src[
                        idx[LAT + l] - 2 * idx[X_LO], aligned(idx[TOK + r], 64), aligned(idx[FEAT + i], 256)
                    ]

    return pl.pallas_call(
        body,
        grid_spec=pltpu.PrefetchScalarGridSpec(
            num_scalar_prefetch=1,
            grid=(1,),
            in_specs=[pl.BlockSpec((2, 256, 1024), lambda n, idx: (idx[X_LO], 0, 0))]
            + [pl.BlockSpec(memory_space=pl.ANY)] * len(after),
            out_specs=pl.BlockSpec((512, 1024), lambda n, idx: (0, 0)),
        ),
        out_shape=jax.ShapeDtypeStruct((512, 1024), array.dtype),
        compiler_params=pltpu.CompilerParams(vmem_limit_bytes=16 * 2**20),
        cost_estimate=pl.CostEstimate(flops=2**31, bytes_accessed=1024, transcendentals=0),
        name="arrange",
    )(index, array, *after)


def restore(index, blocks, after=()):
    def body(idx, *refs):
        out = refs[-1]
        for x in range(2):
            for r in range(4):
                for l in range(2):
                    for i in range(4):
                        out[idx[OUT_LAT + 2 * x + l], aligned(idx[TOK + r], 64), aligned(idx[FEAT + i], 256)] = refs[
                            4 * x + r
                        ][l * 64 : l * 64 + 64, i * 256 : (i + 1) * 256].astype(F32)

    return kernel(body, [((4, 256, 1024), F32)], index, *blocks, after=after, cost=31, token=True, name="restore")


def pack_first(index, qkv, proj, after):
    def body(idx, q_ref, p_ref, out_ref):
        for j in range(3):
            out_ref[:, j * 128 : (j + 1) * 128] = q_ref[:, j]
        for h in range(2):
            out_ref[h * 128 : (h + 1) * 128, 384:512] = p_ref[:, h * 128 : (h + 1) * 128]

    return kernel(body, [((256, 512), BF)], index, qkv, proj, after=after, name="pack_first")[0]


def pack_second(index, up, down, after):
    def body(idx, u_ref, d_ref, out_ref):
        out_ref[0:256] = u_ref[:, 0:256]
        out_ref[256:512] = u_ref[:, 256:512]
        out_ref[512:1024] = d_ref[...]

    return kernel(body, [((1024, 256), BF)], index, up, down, after=after, cost=31, name="pack_second")[0]


def mod_terms(index, conds, ada):
    def body(idx, a, b, c, d, w_ref, kept_ref, sent_ref, s_s):
        for i, ref in enumerate((a, b, c, d)):
            s_s[4 * i : 4 * i + 4] = jax.nn.silu(ref[:, aligned(idx[FEAT], 256)].astype(F32))
        terms = dot(s_s[...].astype(BF), w_ref[...], ((1,), (0,)))
        for h in range(2):
            kept_ref[4 * h : 4 * h + 4] = terms[8 * h : 8 * h + 4]
            sent_ref[4 * h : 4 * h + 4] = terms[8 * h + 4 : 8 * h + 8]

    return kernel(
        body, [((8, 768), F32)] * 2, index, *conds, ada, scratch=[((16, 256), F32)], name="mod_terms"
    )


def mod_core(index, kept, got):
    def body(idx, a, b, *outs):
        value = a[...] + b[...]
        for n in range(4):
            rows = value[4 * (n >> 1) : 4 * (n >> 1) + 4]
            wanted = idx[X_LO] ^ (n & 1)
            outs[n][...] = jnp.where(wanted == 1, rows[2:4], rows[0:2])

    return kernel(body, [((2, 768), F32)] * 4, index, kept, got, name="mod_core")


def mod_ring(index, terms):
    def body(idx, a, b, c, d, out_ref):
        out_ref[0] = (a[...] + c[...]).astype(BF).astype(F32)
        out_ref[1] = (b[...] + d[...]).astype(BF).astype(F32)

    return kernel(body, [((2, 2, 768), F32)], index, *terms, name="mod_ring")[0]


def mod_assemble(index, near, far, after):
    def body(idx, near_ref, far_ref, out_ref, all_s):
        all_s[0:4] = near_ref[...]
        all_s[4:8] = far_ref[...]
        for p in range(8):
            column = 2 * idx[FEAT + (p >> 1)] + (p & 1)
            block = all_s[2 * ((column & 3) ^ idx[TOK]) + ((column >> 2) ^ idx[X_LO])]
            block = jnp.where(idx[Z_LAT] == 1, jnp.concatenate([block[1:2], block[0:1]], axis=0), block)
            for l in range(2):
                for k in range(6):
                    out_ref[6 * l + k : 6 * l + k + 1, p * 128 : (p + 1) * 128] = block[
                        l : l + 1, k * 128 : (k + 1) * 128
                    ]

    return kernel(
        body, [((12, 1024), F32)], index, near, far, scratch=[((8, 2, 768), F32)], after=after, token=True, name="mod_assemble"
    )


def stack_blocks(index, blocks, after):
    rows, width = blocks[0].shape

    def body(idx, *refs):
        for r, ref in enumerate(refs[:-1]):
            refs[-1][r * rows : (r + 1) * rows] = ref[...]

    outs = [((len(blocks) * rows, width), BF)]
    return kernel(body, outs, index, *blocks, after=after, cost=31, token=True, name="stack_blocks")


def mod_rows(mod, k, width=64):
    return jnp.concatenate(
        [jnp.broadcast_to(mod[6 * l + k : 6 * l + k + 1], (64, mod.shape[1])) for l in range(2)], axis=0
    )


def latent_sums(value):
    return [jnp.sum(value[l * 64 : (l + 1) * 64], axis=0, keepdims=True) for l in range(2)]


def project_in(index, latent, mod, mine, other, after=()):
    def body(idx, x_ref, mod_ref, *refs):
        blocks, (in_ref, w_ref, stat_ref, proj_ref), outs = refs[:2], refs[2:6], refs[6:]
        flip = idx[Z_HEAD] == 1
        for i in range(4):
            pair = [blocks[i & 1][2 * (i >> 1) + j] for j in range(2)]
            for j in range(2):
                block = jnp.where(flip, pair[1 - j], pair[j])
                w_ref[i * 256 : (i + 1) * 256, j * 384 : (j + 1) * 384] = block[:, 0:384]
                for h in range(2):
                    proj_ref[j * 128 : (j + 1) * 128, i * 256 + h * 128 : i * 256 + (h + 1) * 128] = block[
                        h * 128 : (h + 1) * 128, 384:512
                    ]

        @pl.loop(0, 4)
        def _(r):
            rows = aligned(r, 128)
            x = x_ref[rows].astype(F32)
            centred = x - jnp.mean(x, axis=-1, keepdims=True)
            inverse = lax.rsqrt(jnp.mean(centred * centred, axis=-1, keepdims=True) + EPSILON)
            normed = centred * inverse
            in_ref[rows] = (normed * (1.0 + mod_rows(mod_ref[...], 1)) + mod_rows(mod_ref[...], 0)).astype(BF)
            stat_ref[rows, 0:128] = jnp.broadcast_to(x[:, 0:1] - centred[:, 0:1], (128, 128))
            stat_ref[rows, 128:256] = jnp.broadcast_to(inverse, (128, 128))

        for j in range(2):
            block = dot(in_ref[...], w_ref[:, j * 384 : (j + 1) * 384], ((1,), (0,))).astype(BF)
            block = block.reshape(4, 2, 64, 384)
            for l in range(2):
                outs[2 * l + j][...] = block[:, l].reshape(256, 384)

    return kernel(
        body,
        [((512, 1024), BF), ((1024, 768), BF), ((512, 256), F32), ((256, 1024), BF)] + [((256, 384), BF)] * 4,
        index, latent, mod, mine, other, after=after, cost=33, token=True, name="project_in",
    )


def assemble(index, *blocks):
    def body(idx, a, b, c, d, up_ref, down_ref):
        for i, block in enumerate((a, b, c, d)):
            wide = slice(i * 256, (i + 1) * 256)
            for j in range(2):
                rows = j * 1024
                up_ref[wide, j * 512 : j * 512 + 256] = block[rows : rows + 256]
                up_ref[wide, j * 512 + 256 : (j + 1) * 512] = block[rows + 256 : rows + 512]
                down_ref[j * 512 : (j + 1) * 512, wide] = block[rows + 512 : rows + 1024]

    return kernel(body, [((1024, 1024), BF)] * 2, index, *blocks, cost=32, name="assemble")


def only_head(block, head, axis):
    lane = lax.broadcasted_iota(jnp.int32, block.shape, axis)
    return jnp.where((lane >= head * HD) & (lane < (head + 1) * HD), block, jnp.zeros_like(block))


def head_probs(k, q_head):
    scores = dot(k, q_head, ((1,), (1,)))
    powered = jnp.exp(scores - jnp.max(scores, axis=0, keepdims=True))
    return powered * (1.0 / jnp.sum(powered, axis=0, keepdims=True))


def attention(index, parts, after=()):
    def body(idx, *refs):
        ins, all_ref, outs, out_s = refs[:4], refs[4], refs[5:9], refs[9]
        for i, ref in enumerate(ins):
            rows = slice(i * 256, (i + 1) * 256)
            all_ref[rows, 0:128] = ref[:, 0:128] * jnp.asarray(HD**-0.5, BF)
            all_ref[rows, 128:384] = ref[:, 128:384]
        v_t = all_ref[:, 256:384].T

        @pl.loop(0, 4)
        def _(i):
            rows = aligned(i, 256)
            q = all_ref[rows, 0:128]
            total = None
            for head in range(2):
                probs = head_probs(all_ref[:, 128:256], only_head(q, head, 1)).astype(BF)
                term = dot(only_head(v_t, head, 0), probs, ((1,), (0,)))
                total = term if total is None else total + term
            out_s[rows] = total.T.astype(BF)

        for i in range(4):
            outs[i][...] = out_s[i * 256 : (i + 1) * 256]

    return kernel(
        body, [((1024, 384), BF)] + [((256, 128), BF)] * 4, index, *parts,
        scratch=[((1024, 128), BF)], after=after, cost=35, name="attention",
    )


def attention_back(index, qkv, grads, after):
    def body(idx, all_ref, *refs):
        gs, outs, (g_s, dq_s, dk_s, dv_s) = refs[:4], refs[4:8], refs[8:]
        for i in range(4):
            g_s[i * 256 : (i + 1) * 256] = gs[i][...]
        k_t = all_ref[:, 128:256].T
        dk_s[...] = jnp.zeros_like(dk_s)
        dv_s[...] = jnp.zeros_like(dv_s)

        @pl.loop(0, 4)
        def _(i):
            rows = aligned(i, 256)
            q, g = all_ref[rows, 0:128], g_s[rows]
            dq_t = None
            for head in range(2):
                q_head, g_head = only_head(q, head, 1), only_head(g, head, 1)
                probs = head_probs(all_ref[:, 128:256], q_head)
                g_probs = dot(all_ref[:, 256:384], g_head, ((1,), (1,)))
                dv_s[...] += dot(probs.astype(BF), g_head, ((1,), (0,)))
                inner = jnp.sum(probs * g_probs, axis=0, keepdims=True)
                g_scores = (probs * (g_probs - inner)).astype(BF)
                dk_s[...] += dot(g_scores, q_head, ((1,), (0,)))
                term = dot(only_head(k_t, head, 0), g_scores, ((1,), (0,)))
                dq_t = term if dq_t is None else dq_t + term
            dq_s[rows] = (dq_t.T * HD**-0.5).astype(BF)

        for i in range(4):
            rows = slice(i * 256, (i + 1) * 256)
            outs[i][:, 0:128] = dq_s[rows]
            outs[i][:, 128:256] = dk_s[rows].astype(BF)
            outs[i][:, 256:384] = dv_s[rows].astype(BF)

    return kernel(
        body, [((256, 384), BF)] * 4, index, qkv, *grads,
        scratch=[((1024, 128), BF)] * 2 + [((1024, 128), F32)] * 2, after=after, cost=36, name="attention_back",
    )


def by_token(refs, dst):
    width = refs[0].shape[-1]
    for l in range(2):
        for j in range(2):
            for r in range(4):
                dst[r * 128 + l * 64 : r * 128 + l * 64 + 64, j * width : (j + 1) * width] = refs[2 * l + j][
                    r * 64 : (r + 1) * 64
                ]


ROWS_OUT = [((128, 1024), F32)] + [((128, 1024), BF)] * 3


def put_rows(value, outs, cols):
    outs[0][:, cols] = value[0:128]
    for r in (1, 2, 3):
        outs[r][0:128, cols] = value[r * 128 : (r + 1) * 128].astype(BF)


def project_out(index, heads, proj):
    def body(idx, a, b, c, d, w_ref, att_ref, *outs):
        by_token((a, b, c, d), att_ref)

        @pl.loop(0, 4)
        def _(n):
            cols = aligned(n, 256)
            put_rows(dot(att_ref[...], w_ref[:, cols], ((1,), (0,))), outs, cols)

    return kernel(body, [((512, 256), BF)] + ROWS_OUT, index, *heads, proj, name="project_out")


def sum_rows(refs):
    return refs[0][...] + (refs[1][0:128].astype(F32) + refs[2][0:128].astype(F32) + refs[3][0:128].astype(F32))


def middle_rows(index, terms, latent, mod, after=()):
    def body(idx, a, b, c, d, x_ref, mod_ref, attn_ref, mid_ref, in_ref):
        mod = mod_ref[...]
        attn = sum_rows((a, b, c, d))
        middle = x_ref[0:128].astype(F32) + mod_rows(mod, 2) * attn
        normed, _ = normalize(middle)
        attn_ref[...] = attn
        mid_ref[...] = middle
        in_ref[...] = (normed * (1.0 + mod_rows(mod, 4)) + mod_rows(mod, 3)).astype(BF)

    outs = [((128, 1024), F32), ((128, 1024), F32), ((128, 1024), BF)]
    return kernel(body, outs, index, *terms, latent, mod, after=after, cost=35, name="middle_rows")


def grad_mlp(index, grad_out, mod, after=()):
    def body(idx, g_ref, mod_ref, out_ref):
        @pl.loop(0, 4)
        def _(r):
            rows = aligned(r, 128)
            out_ref[rows] = (mod_rows(mod_ref[...], 5) * g_ref[rows].astype(F32)).astype(BF)

    return kernel(body, [((512, 1024), BF)], index, grad_out, mod, after=after, cost=31, token=True, name="grad_mlp")


def grad_act(index, g_mlp, down):
    def body(idx, g_ref, w_ref, out_ref):
        @pl.loop(0, 4)
        def _(n):
            out_ref[:, aligned(n, 256)] = dot(g_ref[...], w_ref[aligned(n, 256)], ((1,), (1,)))

    return kernel(body, [((512, 1024), F32)], index, g_mlp, down, cost=33, name="grad_act")[0]


def feed_forward(index, blocks, g_act, up):
    def body(idx, a, b, c, d, g_ref, w_ref, x_ref, act_ref, gup_ref, *outs):
        for r, ref in enumerate((a, b, c, d)):
            x_ref[r * 128 : (r + 1) * 128] = ref[...]

        @pl.loop(0, 4)
        def _(n):
            cols = aligned(n, 256)
            act, slope = gelu_and_slope(dot(x_ref[...], w_ref[:, cols], ((1,), (0,))))
            act_ref[:, cols] = act.astype(BF)
            gup_ref[:, cols] = (g_ref[:, cols] * slope).astype(BF)

        @pl.loop(0, 4)
        def _(n):
            cols = aligned(n, 256)
            put_rows(dot(gup_ref[...], w_ref[cols], ((1,), (1,))), outs, cols)

    return kernel(
        body, [((512, 1024), BF)] * 3 + ROWS_OUT, index, *blocks, g_act, up, name="feed_forward"
    )


def mlp_rows(index, act, down, after=()):
    def body(idx, a_ref, w_ref, *outs):
        @pl.loop(0, 4)
        def _(n):
            cols = aligned(n, 256)
            put_rows(dot(a_ref[...], w_ref[:, cols], ((1,), (0,))), outs, cols)

    return kernel(body, ROWS_OUT, index, act, down, after=after, cost=33, token=True, name="mlp_rows")


def hidden_grads(index, rows, g_up, g_mlp, act):
    def body(idx, x_ref, gup_ref, gm_ref, act_ref, kept_ref, sent_ref):
        for n, (left, right) in enumerate(((x_ref, gup_ref), (gm_ref, act_ref))):
            for i in range(4):
                turned = left[:, i * 256 : (i + 1) * 256].T
                dst = sent_ref if i & 1 else kept_ref

                @pl.loop(0, 4)
                def _(m):
                    cols = aligned(m, 256)
                    dst[n, i >> 1, :, cols] = dot(turned, right[:, cols], ((1,), (0,))).astype(dst.dtype)

    return kernel(
        body, [((2, 2, 256, 1024), F32), ((2, 2, 256, 1024), BF)], index, rows, g_up, g_mlp, act, cost=33, space=pltpu.VMEM, token=True, name="hidden_grads"
    )


def out_rows(index, terms, middle, grad_out, mod, after):
    def body(idx, a, b, c, d, mid_ref, g_ref, mod_ref, out_ref, row_ref):
        mlp = sum_rows((a, b, c, d))
        out_ref[...] = (mid_ref[...] + mod_rows(mod_ref[...], 5) * mlp).astype(BF)
        sums = latent_sums(g_ref[0:128].astype(F32) * mlp)
        row_ref[...] = jnp.zeros_like(row_ref)
        for l in range(2):
            row_ref[l : l + 1] = sums[l]

    outs = [((128, 1024), BF), ((8, 1024), F32)]
    return kernel(body, outs, index, *terms, middle, grad_out, mod, after=after, cost=30, name="out_rows")


def middle_back(index, terms, middle, attn, grad_out, mod, after=()):
    def body(idx, a, b, c, d, mid_ref, attn_ref, g_ref, mod_ref, gmid_ref, gattn_ref, row_ref):
        mod = mod_ref[...]
        g_in = sum_rows((a, b, c, d))
        normed, inverse = normalize(mid_ref[...])
        g_mid = g_ref[0:128].astype(F32) + norm_back(g_in * (1.0 + mod_rows(mod, 4)), normed, inverse)
        gmid_ref[...] = g_mid
        gattn_ref[...] = (mod_rows(mod, 2) * g_mid).astype(BF)
        row_ref[...] = jnp.zeros_like(row_ref)
        for k, value in enumerate((g_mid * attn_ref[...], g_in, g_in * normed)):
            sums = latent_sums(value)
            for l in range(2):
                row_ref[3 * l + k : 3 * l + k + 1] = sums[l]

    outs = [((128, 1024), F32), ((128, 1024), BF), ((8, 1024), F32)]
    return kernel(body, outs, index, *terms, middle, attn, grad_out, mod, after=after, cost=35, name="middle_back")


def heads_back(index, blocks, proj, after=()):
    def body(idx, a, b, c, d, w_ref, g_ref, *outs):
        for r, ref in enumerate((a, b, c, d)):
            g_ref[r * 128 : (r + 1) * 128] = ref[...]
        for j in range(2):
            block = dot(g_ref[...], w_ref[j * 128 : (j + 1) * 128], ((1,), (1,))).astype(BF).reshape(4, 2, 64, 128)
            for l in range(2):
                outs[2 * l + j][...] = block[:, l].reshape(256, 128)

    outs = [((512, 1024), BF)] + [((256, 128), BF)] * 4
    return kernel(body, outs, index, *blocks, proj, after=after, name="heads_back")


def input_back(index, blocks, w_qkv, latent, stats, row_mlp, rows_mid, after):
    def body(idx, a, b, c, d, w_ref, x_ref, stat_ref, row5_ref, row234_ref, g_ref, *rest):
        outs, own_ref, gm = rest[:4], rest[4], rest[5]
        by_token((a, b, c, d), g_ref)
        gm[...] = jnp.zeros_like(gm)

        @pl.loop(0, 4)
        def _(n):
            cols = aligned(n, 256)
            value = dot(g_ref[...], w_ref[cols], ((1,), (1,)))
            put_rows(value, outs, cols)
            mean = jnp.concatenate([stat_ref[:, 0:128]] * 2, axis=1)
            inverse = jnp.concatenate([stat_ref[:, 128:256]] * 2, axis=1)
            scaled = value * ((x_ref[:, cols].astype(F32) - mean) * inverse)
            for l in range(2):
                for k, part in enumerate((value, scaled)):
                    total = part.reshape(4, 2, 64, 256)[:, l].reshape(256, 256)
                    gm[6 * l + k : 6 * l + k + 1, cols] = jnp.sum(total, axis=0, keepdims=True)

        for l in range(2):
            for k in range(3):
                gm[6 * l + 2 + k : 6 * l + 3 + k] = row234_ref[3 * l + k : 3 * l + k + 1]
            gm[6 * l + 5 : 6 * l + 6] = row5_ref[l : l + 1]
        for r in range(4):
            for x in range(2):
                block = gm[:, aligned(idx[COLS + 2 * r + x], 128)]
                flipped = jnp.concatenate([block[6:12], block[0:6], block[12:16]], axis=0)
                block = jnp.where(idx[Z_LAT] == 1, flipped, block)
                if r == 0:
                    own_ref[:, x * 128 : (x + 1) * 128] = block
                else:
                    high = block.astype(BF)
                    outs[r][128:144, x * 128 : (x + 1) * 128] = high
                    outs[r][128:144, 256 + x * 128 : 384 + x * 128] = (block - high.astype(F32)).astype(BF)
                    outs[r][128:144, 512 + x * 256 : 768 + x * 256] = jnp.zeros((16, 256), BF)

    return kernel(
        body,
        [((512, 768), BF), ((128, 1024), F32)] + [((144, 1024), BF)] * 3 + [((16, 256), F32)],
        index, *blocks, w_qkv, latent, stats, row_mlp, rows_mid,
        scratch=[((16, 1024), F32)], after=after, token=True, name="input_back",
    )


def attention_grads(index, rows, g_triple, g_attn, attended, after=()):
    def body(idx, x_ref, gt_ref, ga_ref, att_ref, kept_ref, sent_ref):
        for i in range(4):
            dst = sent_ref if i & 1 else kept_ref
            x_t = x_ref[:, i * 256 : (i + 1) * 256].T
            g_t = ga_ref[:, i * 256 : (i + 1) * 256].T
            for j in range(2):
                start = (j ^ idx[Z_HEAD]) * 512
                dst[i >> 1, :, pl.ds(pl.multiple_of(start, 512), 384)] = dot(
                    x_t, gt_ref[:, j * 384 : (j + 1) * 384], ((1,), (0,))
                ).astype(dst.dtype)
                dst[i >> 1, :, pl.ds(pl.multiple_of(start + 384, 128), 128)] = dot(
                    g_t, att_ref[:, j * 128 : (j + 1) * 128], ((1,), (0,))
                ).astype(dst.dtype)

    return kernel(
        body, [((2, 256, 1024), F32), ((2, 256, 1024), BF)], index, rows, g_triple, g_attn, attended, after=after, cost=33, token=True, name="attention_grads"
    )


def latent_back(index, terms, g_mod, g_mid, latent, mod, after=()):
    def body(idx, a, b, c, d, gm_ref, gmid_ref, x_ref, mod_ref, out_ref, sum_ref):
        normed, inverse = normalize(x_ref[0:128].astype(F32))
        g_in = sum_rows((a, b, c, d)) * (1.0 + mod_rows(mod_ref[...], 1))
        out_ref[...] = (gmid_ref[...] + norm_back(g_in, normed, inverse)).astype(BF)
        total = gm_ref[...]
        for ref in (b, c, d):
            total = total + (ref[128:144, 0:256].astype(F32) + ref[128:144, 256:512].astype(F32))
        sum_ref[...] = total

    return kernel(
        body, [((128, 1024), BF), ((16, 256), F32)], index, *terms, g_mod, g_mid, latent, mod, after=after, cost=35, token=True, name="latent_back"
    )


def mod_sum(index, near, far, after):
    def body(idx, a, b, own_ref, far_ref, sum_s):
        sum_s[...] = a[...] + b[...]
        own_ref[...] = sum_s[:, aligned(idx[X_LO], 128)]
        far_ref[...] = sum_s[:, aligned(1 - idx[X_LO], 128)]

    outs = [((16, 128), F32)] * 2
    return kernel(body, outs, index, near, far, scratch=[((16, 256), F32)], after=after, token=True, name="mod_sum")


def cond_terms(index, near, rows, after):
    def body(idx, near_ref, a, b, c, d, out_ref, g_s):
        g_s[...] = jnp.zeros_like(g_s)
        for x in range(2):
            for l in range(2):
                for k in range(6):
                    g_s[2 * x + l : 2 * x + l + 1, k * 128 : (k + 1) * 128] = near_ref[x, 6 * l + k : 6 * l + k + 1]
        value = g_s[...]
        value = jnp.where(idx[X_LO] == 1, jnp.concatenate([value[2:4], value[0:2], value[4:8]], axis=0), value)
        high = value.astype(BF)
        rest = value - high.astype(F32)
        middle = rest.astype(BF)
        low = (rest - middle.astype(F32)).astype(BF)
        parts = jnp.concatenate([high.astype(F32), middle.astype(F32), low.astype(F32)], axis=0).astype(BF)
        for i, ref in enumerate((a, b, c, d)):
            term = dot(parts, ref[...], ((1,), (1,)))
            out_ref[:, aligned(idx[FEAT + i], 256)] = term[0:8] + (term[8:16] + term[16:24])

    return kernel(
        body, [((8, 1024), F32)], index, near, *rows, scratch=[((8, 768), F32)], after=after, token=True, name="cond_terms"
    )


def ada_grads(index, near, far, other, conds, after):
    def body(idx, *refs):
        near, far, other, conds, out_ref, g_s, s_s = *refs[:3], refs[3:7], *refs[7:]
        for i, ref in enumerate(conds):
            rows = jax.nn.silu(ref[:, aligned(idx[FEAT], 256)].astype(F32)).astype(BF).astype(F32)
            flipped = jnp.concatenate([rows[2:4], rows[0:2]], axis=0)
            s_s[4 * i : 4 * i + 4] = jnp.where(idx[X_LO] == 1, flipped, rows)
        g_s[...] = jnp.zeros_like(g_s)
        for b in range(4):
            for c in range(2):
                block = other[b] if c else (near, far)[b >> 1][b & 1]
                for l in range(2):
                    row = (2 * (b >> 1) + c) * 4 + 2 * (b & 1) + l
                    for k in range(6):
                        g_s[row : row + 1, k * 128 : (k + 1) * 128] = block[6 * l + k : 6 * l + k + 1]
        silu = s_s[...].T
        for k in range(6):
            out_ref[:, k, :] = lax.dot_general(
                silu, g_s[:, k * 128 : (k + 1) * 128], (((1,), (0,)), ((), ())), precision=HIGHEST
            )

    return kernel(
        body, [((256, 6, 128), F32)], index, near, far, other, *conds,
        scratch=[((16, 768), F32), ((16, 256), F32)], after=after, token=True, name="ada_grads"
    )


def hidden_core(index, kept, got, after):
    count = kept.shape[0]

    def body(idx, kept_ref, got_ref, own_ref, out_ref):
        for n in range(count):
            for h in range(2):
                own_ref[n, h] = kept_ref[n, h, :, 0:512] + got_ref[n, h, :, 0:512].astype(F32)
                out_ref[n, h] = (kept_ref[n, h, :, 512:1024] + got_ref[n, h, :, 512:1024].astype(F32)).astype(BF)

    outs = [((count, 2, 256, 512), F32), ((count, 2, 256, 512), BF)]
    return kernel(body, outs, index, kept, got, after=after, cost=31, token=True, name="hidden_core")


def hidden_x_lo(index, own, got, after):
    count = own.shape[0]

    def body(idx, own_ref, got_ref, kept_ref, out_ref):
        for n in range(count):
            kept_ref[n] = own_ref[n, 0] + got_ref[n, 0].astype(F32)
            out_ref[n] = (own_ref[n, 1] + got_ref[n, 1].astype(F32)).astype(BF)

    outs = [((count, 256, 512), F32), ((count, 256, 512), BF)]
    return kernel(body, outs, index, own, got, after=after, cost=31, token=True, name="hidden_x_lo")


def pair_sum(index, own, got, after):
    def body(idx, own_ref, got_ref, out_ref):
        out_ref[...] = (own_ref[...].astype(F32) + got_ref[...].astype(F32)).astype(BF)

    return kernel(body, [(own.shape, BF)], index, own, got, after=after, cost=31, token=True, name="pair_sum")


def hidden_out(index, own, got, after):
    def body(idx, own_ref, got_ref, up_ref, down_ref):
        up_ref[...] = own_ref[0].astype(F32) + got_ref[0].astype(F32)
        down_ref[...] = (own_ref[1].astype(F32) + got_ref[1].astype(F32)).T

    outs = [((256, 512), F32), ((512, 256), F32)]
    return kernel(body, outs, index, own, got, after=after, cost=31, token=True, name="hidden_out")


def attention_out(index, own, got):
    def body(idx, a, b, qkv_ref, proj_ref):
        def total(cols):
            return a[0, :, cols].astype(F32) + b[0, :, cols].astype(F32)

        for j in range(3):
            qkv_ref[:, j, :] = total(slice(j * 128, (j + 1) * 128))
        proj_ref[...] = total(slice(384, 512)).T

    return kernel(body, [((256, 3, 128), F32), ((128, 256), F32)], index, own, got, name="attention_out")


def exchange_y(blocks):
    return [blocks[0]] + [swap(blocks[r], "tp", r) for r in (1, 2, 3)]


def gather_y(block):
    return [block] + [swap(block, "tp", r) for r in (1, 2, 3)]


def gather_tp(block):
    near = gather_y(block)
    far = swap(block, "tp", 4)
    return near + [far, swap(far, "tp", 1), swap(near[2], "tp", 4), swap(far, "tp", 3)]


def exchange_z(blocks):
    return [blocks[0]] + [swap(blocks[q], "ctx", q) for q in (1, 2, 3)]


def corner(array):
    return array[:16, :128]


def sum_four(terms):
    return (terms[0] + terms[1]) + (terms[2] + terms[3])


def shards(
    latent_in, condition, ada_weight, qkv_weight, proj_weight, up_matrix, down_matrix, out_grad
):
    s, z, t = lax.axis_index("shard"), lax.axis_index("ctx"), lax.axis_index("tp")
    x_lo, y, z_lat, z_head = t >> 2, t & 3, z >> 1, z & 1
    columns = [[((4 * x + (y ^ r)) >> 1 ^ s) * 2 + ((y ^ r) & 1) for x in range(2)] for r in range(4)]
    index = jnp.stack(
        [2 * x_lo + (l ^ z_lat) for l in range(2)]
        + [y ^ r for r in range(4)]
        + [s ^ i for i in range(4)]
        + [2 * (x_lo ^ x) + (l ^ z_lat) for x in range(2) for l in range(2)]
        + [z_head, x_lo, z_lat, t]
        + [c for pair in columns for c in pair]
    ).astype(jnp.int32)

    ada = ada_weight.reshape(256, 768)
    conds = [condition] + [swap(condition, "shard", i) for i in (1, 2, 3)]
    kept, sent = mod_terms(index, conds, ada)
    terms = mod_core(index, kept, swap(sent, "shard", 1))
    terms = [terms[0]] + [swap_x(terms[b], b) for b in (1, 2, 3)]
    packed = pack_first(index, qkv_weight, proj_weight, tuple(terms[1:]))
    first = [packed] + [swap_x(packed, b) for b in (1, 2, 3)]
    packed = pack_second(index, up_matrix, down_matrix, (corner(first[3]),))
    mod_x = mod_ring(index, terms)
    near = jnp.concatenate([mod_x, swap(mod_x, "tp", 1)])
    latent = arrange(index, latent_in)
    mod, done = mod_assemble(index, near, swap(near, "tp", 2), (latent,))
    first = stack_blocks(index, first, (done,))[0].reshape(4, 256, 512)

    input_a, w_qkv, stats, proj, *parts, done = project_in(index, latent, mod, first, swap(first, "shard", 1))
    parts = exchange_z(parts)
    grad_out = arrange(index, out_grad, (done,))
    g_mlp, g_done = grad_mlp(index, grad_out, mod, (done,))
    packed, done = stack_blocks(index, [packed, swap(packed, "tp", 4)], tuple(corner(b) for b in parts[1:]))
    ada_far = swap(ada, "shard", 2)
    ada_rows = [ada, swap(ada, "shard", 1), ada_far, swap(ada_far, "shard", 1)]
    far = swap(packed, "shard", 2)
    up, down = assemble(index, packed, swap(packed, "shard", 1), far, swap(far, "shard", 1))
    g_act = grad_act(index, g_mlp, down)

    qkv, *heads = attention(index, parts, (g_done, done))
    heads = exchange_z(heads)
    attended, *terms = project_out(index, heads, proj)
    attn, middle, input_b = middle_rows(index, exchange_y(terms), latent, mod, (corner(far),))
    rows_b, act, g_up, *terms = feed_forward(index, gather_y(input_b), g_act, up)
    ud_kept, ud_sent, done = hidden_grads(index, rows_b, g_up, g_mlp, act)
    g_mid, g_attn, rows_mid = middle_back(
        index, exchange_y(terms), middle, attn, grad_out, mod, (done, corner(ada_rows[1]), corner(ada_rows[3]))
    )
    *mlp_terms, done = mlp_rows(index, act, down, (g_attn,))
    ud, ud_sent, done = hidden_core(index, ud_kept, swap(ud_sent, "shard", 1), (done,))
    g_attn, *g_parts = heads_back(index, gather_y(g_attn), proj, (done,))
    g_parts = exchange_z(g_parts)

    g_blocks = attention_back(index, qkv, g_parts, ())
    out_block, row_mlp = out_rows(index, exchange_y(mlp_terms), middle, grad_out, mod, (g_blocks[0],))
    out_blocks = gather_tp(out_block)
    ud, ud_sent, done = hidden_x_lo(index, ud, swap(ud_sent, "tp", 4), (out_block,))
    g_blocks = exchange_z(g_blocks)
    g_triple, *rest, done = input_back(
        index, g_blocks, w_qkv, latent, stats, row_mlp, rows_mid, (done, corner(out_blocks[1]))
    )
    ud, ud_done = pair_sum(index, ud, swap(ud_sent, "shard", 2), (done,))
    kept, sent, done = attention_grads(index, input_a, g_triple, g_attn, attended)
    own, g_mod, done = latent_back(index, exchange_y(rest[:4]), rest[4], g_mid, latent, mod, (done, ud_done))

    blocks = gather_tp(own)
    g_mod = g_mod + swap(g_mod, "ctx", 1)
    qp, qp_sent, done = hidden_core(index, kept[None], swap(sent[None], "shard", 1), (done,))
    mod_own, mod_far, done = mod_sum(index, g_mod, swap(g_mod, "ctx", 2), (done,))
    near = jnp.stack([mod_own, swap(mod_far, "tp", 4)])
    ud, done = pair_sum(index, ud, swap(ud, "ctx", 1), (done,))
    qp, qp_sent, done = hidden_x_lo(
        index, qp, swap(qp_sent, "tp", 4), (done, *[corner(b) for b in blocks[1:4]])
    )
    terms, done = cond_terms(index, near, ada_rows, (done,))
    qp, done = pair_sum(index, qp, swap(qp_sent, "shard", 2), (done,))
    far = swap(near, "shard", 2)
    terms = terms + swap(terms, "tp", 4)
    up_grad, down_grad, done = hidden_out(index, ud, swap(ud, "ctx", 2), (done,))
    ada_grad, done = ada_grads(index, near, far, swap(jnp.concatenate([near, far]), "shard", 1), conds, (done,))
    terms = terms + swap(terms, "tp", 1)
    qp, done = pair_sum(index, qp, swap(qp, "ctx", 1), (done,))
    latent_grad, done = restore(index, blocks, (done,))
    latent_out, done = restore(index, out_blocks, (done,))
    terms = terms + swap(terms, "tp", 2)
    qkv_grad, proj_grad = attention_out(index, qp, swap(qp, "ctx", 2))
    _, silu_pull = jax.vjp(jax.nn.silu, condition.astype(F32))
    condition_grad = silu_pull(terms[:4])[0]

    return (
        latent_out,
        latent_grad,
        condition_grad,
        ada_grad,
        qkv_grad,
        proj_grad,
        up_grad,
        down_grad,
    )


def solution(mesh):
    placed = (
        P("shard", "ctx", None),
        P("shard", None),
        P("shard", None, "tp"),
        P("shard", None, "tp"),
        P("tp", "shard"),
        P("shard", "tp"),
        P("tp", "shard"),
        P("shard", "ctx", None),
    )
    return jax.shard_map(
        shards,
        mesh=mesh,
        in_specs=placed,
        out_specs=(
            P("shard", "ctx", None),
            P("shard", "ctx", None),
            P("shard", None),
            P("shard", None, "tp"),
            P("shard", None, "tp"),
            P("tp", "shard"),
            P("shard", "tp"),
            P("tp", "shard"),
        ),
        check_vma=False,
    )
```

```python
import jax
import jax.numpy as jnp
from jax import lax
from jax.experimental import pallas as pl
from jax.experimental.pallas import tpu as pltpu
from jax.sharding import PartitionSpec as P

HD = 64
EPSILON = 1e-06
HIGHEST = lax.Precision.HIGHEST
BF = jnp.bfloat16
F32 = jnp.float32


def swap(value, axis, bits):
    size = {"shard": 4, "ctx": 4, "tp": 8}[axis]
    return lax.ppermute(value, axis, [(i, i ^ bits) for i in range(size)])


def swap_x(value, bits):
    if bits == 1:
        return swap(value, "tp", 4)
    if bits == 2:
        return swap(value, "shard", 2)
    return lax.ppermute(value, ("shard", "tp"), [(i, i ^ 20) for i in range(32)])


def pick(array, index, axis=0):
    return lax.dynamic_index_in_dim(array, index, axis, keepdims=False)


def dot(a, b, contract):
    return lax.dot_general(a, b, (contract, ((), ())), preferred_element_type=F32)


def normalize(rows):
    centred = rows - jnp.mean(rows, axis=-1, keepdims=True)
    inverse = lax.rsqrt(jnp.mean(centred * centred, axis=-1, keepdims=True) + EPSILON)
    return centred * inverse, inverse


def norm_back(grad, normed, inverse):
    first = jnp.mean(grad, axis=-1, keepdims=True)
    second = jnp.mean(grad * normed, axis=-1, keepdims=True)
    return inverse * (grad - first - normed * second)


GELU_A = 0.7978845608028654
GELU_B = 0.044715


def gelu_and_slope(v):
    square = v * v
    t = jnp.tanh(GELU_A * (v + GELU_B * v * square))
    half = 0.5 * (1.0 + t)
    return v * half, half + 0.5 * v * (1.0 - t * t) * (GELU_A * (1.0 + 3.0 * GELU_B * square))


LAT, TOK, FEAT, OUT_LAT, Z_HEAD, X_LO, Z_LAT, TP, COLS = 0, 2, 6, 10, 14, 15, 16, 17, 18


def kernel(body, outs, index, *arrays, scratch=(), after=(), vmem=16, cost=10, space=None, token=False, name):
    count = 1 + len(arrays)

    outs = list(outs)
    if token:
        outs.append(((8, 128), F32))

    def run(*refs):
        results = refs[count + len(after) :]
        if token:
            place = len(outs) - 1
            results[place][...] = jnp.zeros((8, 128), F32)
            results = results[:place] + results[place + 1 :]
        body(*refs[:count], *results)

    return pl.pallas_call(
        run,
        in_specs=[pl.BlockSpec(memory_space=pltpu.SMEM)]
        + [pl.BlockSpec()] * len(arrays)
        + [pl.BlockSpec(memory_space=pl.ANY)] * len(after),
        out_specs=[pl.BlockSpec(memory_space=space)] * len(outs),
        out_shape=[jax.ShapeDtypeStruct(shape, kind) for shape, kind in outs],
        scratch_shapes=[pltpu.VMEM(shape, kind) for shape, kind in scratch],
        compiler_params=pltpu.CompilerParams(vmem_limit_bytes=vmem * 2**20),
        cost_estimate=pl.CostEstimate(flops=2**cost, bytes_accessed=1024, transcendentals=0),
        name=name,
    )(index, *arrays, *after)


def aligned(start, step):
    return pl.ds(pl.multiple_of(start * step, step), step)


def arrange(index, array, after=()):
    def body(idx, src, *refs):
        dst = refs[-1]
        for r in range(4):
            for l in range(2):
                for i in range(4):
                    dst[r * 128 + l * 64 : r * 128 + l * 64 + 64, i * 256 : (i + 1) * 256] = src[
                        idx[LAT + l] - 2 * idx[X_LO], aligned(idx[TOK + r], 64), aligned(idx[FEAT + i], 256)
                    ]

    return pl.pallas_call(
        body,
        grid_spec=pltpu.PrefetchScalarGridSpec(
            num_scalar_prefetch=1,
            grid=(1,),
            in_specs=[pl.BlockSpec((2, 256, 1024), lambda n, idx: (idx[X_LO], 0, 0))]
            + [pl.BlockSpec(memory_space=pl.ANY)] * len(after),
            out_specs=pl.BlockSpec((512, 1024), lambda n, idx: (0, 0)),
        ),
        out_shape=jax.ShapeDtypeStruct((512, 1024), array.dtype),
        compiler_params=pltpu.CompilerParams(vmem_limit_bytes=16 * 2**20),
        cost_estimate=pl.CostEstimate(flops=2**31, bytes_accessed=1024, transcendentals=0),
        name="arrange",
    )(index, array, *after)


def restore(index, blocks, after=()):
    def body(idx, *refs):
        out = refs[-1]
        for x in range(2):
            for r in range(4):
                for l in range(2):
                    for i in range(4):
                        out[idx[OUT_LAT + 2 * x + l], aligned(idx[TOK + r], 64), aligned(idx[FEAT + i], 256)] = refs[
                            4 * x + r
                        ][l * 64 : l * 64 + 64, i * 256 : (i + 1) * 256].astype(F32)

    return kernel(body, [((4, 256, 1024), F32)], index, *blocks, after=after, cost=31, token=True, name="restore")


def pack_first(index, qkv, proj, after):
    def body(idx, q_ref, p_ref, out_ref):
        for j in range(3):
            out_ref[:, j * 128 : (j + 1) * 128] = q_ref[:, j]
        for h in range(2):
            out_ref[h * 128 : (h + 1) * 128, 384:512] = p_ref[:, h * 128 : (h + 1) * 128]

    return kernel(body, [((256, 512), BF)], index, qkv, proj, after=after, name="pack_first")[0]


def pack_second(index, up, down, after):
    def body(idx, u_ref, d_ref, out_ref):
        out_ref[0:256] = u_ref[:, 0:256]
        out_ref[256:512] = u_ref[:, 256:512]
        out_ref[512:1024] = d_ref[...]

    return kernel(body, [((1024, 256), BF)], index, up, down, after=after, cost=31, name="pack_second")[0]


def mod_terms(index, conds, ada):
    def body(idx, a, b, c, d, w_ref, kept_ref, sent_ref, s_s):
        for i, ref in enumerate((a, b, c, d)):
            s_s[4 * i : 4 * i + 4] = jax.nn.silu(ref[:, aligned(idx[FEAT], 256)].astype(F32))
        terms = dot(s_s[...].astype(BF), w_ref[...], ((1,), (0,)))
        for h in range(2):
            kept_ref[4 * h : 4 * h + 4] = terms[8 * h : 8 * h + 4]
            sent_ref[4 * h : 4 * h + 4] = terms[8 * h + 4 : 8 * h + 8]

    return kernel(
        body, [((8, 768), F32)] * 2, index, *conds, ada, scratch=[((16, 256), F32)], name="mod_terms"
    )


def mod_core(index, kept, got):
    def body(idx, a, b, *outs):
        value = a[...] + b[...]
        for n in range(4):
            rows = value[4 * (n >> 1) : 4 * (n >> 1) + 4]
            wanted = idx[X_LO] ^ (n & 1)
            outs[n][...] = jnp.where(wanted == 1, rows[2:4], rows[0:2])

    return kernel(body, [((2, 768), F32)] * 4, index, kept, got, name="mod_core")


def mod_ring(index, terms):
    def body(idx, a, b, c, d, out_ref):
        out_ref[0] = (a[...] + c[...]).astype(BF).astype(F32)
        out_ref[1] = (b[...] + d[...]).astype(BF).astype(F32)

    return kernel(body, [((2, 2, 768), F32)], index, *terms, name="mod_ring")[0]


def mod_assemble(index, near, far, after):
    def body(idx, near_ref, far_ref, out_ref, all_s):
        all_s[0:4] = near_ref[...]
        all_s[4:8] = far_ref[...]
        for p in range(8):
            column = 2 * idx[FEAT + (p >> 1)] + (p & 1)
            block = all_s[2 * ((column & 3) ^ idx[TOK]) + ((column >> 2) ^ idx[X_LO])]
            block = jnp.where(idx[Z_LAT] == 1, jnp.concatenate([block[1:2], block[0:1]], axis=0), block)
            for l in range(2):
                for k in range(6):
                    out_ref[6 * l + k : 6 * l + k + 1, p * 128 : (p + 1) * 128] = block[
                        l : l + 1, k * 128 : (k + 1) * 128
                    ]

    return kernel(
        body, [((12, 1024), F32)], index, near, far, scratch=[((8, 2, 768), F32)], after=after, token=True, name="mod_assemble"
    )


def stack_blocks(index, blocks, after):
    rows, width = blocks[0].shape

    def body(idx, *refs):
        for r, ref in enumerate(refs[:-1]):
            refs[-1][r * rows : (r + 1) * rows] = ref[...]

    outs = [((len(blocks) * rows, width), BF)]
    return kernel(body, outs, index, *blocks, after=after, cost=31, token=True, name="stack_blocks")


def mod_rows(mod, k, width=64):
    return jnp.concatenate(
        [jnp.broadcast_to(mod[6 * l + k : 6 * l + k + 1], (64, mod.shape[1])) for l in range(2)], axis=0
    )


def latent_sums(value):
    return [jnp.sum(value[l * 64 : (l + 1) * 64], axis=0, keepdims=True) for l in range(2)]


def project_in(index, latent, mod, mine, other, after=()):
    def body(idx, x_ref, mod_ref, *refs):
        blocks, (in_ref, w_ref, stat_ref, proj_ref), outs = refs[:2], refs[2:6], refs[6:]
        flip = idx[Z_HEAD] == 1
        for i in range(4):
            pair = [blocks[i & 1][2 * (i >> 1) + j] for j in range(2)]
            for j in range(2):
                block = jnp.where(flip, pair[1 - j], pair[j])
                w_ref[i * 256 : (i + 1) * 256, j * 384 : (j + 1) * 384] = block[:, 0:384]
                for h in range(2):
                    proj_ref[j * 128 : (j + 1) * 128, i * 256 + h * 128 : i * 256 + (h + 1) * 128] = block[
                        h * 128 : (h + 1) * 128, 384:512
                    ]

        @pl.loop(0, 4)
        def _(r):
            rows = aligned(r, 128)
            x = x_ref[rows].astype(F32)
            centred = x - jnp.mean(x, axis=-1, keepdims=True)
            inverse = lax.rsqrt(jnp.mean(centred * centred, axis=-1, keepdims=True) + EPSILON)
            normed = centred * inverse
            in_ref[rows] = (normed * (1.0 + mod_rows(mod_ref[...], 1)) + mod_rows(mod_ref[...], 0)).astype(BF)
            stat_ref[rows, 0:128] = jnp.broadcast_to(x[:, 0:1] - centred[:, 0:1], (128, 128))
            stat_ref[rows, 128:256] = jnp.broadcast_to(inverse, (128, 128))

        for j in range(2):
            block = dot(in_ref[...], w_ref[:, j * 384 : (j + 1) * 384], ((1,), (0,))).astype(BF)
            block = block.reshape(4, 2, 64, 384)
            for l in range(2):
                outs[2 * l + j][...] = block[:, l].reshape(256, 384)

    return kernel(
        body,
        [((512, 1024), BF), ((1024, 768), BF), ((512, 256), F32), ((256, 1024), BF)] + [((256, 384), BF)] * 4,
        index, latent, mod, mine, other, after=after, cost=33, token=True, name="project_in",
    )


def assemble(index, *blocks):
    def body(idx, a, b, c, d, up_ref, down_ref):
        for i, block in enumerate((a, b, c, d)):
            wide = slice(i * 256, (i + 1) * 256)
            for j in range(2):
                rows = j * 1024
                up_ref[wide, j * 512 : j * 512 + 256] = block[rows : rows + 256]
                up_ref[wide, j * 512 + 256 : (j + 1) * 512] = block[rows + 256 : rows + 512]
                down_ref[j * 512 : (j + 1) * 512, wide] = block[rows + 512 : rows + 1024]

    return kernel(body, [((1024, 1024), BF)] * 2, index, *blocks, cost=32, name="assemble")


def only_head(block, head, axis):
    lane = lax.broadcasted_iota(jnp.int32, block.shape, axis)
    return jnp.where((lane >= head * HD) & (lane < (head + 1) * HD), block, jnp.zeros_like(block))


def head_probs(k, q_head):
    scores = dot(k, q_head, ((1,), (1,)))
    powered = jnp.exp(scores - jnp.max(scores, axis=0, keepdims=True))
    return powered * (1.0 / jnp.sum(powered, axis=0, keepdims=True))


def attention(index, parts, after=()):
    def body(idx, *refs):
        ins, all_ref, outs, out_s = refs[:4], refs[4], refs[5:9], refs[9]
        for i, ref in enumerate(ins):
            rows = slice(i * 256, (i + 1) * 256)
            all_ref[rows, 0:128] = ref[:, 0:128] * jnp.asarray(HD**-0.5, BF)
            all_ref[rows, 128:384] = ref[:, 128:384]
        v_t = all_ref[:, 256:384].T

        @pl.loop(0, 4)
        def _(i):
            rows = aligned(i, 256)
            q = all_ref[rows, 0:128]
            total = None
            for head in range(2):
                probs = head_probs(all_ref[:, 128:256], only_head(q, head, 1)).astype(BF)
                term = dot(only_head(v_t, head, 0), probs, ((1,), (0,)))
                total = term if total is None else total + term
            out_s[rows] = total.T.astype(BF)

        for i in range(4):
            outs[i][...] = out_s[i * 256 : (i + 1) * 256]

    return kernel(
        body, [((1024, 384), BF)] + [((256, 128), BF)] * 4, index, *parts,
        scratch=[((1024, 128), BF)], after=after, cost=35, name="attention",
    )


def attention_back(index, qkv, grads, after):
    def body(idx, all_ref, *refs):
        gs, outs, (g_s, dq_s, dk_s, dv_s) = refs[:4], refs[4:8], refs[8:]
        for i in range(4):
            g_s[i * 256 : (i + 1) * 256] = gs[i][...]
        k_t = all_ref[:, 128:256].T
        dk_s[...] = jnp.zeros_like(dk_s)
        dv_s[...] = jnp.zeros_like(dv_s)

        @pl.loop(0, 4)
        def _(i):
            rows = aligned(i, 256)
            q, g = all_ref[rows, 0:128], g_s[rows]
            dq_t = None
            for head in range(2):
                q_head, g_head = only_head(q, head, 1), only_head(g, head, 1)
                probs = head_probs(all_ref[:, 128:256], q_head)
                g_probs = dot(all_ref[:, 256:384], g_head, ((1,), (1,)))
                dv_s[...] += dot(probs.astype(BF), g_head, ((1,), (0,)))
                inner = jnp.sum(probs * g_probs, axis=0, keepdims=True)
                g_scores = (probs * (g_probs - inner)).astype(BF)
                dk_s[...] += dot(g_scores, q_head, ((1,), (0,)))
                term = dot(only_head(k_t, head, 0), g_scores, ((1,), (0,)))
                dq_t = term if dq_t is None else dq_t + term
            dq_s[rows] = (dq_t.T * HD**-0.5).astype(BF)

        for i in range(4):
            rows = slice(i * 256, (i + 1) * 256)
            outs[i][:, 0:128] = dq_s[rows]
            outs[i][:, 128:256] = dk_s[rows].astype(BF)
            outs[i][:, 256:384] = dv_s[rows].astype(BF)

    return kernel(
        body, [((256, 384), BF)] * 4, index, qkv, *grads,
        scratch=[((1024, 128), BF)] * 2 + [((1024, 128), F32)] * 2, after=after, cost=36, name="attention_back",
    )


def by_token(refs, dst):
    width = refs[0].shape[-1]
    for l in range(2):
        for j in range(2):
            for r in range(4):
                dst[r * 128 + l * 64 : r * 128 + l * 64 + 64, j * width : (j + 1) * width] = refs[2 * l + j][
                    r * 64 : (r + 1) * 64
                ]


ROWS_OUT = [((128, 1024), F32)] + [((128, 1024), BF)] * 3


def put_rows(value, outs, cols):
    outs[0][:, cols] = value[0:128]
    for r in (1, 2, 3):
        outs[r][0:128, cols] = value[r * 128 : (r + 1) * 128].astype(BF)


def project_out(index, heads, proj):
    def body(idx, a, b, c, d, w_ref, att_ref, *outs):
        by_token((a, b, c, d), att_ref)

        @pl.loop(0, 4)
        def _(n):
            cols = aligned(n, 256)
            put_rows(dot(att_ref[...], w_ref[:, cols], ((1,), (0,))), outs, cols)

    return kernel(body, [((512, 256), BF)] + ROWS_OUT, index, *heads, proj, name="project_out")


def sum_rows(refs):
    return refs[0][...] + (refs[1][0:128].astype(F32) + refs[2][0:128].astype(F32) + refs[3][0:128].astype(F32))


def middle_rows(index, terms, latent, mod, after=()):
    def body(idx, a, b, c, d, x_ref, mod_ref, attn_ref, mid_ref, in_ref):
        mod = mod_ref[...]
        attn = sum_rows((a, b, c, d))
        middle = x_ref[0:128].astype(F32) + mod_rows(mod, 2) * attn
        normed, _ = normalize(middle)
        attn_ref[...] = attn
        mid_ref[...] = middle
        in_ref[...] = (normed * (1.0 + mod_rows(mod, 4)) + mod_rows(mod, 3)).astype(BF)

    outs = [((128, 1024), F32), ((128, 1024), F32), ((128, 1024), BF)]
    return kernel(body, outs, index, *terms, latent, mod, after=after, cost=35, name="middle_rows")


def grad_mlp(index, grad_out, mod, after=()):
    def body(idx, g_ref, mod_ref, out_ref):
        @pl.loop(0, 4)
        def _(r):
            rows = aligned(r, 128)
            out_ref[rows] = (mod_rows(mod_ref[...], 5) * g_ref[rows].astype(F32)).astype(BF)

    return kernel(body, [((512, 1024), BF)], index, grad_out, mod, after=after, cost=31, token=True, name="grad_mlp")


def grad_act(index, g_mlp, down):
    def body(idx, g_ref, w_ref, out_ref):
        @pl.loop(0, 4)
        def _(n):
            out_ref[:, aligned(n, 256)] = dot(g_ref[...], w_ref[aligned(n, 256)], ((1,), (1,)))

    return kernel(body, [((512, 1024), F32)], index, g_mlp, down, cost=33, name="grad_act")[0]


def feed_forward(index, blocks, g_act, up):
    def body(idx, a, b, c, d, g_ref, w_ref, x_ref, act_ref, gup_ref, *outs):
        for r, ref in enumerate((a, b, c, d)):
            x_ref[r * 128 : (r + 1) * 128] = ref[...]

        @pl.loop(0, 4)
        def _(n):
            cols = aligned(n, 256)
            act, slope = gelu_and_slope(dot(x_ref[...], w_ref[:, cols], ((1,), (0,))))
            act_ref[:, cols] = act.astype(BF)
            gup_ref[:, cols] = (g_ref[:, cols] * slope).astype(BF)

        @pl.loop(0, 4)
        def _(n):
            cols = aligned(n, 256)
            put_rows(dot(gup_ref[...], w_ref[cols], ((1,), (1,))), outs, cols)

    return kernel(
        body, [((512, 1024), BF)] * 3 + ROWS_OUT, index, *blocks, g_act, up, name="feed_forward"
    )


def mlp_rows(index, act, down, after=()):
    def body(idx, a_ref, w_ref, *outs):
        @pl.loop(0, 4)
        def _(n):
            cols = aligned(n, 256)
            put_rows(dot(a_ref[...], w_ref[:, cols], ((1,), (0,))), outs, cols)

    return kernel(body, ROWS_OUT, index, act, down, after=after, cost=33, token=True, name="mlp_rows")


def hidden_grads(index, rows, g_up, g_mlp, act):
    def body(idx, x_ref, gup_ref, gm_ref, act_ref, kept_ref, sent_ref):
        for n, (left, right) in enumerate(((x_ref, gup_ref), (gm_ref, act_ref))):
            for i in range(4):
                turned = left[:, i * 256 : (i + 1) * 256].T
                dst = sent_ref if i & 1 else kept_ref

                @pl.loop(0, 4)
                def _(m):
                    cols = aligned(m, 256)
                    dst[n, i >> 1, :, cols] = dot(turned, right[:, cols], ((1,), (0,))).astype(dst.dtype)

    return kernel(
        body, [((2, 2, 256, 1024), F32), ((2, 2, 256, 1024), BF)], index, rows, g_up, g_mlp, act, cost=33, space=pltpu.VMEM, token=True, name="hidden_grads"
    )


def out_rows(index, terms, middle, grad_out, mod, after):
    def body(idx, a, b, c, d, mid_ref, g_ref, mod_ref, out_ref, row_ref):
        mlp = sum_rows((a, b, c, d))
        out_ref[...] = (mid_ref[...] + mod_rows(mod_ref[...], 5) * mlp).astype(BF)
        sums = latent_sums(g_ref[0:128].astype(F32) * mlp)
        row_ref[...] = jnp.zeros_like(row_ref)
        for l in range(2):
            row_ref[l : l + 1] = sums[l]

    outs = [((128, 1024), BF), ((8, 1024), F32)]
    return kernel(body, outs, index, *terms, middle, grad_out, mod, after=after, cost=30, name="out_rows")


def middle_back(index, terms, middle, attn, grad_out, mod, after=()):
    def body(idx, a, b, c, d, mid_ref, attn_ref, g_ref, mod_ref, gmid_ref, gattn_ref, row_ref):
        mod = mod_ref[...]
        g_in = sum_rows((a, b, c, d))
        normed, inverse = normalize(mid_ref[...])
        g_mid = g_ref[0:128].astype(F32) + norm_back(g_in * (1.0 + mod_rows(mod, 4)), normed, inverse)
        gmid_ref[...] = g_mid
        gattn_ref[...] = (mod_rows(mod, 2) * g_mid).astype(BF)
        row_ref[...] = jnp.zeros_like(row_ref)
        for k, value in enumerate((g_mid * attn_ref[...], g_in, g_in * normed)):
            sums = latent_sums(value)
            for l in range(2):
                row_ref[3 * l + k : 3 * l + k + 1] = sums[l]

    outs = [((128, 1024), F32), ((128, 1024), BF), ((8, 1024), F32)]
    return kernel(body, outs, index, *terms, middle, attn, grad_out, mod, after=after, cost=35, name="middle_back")


def heads_back(index, blocks, proj, after=()):
    def body(idx, a, b, c, d, w_ref, g_ref, *outs):
        for r, ref in enumerate((a, b, c, d)):
            g_ref[r * 128 : (r + 1) * 128] = ref[...]
        for j in range(2):
            block = dot(g_ref[...], w_ref[j * 128 : (j + 1) * 128], ((1,), (1,))).astype(BF).reshape(4, 2, 64, 128)
            for l in range(2):
                outs[2 * l + j][...] = block[:, l].reshape(256, 128)

    outs = [((512, 1024), BF)] + [((256, 128), BF)] * 4
    return kernel(body, outs, index, *blocks, proj, after=after, name="heads_back")


def input_back(index, blocks, w_qkv, latent, stats, row_mlp, rows_mid, after):
    def body(idx, a, b, c, d, w_ref, x_ref, stat_ref, row5_ref, row234_ref, g_ref, *rest):
        outs, own_ref, gm = rest[:4], rest[4], rest[5]
        by_token((a, b, c, d), g_ref)
        gm[...] = jnp.zeros_like(gm)

        @pl.loop(0, 4)
        def _(n):
            cols = aligned(n, 256)
            value = dot(g_ref[...], w_ref[cols], ((1,), (1,)))
            put_rows(value, outs, cols)
            mean = jnp.concatenate([stat_ref[:, 0:128]] * 2, axis=1)
            inverse = jnp.concatenate([stat_ref[:, 128:256]] * 2, axis=1)
            scaled = value * ((x_ref[:, cols].astype(F32) - mean) * inverse)
            for l in range(2):
                for k, part in enumerate((value, scaled)):
                    total = part.reshape(4, 2, 64, 256)[:, l].reshape(256, 256)
                    gm[6 * l + k : 6 * l + k + 1, cols] = jnp.sum(total, axis=0, keepdims=True)

        for l in range(2):
            for k in range(3):
                gm[6 * l + 2 + k : 6 * l + 3 + k] = row234_ref[3 * l + k : 3 * l + k + 1]
            gm[6 * l + 5 : 6 * l + 6] = row5_ref[l : l + 1]
        for r in range(4):
            for x in range(2):
                block = gm[:, aligned(idx[COLS + 2 * r + x], 128)]
                flipped = jnp.concatenate([block[6:12], block[0:6], block[12:16]], axis=0)
                block = jnp.where(idx[Z_LAT] == 1, flipped, block)
                if r == 0:
                    own_ref[:, x * 128 : (x + 1) * 128] = block
                else:
                    high = block.astype(BF)
                    outs[r][128:144, x * 128 : (x + 1) * 128] = high
                    outs[r][128:144, 256 + x * 128 : 384 + x * 128] = (block - high.astype(F32)).astype(BF)
                    outs[r][128:144, 512 + x * 256 : 768 + x * 256] = jnp.zeros((16, 256), BF)

    return kernel(
        body,
        [((512, 768), BF), ((128, 1024), F32)] + [((144, 1024), BF)] * 3 + [((16, 256), F32)],
        index, *blocks, w_qkv, latent, stats, row_mlp, rows_mid,
        scratch=[((16, 1024), F32)], after=after, token=True, name="input_back",
    )


def attention_grads(index, rows, g_triple, g_attn, attended, after=()):
    def body(idx, x_ref, gt_ref, ga_ref, att_ref, kept_ref, sent_ref):
        for i in range(4):
            dst = sent_ref if i & 1 else kept_ref
            x_t = x_ref[:, i * 256 : (i + 1) * 256].T
            g_t = ga_ref[:, i * 256 : (i + 1) * 256].T
            for j in range(2):
                start = (j ^ idx[Z_HEAD]) * 512
                dst[i >> 1, :, pl.ds(pl.multiple_of(start, 512), 384)] = dot(
                    x_t, gt_ref[:, j * 384 : (j + 1) * 384], ((1,), (0,))
                ).astype(dst.dtype)
                dst[i >> 1, :, pl.ds(pl.multiple_of(start + 384, 128), 128)] = dot(
                    g_t, att_ref[:, j * 128 : (j + 1) * 128], ((1,), (0,))
                ).astype(dst.dtype)

    return kernel(
        body, [((2, 256, 1024), F32), ((2, 256, 1024), BF)], index, rows, g_triple, g_attn, attended, after=after, cost=33, token=True, name="attention_grads"
    )


def latent_back(index, terms, g_mod, g_mid, latent, mod, after=()):
    def body(idx, a, b, c, d, gm_ref, gmid_ref, x_ref, mod_ref, out_ref, sum_ref):
        normed, inverse = normalize(x_ref[0:128].astype(F32))
        g_in = sum_rows((a, b, c, d)) * (1.0 + mod_rows(mod_ref[...], 1))
        out_ref[...] = (gmid_ref[...] + norm_back(g_in, normed, inverse)).astype(BF)
        total = gm_ref[...]
        for ref in (b, c, d):
            total = total + (ref[128:144, 0:256].astype(F32) + ref[128:144, 256:512].astype(F32))
        sum_ref[...] = total

    return kernel(
        body, [((128, 1024), BF), ((16, 256), F32)], index, *terms, g_mod, g_mid, latent, mod, after=after, cost=35, token=True, name="latent_back"
    )


def mod_sum(index, near, far, after):
    def body(idx, a, b, own_ref, far_ref, sum_s):
        sum_s[...] = a[...] + b[...]
        own_ref[...] = sum_s[:, aligned(idx[X_LO], 128)]
        far_ref[...] = sum_s[:, aligned(1 - idx[X_LO], 128)]

    outs = [((16, 128), F32)] * 2
    return kernel(body, outs, index, near, far, scratch=[((16, 256), F32)], after=after, token=True, name="mod_sum")


def cond_terms(index, near, rows, after):
    def body(idx, near_ref, a, b, c, d, out_ref, g_s):
        g_s[...] = jnp.zeros_like(g_s)
        for x in range(2):
            for l in range(2):
                for k in range(6):
                    g_s[2 * x + l : 2 * x + l + 1, k * 128 : (k + 1) * 128] = near_ref[x, 6 * l + k : 6 * l + k + 1]
        value = g_s[...]
        value = jnp.where(idx[X_LO] == 1, jnp.concatenate([value[2:4], value[0:2], value[4:8]], axis=0), value)
        high = value.astype(BF)
        rest = value - high.astype(F32)
        middle = rest.astype(BF)
        low = (rest - middle.astype(F32)).astype(BF)
        parts = jnp.concatenate([high.astype(F32), middle.astype(F32), low.astype(F32)], axis=0).astype(BF)
        for i, ref in enumerate((a, b, c, d)):
            term = dot(parts, ref[...], ((1,), (1,)))
            out_ref[:, aligned(idx[FEAT + i], 256)] = term[0:8] + (term[8:16] + term[16:24])

    return kernel(
        body, [((8, 1024), F32)], index, near, *rows, scratch=[((8, 768), F32)], after=after, token=True, name="cond_terms"
    )


def ada_grads(index, near, far, other, conds, after):
    def body(idx, *refs):
        near, far, other, conds, out_ref, g_s, s_s = *refs[:3], refs[3:7], *refs[7:]
        for i, ref in enumerate(conds):
            rows = jax.nn.silu(ref[:, aligned(idx[FEAT], 256)].astype(F32)).astype(BF).astype(F32)
            flipped = jnp.concatenate([rows[2:4], rows[0:2]], axis=0)
            s_s[4 * i : 4 * i + 4] = jnp.where(idx[X_LO] == 1, flipped, rows)
        g_s[...] = jnp.zeros_like(g_s)
        for b in range(4):
            for c in range(2):
                block = other[b] if c else (near, far)[b >> 1][b & 1]
                for l in range(2):
                    row = (2 * (b >> 1) + c) * 4 + 2 * (b & 1) + l
                    for k in range(6):
                        g_s[row : row + 1, k * 128 : (k + 1) * 128] = block[6 * l + k : 6 * l + k + 1]
        silu = s_s[...].T
        for k in range(6):
            out_ref[:, k, :] = lax.dot_general(
                silu, g_s[:, k * 128 : (k + 1) * 128], (((1,), (0,)), ((), ())), precision=HIGHEST
            )

    return kernel(
        body, [((256, 6, 128), F32)], index, near, far, other, *conds,
        scratch=[((16, 768), F32), ((16, 256), F32)], after=after, token=True, name="ada_grads"
    )


def hidden_core(index, kept, got, after):
    count = kept.shape[0]

    def body(idx, kept_ref, got_ref, own_ref, out_ref):
        for n in range(count):
            for h in range(2):
                own_ref[n, h] = kept_ref[n, h, :, 0:512] + got_ref[n, h, :, 0:512].astype(F32)
                out_ref[n, h] = (kept_ref[n, h, :, 512:1024] + got_ref[n, h, :, 512:1024].astype(F32)).astype(BF)

    outs = [((count, 2, 256, 512), F32), ((count, 2, 256, 512), BF)]
    return kernel(body, outs, index, kept, got, after=after, cost=31, token=True, name="hidden_core")


def hidden_x_lo(index, own, got, after):
    count = own.shape[0]

    def body(idx, own_ref, got_ref, kept_ref, out_ref):
        for n in range(count):
            kept_ref[n] = own_ref[n, 0] + got_ref[n, 0].astype(F32)
            out_ref[n] = (own_ref[n, 1] + got_ref[n, 1].astype(F32)).astype(BF)

    outs = [((count, 256, 512), F32), ((count, 256, 512), BF)]
    return kernel(body, outs, index, own, got, after=after, cost=31, token=True, name="hidden_x_lo")


def pair_sum(index, own, got, after):
    def body(idx, own_ref, got_ref, out_ref):
        out_ref[...] = (own_ref[...].astype(F32) + got_ref[...].astype(F32)).astype(BF)

    return kernel(body, [(own.shape, BF)], index, own, got, after=after, cost=31, token=True, name="pair_sum")


def hidden_out(index, own, got, after):
    def body(idx, own_ref, got_ref, up_ref, down_ref):
        up_ref[...] = own_ref[0].astype(F32) + got_ref[0].astype(F32)
        down_ref[...] = (own_ref[1].astype(F32) + got_ref[1].astype(F32)).T

    outs = [((256, 512), F32), ((512, 256), F32)]
    return kernel(body, outs, index, own, got, after=after, cost=31, token=True, name="hidden_out")


def attention_out(index, own, got):
    def body(idx, a, b, qkv_ref, proj_ref):
        def total(cols):
            return a[0, :, cols].astype(F32) + b[0, :, cols].astype(F32)

        for j in range(3):
            qkv_ref[:, j, :] = total(slice(j * 128, (j + 1) * 128))
        proj_ref[...] = total(slice(384, 512)).T

    return kernel(body, [((256, 3, 128), F32), ((128, 256), F32)], index, own, got, name="attention_out")


def exchange_y(blocks):
    return [blocks[0]] + [swap(blocks[r], "tp", r) for r in (1, 2, 3)]


def gather_y(block):
    return [block] + [swap(block, "tp", r) for r in (1, 2, 3)]


def gather_tp(block):
    near = gather_y(block)
    far = swap(block, "tp", 4)
    return near + [far, swap(far, "tp", 1), swap(near[2], "tp", 4), swap(far, "tp", 3)]


def exchange_z(blocks):
    return [blocks[0]] + [swap(blocks[q], "ctx", q) for q in (1, 2, 3)]


def corner(array):
    return array[:16, :128]


def sum_four(terms):
    return (terms[0] + terms[1]) + (terms[2] + terms[3])


def shards(
    latent_in, condition, ada_weight, qkv_weight, proj_weight, up_matrix, down_matrix, out_grad
):
    s, z, t = lax.axis_index("shard"), lax.axis_index("ctx"), lax.axis_index("tp")
    x_lo, y, z_lat, z_head = t >> 2, t & 3, z >> 1, z & 1
    columns = [[((4 * x + (y ^ r)) >> 1 ^ s) * 2 + ((y ^ r) & 1) for x in range(2)] for r in range(4)]
    index = jnp.stack(
        [2 * x_lo + (l ^ z_lat) for l in range(2)]
        + [y ^ r for r in range(4)]
        + [s ^ i for i in range(4)]
        + [2 * (x_lo ^ x) + (l ^ z_lat) for x in range(2) for l in range(2)]
        + [z_head, x_lo, z_lat, t]
        + [c for pair in columns for c in pair]
    ).astype(jnp.int32)

    ada = ada_weight.reshape(256, 768)
    conds = [condition] + [swap(condition, "shard", i) for i in (1, 2, 3)]
    kept, sent = mod_terms(index, conds, ada)
    terms = mod_core(index, kept, swap(sent, "shard", 1))
    terms = [terms[0]] + [swap_x(terms[b], b) for b in (1, 2, 3)]
    packed = pack_first(index, qkv_weight, proj_weight, tuple(terms[1:]))
    first = [packed] + [swap_x(packed, b) for b in (1, 2, 3)]
    packed = pack_second(index, up_matrix, down_matrix, (corner(first[3]),))
    mod_x = mod_ring(index, terms)
    near = jnp.concatenate([mod_x, swap(mod_x, "tp", 1)])
    latent = arrange(index, latent_in)
    mod, done = mod_assemble(index, near, swap(near, "tp", 2), (latent,))
    first = stack_blocks(index, first, (done,))[0].reshape(4, 256, 512)

    input_a, w_qkv, stats, proj, *parts, done = project_in(index, latent, mod, first, swap(first, "shard", 1))
    parts = exchange_z(parts)
    grad_out = arrange(index, out_grad, (done,))
    g_mlp, g_done = grad_mlp(index, grad_out, mod, (done,))
    packed, done = stack_blocks(index, [packed, swap(packed, "tp", 4)], tuple(corner(b) for b in parts[1:]))
    ada_far = swap(ada, "shard", 2)
    ada_rows = [ada, swap(ada, "shard", 1), ada_far, swap(ada_far, "shard", 1)]
    far = swap(packed, "shard", 2)
    up, down = assemble(index, packed, swap(packed, "shard", 1), far, swap(far, "shard", 1))
    g_act = grad_act(index, g_mlp, down)

    qkv, *heads = attention(index, parts, (g_done, done))
    heads = exchange_z(heads)
    attended, *terms = project_out(index, heads, proj)
    attn, middle, input_b = middle_rows(index, exchange_y(terms), latent, mod, (corner(far),))
    rows_b, act, g_up, *terms = feed_forward(index, gather_y(input_b), g_act, up)
    ud_kept, ud_sent, done = hidden_grads(index, rows_b, g_up, g_mlp, act)
    g_mid, g_attn, rows_mid = middle_back(
        index, exchange_y(terms), middle, attn, grad_out, mod, (done, corner(ada_rows[1]), corner(ada_rows[3]))
    )
    *mlp_terms, done = mlp_rows(index, act, down, (g_attn,))
    ud, ud_sent, done = hidden_core(index, ud_kept, swap(ud_sent, "shard", 1), (done,))
    g_attn, *g_parts = heads_back(index, gather_y(g_attn), proj, (done,))
    g_parts = exchange_z(g_parts)

    g_blocks = attention_back(index, qkv, g_parts, ())
    out_block, row_mlp = out_rows(index, exchange_y(mlp_terms), middle, grad_out, mod, (g_blocks[0],))
    out_blocks = gather_tp(out_block)
    ud, ud_sent, done = hidden_x_lo(index, ud, swap(ud_sent, "tp", 4), (out_block,))
    g_blocks = exchange_z(g_blocks)
    g_triple, *rest, done = input_back(
        index, g_blocks, w_qkv, latent, stats, row_mlp, rows_mid, (done,)
    )
    ud, ud_done = pair_sum(index, ud, swap(ud_sent, "shard", 2), (done,))
    kept, sent, done = attention_grads(index, input_a, g_triple, g_attn, attended)
    own, g_mod, done = latent_back(index, exchange_y(rest[:4]), rest[4], g_mid, latent, mod, (done, ud_done))

    blocks = gather_tp(own)
    g_mod = g_mod + swap(g_mod, "ctx", 1)
    qp, qp_sent, done = hidden_core(index, kept[None], swap(sent[None], "shard", 1), (done,))
    mod_own, mod_far, done = mod_sum(index, g_mod, swap(g_mod, "ctx", 2), (done,))
    near = jnp.stack([mod_own, swap(mod_far, "tp", 4)])
    ud, done = pair_sum(index, ud, swap(ud, "ctx", 1), (done,))
    qp, qp_sent, done = hidden_x_lo(
        index, qp, swap(qp_sent, "tp", 4), (done, *[corner(b) for b in blocks[1:4]])
    )
    terms, done = cond_terms(index, near, ada_rows, (done,))
    qp, done = pair_sum(index, qp, swap(qp_sent, "shard", 2), (done,))
    far = swap(near, "shard", 2)
    terms = terms + swap(terms, "tp", 4)
    up_grad, down_grad, done = hidden_out(index, ud, swap(ud, "ctx", 2), (done,))
    ada_grad, done = ada_grads(index, near, far, swap(jnp.concatenate([near, far]), "shard", 1), conds, (done,))
    terms = terms + swap(terms, "tp", 1)
    qp, done = pair_sum(index, qp, swap(qp, "ctx", 1), (done,))
    latent_grad, done = restore(index, blocks, (done,))
    latent_out, done = restore(index, out_blocks, (done,))
    terms = terms + swap(terms, "tp", 2)
    qkv_grad, proj_grad = attention_out(index, qp, swap(qp, "ctx", 2))
    _, silu_pull = jax.vjp(jax.nn.silu, condition.astype(F32))
    condition_grad = silu_pull(terms[:4])[0]

    return (
        latent_out,
        latent_grad,
        condition_grad,
        ada_grad,
        qkv_grad,
        proj_grad,
        up_grad,
        down_grad,
    )


def solution(mesh):
    placed = (
        P("shard", "ctx", None),
        P("shard", None),
        P("shard", None, "tp"),
        P("shard", None, "tp"),
        P("tp", "shard"),
        P("shard", "tp"),
        P("tp", "shard"),
        P("shard", "ctx", None),
    )
    return jax.shard_map(
        shards,
        mesh=mesh,
        in_specs=placed,
        out_specs=(
            P("shard", "ctx", None),
            P("shard", "ctx", None),
            P("shard", None),
            P("shard", None, "tp"),
            P("shard", None, "tp"),
            P("tp", "shard"),
            P("shard", "tp"),
            P("tp", "shard"),
        ),
        check_vma=False,
    )
```
